32 devices in a mesh: gx: 8 (over y, x, core), gy: 4 (over z).
Axes of the slice: x: 2, y: 2, z: 4, core: 2. Of those that a mesh axis runs over, the one named last changes fastest.
Arguments:
- estimate: float32 [32, 128, 512], P(None, 'gx', 'gy'), may hold values from 0.5 to 2
- stored: bfloat16 [4096, 16, 128], P(('gx', 'gy')), may hold values from 0.19921875 to 5
- placement: int32 [4096], replicated, may hold values from 0 to 4095, as said below
- psf_taps: float32 [48, 31], replicated, may hold values from 0.05 to 1
- kernel_index: int32 [8, 4, 4, 3], replicated, may hold values from 0 to 47
Outputs:
- refined: float32 [32, 128, 512], P(None, 'gx', 'gy')
The draws below stay inside these ranges and needn't reach their ends.
Inputs may be any that keep to these rules, and one draw needn't show every extreme that they name: `placement`: each value occurs once; the value b * 128 + v * 32 + z marks plane z of view v of brick b. Entries d * 128 to (d + 1) * 128 - 1 are the slots of device d of gx+gy; among them at most 8 name any one brick, every device has exactly 8 naming some brick, and every brick has exactly 8 on some device.
All inputs are finite; a program needn't handle non-finite values.
Results may differ from the reference program's by a relative error of at most 0.0003.
Values may be sent and summed in bfloat16 or wider, within the bound.
No kernel may reach another device: no remote copies, remote signals or barrier semaphores. Data moves between devices by JAX's collectives and lax.ppermute only.
A program may use at most 128 MiB of HBM per device.

```python
import math
import jax
import jax.numpy as jnp
from jax import lax

BX = 16
BY = 128
NZ = 32
V = 4
TAPS = 31
NK = 48
ITERS = 2
SLOTS = 128
CAP = 8
NX = 128
NY = 512
N_GX = 8
N_GY = 4
DEVICES = 32


def draw_placement(key, part):
    streams = jax.random.split(jax.random.fold_in(key, 7), 4)
    relabel = jax.random.permutation(streams[0], DEVICES).astype(jnp.int32)
    restore = jnp.argsort(relabel).astype(jnp.int32)
    crowded = jax.random.randint(streams[1], (), 0, DEVICES, dtype=jnp.int32)
    spread = (jax.random.permutation(streams[2], (DEVICES - 1) * CAP)[:SLOTS - CAP] // CAP).astype(jnp.int32)
    spread = spread + (spread >= crowded).astype(jnp.int32)
    offsets = jnp.concatenate([jnp.full((CAP,), crowded, jnp.int32), spread])
    target_brick = restore[(relabel[:, None] - offsets[None, :]) % DEVICES]
    orders = jax.vmap(lambda subkey: jax.random.permutation(subkey, SLOTS))(jax.random.split(streams[3], DEVICES)).astype(jnp.int32)
    plane_item = orders[target_brick, jnp.arange(SLOTS, dtype=jnp.int32)[None, :]]
    return (target_brick * SLOTS + plane_item).reshape(-1).astype(jnp.int32)


def with_ends(result, rng, least, high):
    dims = result.shape
    spot = [jax.random.randint(jax.random.fold_in(rng, axis), (), 0, dims[axis]) for axis in range(len(dims))]
    result = result.at[tuple(spot)].set(least)
    longest = dims.index(max(dims))
    spot[longest] = (spot[longest] + 1) % dims[longest]
    return result.at[tuple(spot)].set(high)


def block_scale(own_key, extent, shards, low, top_value):
    level = 1.0
    for dim, parts in shards:
        steps = jax.random.uniform(jax.random.fold_in(jax.random.fold_in(own_key, 6), dim), (parts,), jnp.float32, low / len(shards), top_value / len(shards))
        level = level * jnp.repeat(jnp.exp(steps), extent[dim] // parts).reshape((-1,) + (1,) * (len(extent) - 1 - dim))
    return level


def setup_inputs(seed: int = 0) -> dict:
    key_list = jax.random.split(jax.random.key(seed), 6)
    estimate = jnp.clip(jnp.exp(math.log(2.0) - 1.3862944 * jax.random.uniform(key_list[0], (NZ, NX, NY), jnp.float32) ** block_scale(key_list[0], (NZ, NX, NY), ((1, 8), (2, 4)), -0.2, 0.2)), 0.5, 2.0)
    stored = jnp.clip(jnp.exp(math.log(5.0) - 3.2227897 * jax.random.uniform(key_list[1], (DEVICES * SLOTS, BX, BY), jnp.float32) ** block_scale(key_list[1], (DEVICES * SLOTS, BX, BY), ((0, 32),), -0.2, 0.2)), 0.19921875, 5.0).astype(jnp.bfloat16)
    placement = draw_placement(jax.random.fold_in(key_list[5], 71), 0)
    psf_taps = jnp.clip(jnp.exp(jax.random.uniform(key_list[3], (NK, TAPS), jnp.float32, math.log(0.05), math.log(1.0))), 0.05, 1.0)
    kernel_index = with_ends(jax.random.randint(key_list[4], (N_GX, N_GY, V, 3), 0, NK), jax.random.fold_in(key_list[4], 1), 0, NK - 1).astype(jnp.int32)
    return dict(estimate=estimate, stored=stored, placement=placement, psf_taps=psf_taps, kernel_index=kernel_index)


precise = lax.Precision.HIGHEST


def lookup(psf_taps, indices):
    chosen = (indices[..., None] == jnp.arange(psf_taps.shape[0], dtype=jnp.int32)).astype(jnp.float32)
    kernels = jnp.einsum("vek,kt->vet", chosen, psf_taps, precision=precise)
    return kernels / jnp.sum(kernels, axis=-1, keepdims=True)


def places(count, start):
    return jnp.arange(count, dtype=jnp.int32) + start


def banded(kernels, out_pos, in_pos):
    radius = (kernels.shape[-1] - 1) // 2
    offsets = in_pos[None, :] - out_pos[:, None] + radius
    selector = (offsets[:, :, None] == jnp.arange(kernels.shape[-1], dtype=jnp.int32)).astype(jnp.float32)
    return jnp.einsum("oit,vt->voi", selector, kernels, precision=precise)


def brick_kernels(psf_taps, kernel_index, brick_x, brick_y):
    anchor = jnp.zeros((), jnp.int32)
    views = kernel_index.shape[2]
    picked = lax.dynamic_slice(kernel_index, (brick_x, brick_y, anchor, anchor), (1, 1, views, 3))[0, 0]
    return lookup(psf_taps, picked)


def operators(kernels, planes, extent_x, extent_y):
    radius = (kernels.shape[-1] - 1) // 2
    along_z = banded(kernels[:, 2], places(planes, 0), places(planes, 0))
    along_x = banded(kernels[:, 0], places(extent_x + 2 * radius, -radius), places(extent_x, 0))
    along_y = banded(kernels[:, 1], places(extent_y + 2 * radius, -radius), places(extent_y, 0))
    return along_z, along_x, along_y


def forward_blur(inside, along_z, along_x, along_y):
    blurred = jnp.einsum("vpz,zxy->vpxy", along_z, inside, precision=precise)
    blurred = jnp.einsum("vix,vpxy->vpiy", along_x, blurred, precision=precise)
    return jnp.einsum("vjy,vpiy->vpij", along_y, blurred, precision=precise)


def adjoint_blur(spread, along_z, along_x, along_y):
    folded = jnp.einsum("vjy,vpij->vpiy", along_y, spread, precision=precise)
    folded = jnp.einsum("vix,vpiy->vpxy", along_x, folded, precision=precise)
    return jnp.einsum("vpz,vpxy->zxy", along_z, folded, precision=precise)


def reference(estimate, stored, placement, psf_taps, kernel_index):
    radius = (TAPS - 1) // 2
    bricks = N_GX * N_GY
    arranged = jnp.zeros_like(stored).at[placement].set(stored)
    measured = arranged.reshape(N_GX, N_GY, V, NZ, BX, BY).transpose(2, 3, 0, 4, 1, 5).reshape(V, NZ, NX, NY).astype(jnp.float32)
    anchor = jnp.zeros((), jnp.int32)

    def setup(brick_id):
        brick_id = jnp.asarray(brick_id).astype(jnp.int32)
        brick_x = brick_id // N_GY
        brick_y = brick_id % N_GY
        kernels = brick_kernels(psf_taps, kernel_index, brick_x, brick_y)
        return brick_x * BX, brick_y * BY, operators(kernels, NZ, BX, BY)

    current = estimate
    for iteration in range(ITERS):
        def spread_one(brick_id, summed):
            start_x, start_y, mats = setup(brick_id)
            inside = lax.dynamic_slice(current, (anchor, start_x, start_y), (NZ, BX, BY))
            spread = forward_blur(inside, mats[0], mats[1], mats[2])
            corner = (anchor, anchor, start_x, start_y)
            return lax.dynamic_update_slice(summed, lax.dynamic_slice(summed, corner, spread.shape) + spread, corner)

        summed = lax.fori_loop(0, bricks, spread_one, jnp.zeros((V, NZ, NX + 2 * radius, NY + 2 * radius), jnp.float32))
        blurred = summed[:, :, radius:radius + NX, radius:radius + NY]
        quotient = measured / blurred
        padded = jnp.pad(quotient, ((0, 0), (0, 0), (radius, radius), (radius, radius)))

        def fold_one(brick_id, correction):
            start_x, start_y, mats = setup(brick_id)
            spread = lax.dynamic_slice(padded, (anchor, anchor, start_x, start_y), (V, NZ, BX + 2 * radius, BY + 2 * radius))
            piece_corr = adjoint_blur(spread, mats[0], mats[1], mats[2]) / V
            return lax.dynamic_update_slice(correction, piece_corr, (anchor, start_x, start_y))

        correction = lax.fori_loop(0, bricks, fold_one, jnp.zeros_like(current))
        current = current * correction
    return current
```

```python
import functools

import jax
import jax.numpy as jnp
from jax import lax
from jax.experimental import pallas as pl
from jax.experimental.pallas import tpu as pltpu
from jax.sharding import PartitionSpec as P

f32 = jnp.float32
bf16 = jnp.bfloat16
i32 = jnp.int32

NZ = 32
BX = 16
BY = 128
V = 4
TAPS = 31
RADIUS = 15
FIELD = BX * NZ
STRIP = 16
LANES = 128
ROLES = 3


def iota(shape, axis):
    return lax.broadcasted_iota(i32, shape, axis)


def one_hot(mask):
    return jnp.where(mask, 1.0, 0.0).astype(bf16)


def split(a):
    hi = a.astype(bf16)
    return hi, (a - hi.astype(f32)).astype(bf16)


def dot(a, b):
    return jnp.dot(a, b, preferred_element_type=f32)


def earlier(count):
    return one_hot(iota((count, count), 0) < iota((count, count), 1))


def route_kernel(cap, target_ref, stored_ref, out_ref):
    rows, slots = out_ref.shape[0], stored_ref.shape[0]
    place = iota((rows, slots), 0) - target_ref[...] * cap
    marked = jnp.logical_and(place >= 0, place < cap)
    rank = dot(one_hot(marked), earlier(slots))
    chosen = one_hot(jnp.logical_and(marked, rank == place.astype(f32)))
    out_ref[...] = dot(chosen, stored_ref[...]).astype(bf16)


def arrival_kernel(cap, me_ref, slots_ref, out_ref):
    rows, slots = slots_ref.shape
    item = slots_ref[...] - me_ref[0] * slots
    wanted = jnp.logical_and(item >= 0, item < slots)
    rank = dot(one_hot(wanted), earlier(slots))
    order = jnp.bitwise_and(iota((rows, slots), 0), cap - 1)
    found = jnp.logical_and(wanted, rank == order.astype(f32))
    item_of = jnp.sum(jnp.where(found, item + 1, 0).astype(f32), axis=1, keepdims=True) - 1.0
    table = jnp.where(item_of == iota((rows, slots), 1).astype(f32), 1.0, 0.0)
    out_ref[...] = table.T.astype(bf16)


def toeplitz(row, count):
    spread = jnp.broadcast_to(row, (count, LANES))
    return pltpu.roll(spread, LANES - RADIUS, 1, stride=1, stride_axis=0)


def expand(table, selector):
    first = table.astype(bf16)
    rest = table - first.astype(f32)
    second = rest.astype(bf16)
    third = (rest - second.astype(f32)).astype(bf16)
    return dot(first, selector) + dot(second, selector) + dot(third, selector)


def selectors(width, count):
    lane = iota((LANES, width * count), 1)
    row = iota((LANES, width * count), 0)
    each = one_hot(row == jnp.right_shift(lane, width.bit_length() - 1))
    tiled = one_hot(row == jnp.bitwise_and(lane, width - 1))
    return each, tiled


def row_of(xr, yr, view, axis):
    return ((xr * ROLES + yr) * V + view) * 3 + axis


def kron_rows(out, outer, inner, count, width):
    for i in range(count):
        out[i * width : (i + 1) * width, :] = (inner * outer[i : i + 1, :]).astype(bf16)


def stack3(table):
    hi, lo = split(table)
    return jnp.concatenate([hi, hi, lo], axis=0)


def lanes3(table, width):
    inside = iota(table.shape, 1) < width
    kept = jnp.where(inside, table, 0.0)
    hi, lo = split(kept)
    hi, lo = hi.astype(f32), lo.astype(f32)
    return (hi + pltpu.roll(lo, width, 1) + pltpu.roll(hi, 2 * width, 1)).astype(bf16)


def banded_y(row):
    table = toeplitz(row, BY)
    off = iota((BY, BY), 0) - iota((BY, BY), 1)
    return jnp.where(jnp.abs(off) <= RADIUS, table, 0.0)


def build_forward_kernel(taps_ref, back_ref, k_ref, y_ref, xy_ref, z_ref):
    each, tiled = selectors(NZ, BX)
    each16, tiled16 = selectors(STRIP, BX)
    for xr in range(ROLES):
        for v in range(V):
            def fwd(yr, e):
                r = row_of(xr, yr, v, e)
                return taps_ref[r : r + 1, :]

            def bwd(yr, e):
                r = row_of(xr, yr, v, e)
                return back_ref[r : r + 1, :]

            outer = expand(toeplitz(fwd(0, 0), BX), each)
            inner = expand(toeplitz(fwd(0, 2), NZ), tiled)
            kron_rows(k_ref.at[xr, v], outer, inner, BX, NZ)
            y_ref[xr, :, v * BY : (v + 1) * BY] = stack3(banded_y(bwd(0, 1)))
            for yr in (1, 2):
                outer = expand(toeplitz(bwd(yr, 0), BX), each16)
                inner = expand(toeplitz(bwd(yr, 1), STRIP), tiled16)
                kron_rows(xy_ref.at[xr, yr - 1, v], outer, inner, BX, STRIP)
                z_ref[xr, yr - 1, v * NZ : (v + 1) * NZ, :] = lanes3(toeplitz(fwd(yr, 2), NZ), NZ)


def build_adjoint_kernel(taps_ref, back_ref, k_ref, y_ref, xy_ref, z_ref):
    each, tiled = selectors(NZ, BX)
    each16, tiled16 = selectors(STRIP, BX)
    for xr in range(ROLES):
        for v in range(V):
            def fwd(yr, e):
                r = row_of(xr, yr, v, e)
                return taps_ref[r : r + 1, :]

            def bwd(yr, e):
                r = row_of(xr, yr, v, e)
                return back_ref[r : r + 1, :]

            outer = expand(toeplitz(bwd(0, 0), BX), each)
            inner = expand(toeplitz(bwd(0, 2), NZ), tiled) * (1.0 / V)
            kron_rows(k_ref.at[xr, v], outer, inner, BX, NZ)
            y_ref[v, :, xr * BY : (xr + 1) * BY] = stack3(banded_y(fwd(0, 1)))
            for yr in (1, 2):
                outer = expand(toeplitz(fwd(yr, 0), BX), each16)
                inner = expand(toeplitz(fwd(yr, 1), STRIP), tiled16)
                kron_rows(xy_ref.at[xr, yr - 1, v], outer, inner, BX, STRIP)
                z_ref[xr, yr - 1, :, v * LANES : (v + 1) * LANES] = lanes3(
                    toeplitz(bwd(yr, 2), NZ) * (1.0 / V), NZ
                )


def pack_strip(field, shift):
    lane = iota((NZ, LANES), 1)
    halves = []
    for half in range(2):
        total = jnp.zeros((NZ, LANES), f32)
        for j in range(8):
            x = half * 8 + j
            moved = pltpu.roll(field[x * NZ : (x + 1) * NZ, :], shift + STRIP * j, 1)
            inside = jnp.logical_and(lane >= STRIP * j, lane < STRIP * (j + 1))
            total = jnp.where(inside, moved, total)
        halves.append(total)
    return jnp.concatenate(halves, axis=0)


def unpack_strip(halves, shift):
    lane = iota((NZ, LANES), 1)
    first = jnp.where(shift > 0, BY - STRIP, 0)
    inside = jnp.logical_and(lane >= first, lane < first + STRIP)
    rows = []
    for x in range(BX):
        half, j = x // 8, x % 8
        moved = pltpu.roll(halves[half * NZ : (half + 1) * NZ, :], 2 * LANES - shift - STRIP * j, 1)
        rows.append(jnp.where(inside, moved, 0.0))
    return jnp.concatenate(rows, axis=0)


def wide(halves):
    return jnp.concatenate([halves[:NZ], halves[NZ:]], axis=1)


def tall(strip):
    return jnp.concatenate([strip[:, :LANES], strip[:, LANES:]], axis=0)


def column3(a):
    hi, lo = split(a)
    return jnp.concatenate([hi, hi, lo, jnp.zeros_like(hi)], axis=0)


def two_rows(a, matrix):
    hi, lo = split(a)
    both = dot(jnp.concatenate([hi, lo], axis=0), matrix)
    return both[: a.shape[0]] + both[a.shape[0] :]


def two_lanes(matrix, a):
    hi, lo = split(a)
    both = dot(matrix, jnp.concatenate([hi, lo], axis=1))
    return both[:, :LANES] + both[:, LANES:]


def three_lanes(a, stacked):
    hi, lo = split(a)
    return dot(jnp.concatenate([hi, lo, hi], axis=1), stacked)


def forward_parts(sources, k_ref, y_ref, xy_ref, z_ref, shifts, add):
    for xr, field, _ in sources:
        spread = three_lanes(field, y_ref[xr])
        for v in range(V):
            add(v, two_lanes(k_ref[xr, v], spread[:, v * BY : (v + 1) * BY]))
    for yr in (1, 2):
        totals = [jnp.zeros((NZ, 2 * LANES), f32) for _ in range(V)]
        for xr, _, strips in sources:
            along = dot(z_ref[xr, yr - 1], column3(wide(strips[yr - 1])))
            for v in range(V):
                totals[v] += two_rows(along[v * NZ : (v + 1) * NZ], xy_ref[xr, yr - 1, v])
        for v in range(V):
            add(v, unpack_strip(tall(totals[v]), shifts[yr - 1]))


def adjoint_parts(roles, quotient, edges, k_ref, y_ref, xy_ref, z_ref):
    first, last = roles[0], roles[-1] + 1
    totals = [jnp.zeros((FIELD, LANES), f32) for _ in roles]
    for v in range(V):
        spread = three_lanes(quotient(v), y_ref[v, :, first * BY : last * BY])
        for n, xr in enumerate(roles):
            totals[n] += two_lanes(k_ref[xr, v], spread[:, n * BY : (n + 1) * BY])
    strips = [[], []]
    for yr in (1, 2):
        packed = [wide(edges(v, yr)) for v in range(V)]
        for xr in roles:
            parts = [column3(two_rows(packed[v], xy_ref[xr, yr - 1, v])) for v in range(V)]
            strips[yr - 1].append(tall(dot(z_ref[xr, yr - 1], jnp.concatenate(parts, axis=0))))
    return totals, strips


def message_parts(message):
    return message[:FIELD], [message[FIELD : FIELD + 2 * NZ], message[FIELD + 2 * NZ :]]


def start_kernel(info_ref, estimate_ref, field_ref, first_ref, second_ref):
    for x in range(BX):
        field_ref[x * NZ : (x + 1) * NZ, :] = estimate_ref[:, x, :]
    field = field_ref[...]
    first_ref[...] = pack_strip(field, info_ref[0])
    second_ref[...] = pack_strip(field, info_ref[1])


def forward_first_kernel(info_ref, own_ref, first_ref, second_ref, k_ref, y_ref, xy_ref, z_ref, out_ref):
    shifts = (info_ref[0], info_ref[1])
    out_ref[...] = jnp.zeros_like(out_ref)

    def add(v, part):
        out_ref[v] += part

    sources = [(n, *message_parts(ref[...])) for n, ref in enumerate((own_ref, first_ref, second_ref))]
    forward_parts(sources, k_ref, y_ref, xy_ref, z_ref, shifts, add)
    for v in range(V):
        out_ref[v] = 1.0 / out_ref[v]


def adjoint_sides(quotient_ref, edge_ref, shifts, k_ref, y_ref, xy_ref, z_ref, first_ref, second_ref):
    for v in range(V):
        for yr in (1, 2):
            edge_ref[v, yr - 1] = pack_strip(quotient_ref[v], shifts[yr - 1])
    totals, strips = adjoint_parts(
        (1, 2), lambda v: quotient_ref[v], lambda v, yr: edge_ref[v, yr - 1], k_ref, y_ref, xy_ref, z_ref
    )
    for n, ref in enumerate((first_ref, second_ref)):
        ref[:FIELD] = totals[n]
        ref[FIELD : FIELD + 2 * NZ] = strips[0][n]
        ref[FIELD + 2 * NZ :] = strips[1][n]


def quotient_first_kernel(
    info_ref, table_ref, arrived_ref, inverse_ref, k_ref, y_ref, xy_ref, z_ref,
    data_ref, quotient_ref, edge_ref, first_ref, second_ref,
):
    shifts = (info_ref[0], info_ref[1])
    planes = dot(table_ref[...], arrived_ref[...])
    for v in range(V):
        for x in range(BX):
            rows = slice(x * NZ, (x + 1) * NZ)
            piece = planes[v * NZ : (v + 1) * NZ, x * BY : (x + 1) * BY]
            data_ref[v, rows, :] = piece.astype(bf16)
            quotient_ref[v, rows, :] = piece * inverse_ref[v, rows, :]
    adjoint_sides(quotient_ref, edge_ref, shifts, k_ref, y_ref, xy_ref, z_ref, first_ref, second_ref)


def adjoint_center_kernel(quotient_ref, edge_ref, k_ref, y_ref, xy_ref, z_ref, field_ref, strips_ref):
    totals, strips = adjoint_parts(
        (0,), lambda v: quotient_ref[v], lambda v, yr: edge_ref[v, yr - 1], k_ref, y_ref, xy_ref, z_ref
    )
    field_ref[...] = totals[0]
    strips_ref[0] = strips[0][0]
    strips_ref[1] = strips[1][0]


def gather_kernel(info_ref, field_ref, strips_ref, first_ref, second_ref, total_ref, up_ref, down_ref):
    total = field_ref[...] + first_ref[:FIELD] + second_ref[:FIELD]
    total_ref[...] = total
    for n, ref in enumerate((up_ref, down_ref)):
        rows = slice(FIELD + n * 2 * NZ, FIELD + (n + 1) * 2 * NZ)
        ref[: 2 * NZ] = strips_ref[n] + first_ref[rows] + second_ref[rows]
        ref[2 * NZ :] = pack_strip(total, info_ref[n])


def gather_last_kernel(field_ref, strips_ref, first_ref, second_ref, total_ref, up_ref, down_ref):
    total_ref[...] = field_ref[...] + first_ref[:FIELD] + second_ref[:FIELD]
    for n, ref in enumerate((up_ref, down_ref)):
        rows = slice(FIELD + n * 2 * NZ, FIELD + (n + 1) * 2 * NZ)
        ref[...] = strips_ref[n] + first_ref[rows] + second_ref[rows]


def update_kernel(info_ref, old_ref, total_ref, up_ref, down_ref, up_in_ref, down_in_ref, new_ref):
    half = 2 * NZ
    correction = total_ref[...]
    for n, ref in enumerate((up_in_ref, down_in_ref)):
        correction += unpack_strip(ref[:half], info_ref[n])
    new_ref[:FIELD] = old_ref[:FIELD] * correction
    for n, (ref, own) in enumerate(((up_in_ref, up_ref), (down_in_ref, down_ref))):
        rows = slice(FIELD + n * half, FIELD + (n + 1) * half)
        new_ref[rows] = old_ref[rows] * (ref[half:] + own[:half])


def forward_center_kernel(info_ref, own_ref, k_ref, y_ref, xy_ref, z_ref, out_ref):
    shifts = (info_ref[0], info_ref[1])
    out_ref[...] = jnp.zeros_like(out_ref)

    def add(v, part):
        out_ref[v] += part

    forward_parts([(0, *message_parts(own_ref[...]))], k_ref, y_ref, xy_ref, z_ref, shifts, add)


def middle_kernel(
    info_ref, data_ref, blurred_ref, from_first_ref, from_second_ref,
    k_ref, y_ref, xy_ref, z_ref, ka_ref, ya_ref, xya_ref, za_ref,
    quotient_ref, edge_ref, first_ref, second_ref,
):
    shifts = (info_ref[0], info_ref[1])
    quotient_ref[...] = blurred_ref[...]

    def add(v, part):
        quotient_ref[v] += part

    sources = [(1, *message_parts(from_first_ref[...])), (2, *message_parts(from_second_ref[...]))]
    forward_parts(sources, k_ref, y_ref, xy_ref, z_ref, shifts, add)
    for v in range(V):
        quotient_ref[v] = data_ref[v].astype(f32) / quotient_ref[v]
    adjoint_sides(quotient_ref, edge_ref, shifts, ka_ref, ya_ref, xya_ref, za_ref, first_ref, second_ref)


def final_kernel(info_ref, old_ref, total_ref, up_in_ref, down_in_ref, out_ref):
    correction = total_ref[...]
    for n, ref in enumerate((up_in_ref, down_in_ref)):
        correction += unpack_strip(ref[...], info_ref[n])
    result = old_ref[:FIELD] * correction
    for x in range(BX):
        out_ref[:, x, :] = result[x * NZ : (x + 1) * NZ]


def call(kernel, outs, *args, scalars=0):
    specs = [pl.BlockSpec(memory_space=pltpu.SMEM)] * scalars
    specs += [pl.BlockSpec(memory_space=pltpu.VMEM)] * (len(args) - scalars)
    return pl.pallas_call(
        kernel,
        out_shape=[jax.ShapeDtypeStruct(s, d) for s, d in outs],
        in_specs=specs,
        out_specs=[pl.BlockSpec(memory_space=pltpu.VMEM)] * len(outs),
        compiler_params=pltpu.CompilerParams(vmem_limit_bytes=60 * 2**20),
    )(*args)


def partner_swaps(axis):
    count = lax.axis_size(axis)
    near = [(i, i ^ 1) for i in range(count)]
    far = [(i, (i - 1 if i % 2 == 0 else i + 1) % count) for i in range(count)]
    return near, far


def swap(axis, near_value, far_value):
    near, far = partner_swaps(axis)
    far_in = lax.ppermute(far_value, axis, far)
    near_in = lax.ppermute(near_value, axis, near)
    return near_in, far_in


def tap_tables(psf_taps, kernel_index):
    gx, gy = lax.axis_index("gx"), lax.axis_index("gy")
    even_x, even_y = gx % 2 == 0, gy % 2 == 0
    anchor = jnp.zeros((), i32)
    bordered = jnp.pad(kernel_index, ((1, 1), (1, 1), (0, 0), (0, 0)), constant_values=-1)
    around = lax.dynamic_slice(
        bordered, (gx.astype(i32), gy.astype(i32), anchor, anchor), (ROLES, ROLES, V, 3)
    )
    up, down = jnp.array([1, 2, 0]), jnp.array([1, 0, 2])
    around = jnp.where(even_x, around[up], around[down])
    around = jnp.where(even_y, around[:, up], around[:, down])
    normal = psf_taps / jnp.sum(psf_taps, axis=-1, keepdims=True)
    chosen = (around.reshape(-1)[:, None] == jnp.arange(psf_taps.shape[0], dtype=i32)).astype(f32)
    kernels = jnp.dot(chosen, normal, precision=lax.Precision.HIGHEST)
    kernels = jnp.pad(kernels, ((0, 0), (0, LANES - TAPS)))
    backward = jnp.pad(kernels[:, :TAPS][:, ::-1], ((0, 0), (0, LANES - TAPS)))
    role = jnp.arange(kernels.shape[0])
    axis, yr, xr = role % 3, role // (3 * V) % ROLES, role // (3 * V * ROLES)
    step = jnp.where(axis == 0, jnp.where(xr == 1, 1, jnp.where(xr == 2, -1, 0)), 0)
    step = step * jnp.where(even_x, 1, -1)
    step_y = jnp.where(axis == 1, jnp.where(yr == 1, 1, jnp.where(yr == 2, -1, 0)), 0)
    step = (step + step_y * jnp.where(even_y, 1, -1))[:, None]

    def moved(a, sign):
        return jnp.where(
            step * sign > 0, jnp.roll(a, -STRIP, 1), jnp.where(step * sign < 0, jnp.roll(a, STRIP, 1), a)
        )

    shifts = jnp.stack([jnp.where(even_y, STRIP, 0), jnp.where(even_y, 0, STRIP)]).astype(i32)
    return moved(kernels, 1), moved(backward, -1), shifts


def shards(estimate, stored, placement, psf_taps, kernel_index):
    devices_y = lax.axis_size("gy")
    devices = lax.axis_size("gx") * devices_y
    slots = stored.shape[0]
    cap = 2 * slots // devices
    rows = devices * cap
    plane = BX * BY
    me = (lax.axis_index("gx") * devices_y + lax.axis_index("gy")).astype(i32)

    own = lax.dynamic_slice_in_dim(placement, me * slots, slots)
    (outgoing,) = call(
        functools.partial(route_kernel, cap),
        [((rows, plane), bf16)],
        (own // slots).reshape(1, slots),
        stored.reshape(slots, plane),
    )
    arrived = lax.all_to_all(
        outgoing.reshape(devices, cap, plane), ("gx", "gy"), split_axis=0, concat_axis=0, tiled=True
    ).reshape(rows, plane)

    taps, backward, info = tap_tables(psf_taps, kernel_index)
    half, message = (2 * NZ, LANES), (FIELD + 4 * NZ, LANES)
    field, up, down = call(
        start_kernel, [((FIELD, LANES), f32), (half, f32), (half, f32)], info, estimate, scalars=1
    )
    up_in, down_in = swap("gy", up, down)
    old = jnp.concatenate([field, up_in, down_in], axis=0)
    first, second = swap("gx", old, old)

    def shapes(y_shape, z_shape):
        return [
            ((ROLES, V, FIELD, FIELD), bf16),
            (y_shape, bf16),
            ((ROLES, 2, V, 2 * LANES, 2 * LANES), bf16),
            (z_shape, bf16),
        ]

    forward = call(build_forward_kernel, shapes((ROLES, 3 * BY, V * BY), (ROLES, 2, V * NZ, LANES)), taps, backward)
    adjoint = call(build_adjoint_kernel, shapes((V, 3 * BY, ROLES * BY), (ROLES, 2, NZ, V * LANES)), taps, backward)
    every = (V, FIELD, LANES)
    (inverse,) = call(forward_first_kernel, [(every, f32)], info, old, first, second, *forward, scalars=1)
    repeated = jnp.repeat(placement.reshape(devices, slots), cap, axis=0)
    (table,) = call(
        functools.partial(arrival_kernel, cap), [((slots, rows), bf16)], me.reshape(1), repeated, scalars=1
    )

    edges = ((V, 2) + half, f32)
    data, quotient, edge, first, second = call(
        quotient_first_kernel,
        [(every, bf16), (every, f32), edges, (message, f32), (message, f32)],
        info, table, arrived, inverse, *adjoint, scalars=1,
    )
    first, second = swap("gx", first, second)
    field, strips = call(
        adjoint_center_kernel, [((FIELD, LANES), f32), ((2,) + half, f32)], quotient, edge, *adjoint
    )
    both = (4 * NZ, LANES)
    total, up, down = call(
        gather_kernel, [((FIELD, LANES), f32), (both, f32), (both, f32)],
        info, field, strips, first, second, scalars=1,
    )
    up_in, down_in = swap("gy", up, down)
    (new,) = call(update_kernel, [(message, f32)], info, old, total, up, down, up_in, down_in, scalars=1)
    first, second = swap("gx", new, new)
    (blurred,) = call(forward_center_kernel, [(every, f32)], info, new, *forward, scalars=1)
    quotient, edge, first, second = call(
        middle_kernel, [(every, f32), edges, (message, f32), (message, f32)],
        info, data, blurred, first, second, *forward, *adjoint, scalars=1,
    )
    first, second = swap("gx", first, second)
    field, strips = call(
        adjoint_center_kernel, [((FIELD, LANES), f32), ((2,) + half, f32)], quotient, edge, *adjoint
    )
    total, up, down = call(
        gather_last_kernel, [((FIELD, LANES), f32), (half, f32), (half, f32)], field, strips, first, second
    )
    up_in, down_in = swap("gy", up, down)
    (refined,) = call(final_kernel, [(estimate.shape, f32)], info, new, total, up_in, down_in, scalars=1)
    return refined


def solution(mesh):
    return jax.shard_map(
        shards,
        mesh=mesh,
        in_specs=(P(None, "gx", "gy"), P(("gx", "gy"), None, None), P(), P(), P()),
        out_specs=P(None, "gx", "gy"),
        check_vma=False,
    )
```

```python
import functools
import math

import jax
import jax.numpy as jnp
from jax import lax
from jax.experimental import pallas as pl
from jax.experimental.pallas import tpu as pltpu
from jax.sharding import PartitionSpec as P

f32 = jnp.float32
bf16 = jnp.bfloat16
i32 = jnp.int32

NZ = 32
BX = 16
BY = 128
V = 4
TAPS = 31
RADIUS = 15
FIELD = BX * NZ
STRIP = 16
LANES = 128
WORKSPACE = 8 * 2**20
PEAK = 14.0
ROLES = 3


def iota(shape, axis):
    return lax.broadcasted_iota(i32, shape, axis)


def one_hot(mask):
    return jnp.where(mask, 1.0, 0.0).astype(bf16)


def split(a):
    hi = a.astype(bf16)
    return hi, (a - hi.astype(f32)).astype(bf16)


def dot(a, b):
    return jnp.dot(a, b, preferred_element_type=f32)


def earlier(count):
    return one_hot(iota((count, count), 0) < iota((count, count), 1))


def route_kernel(cap, me_ref, slots_ref, stored_ref, out_ref, wide_ref):
    rows, slots = out_ref.shape[0], stored_ref.shape[0]
    wide_ref[...] = stored_ref[...].reshape(slots * BX, BY).astype(f32)
    target = jnp.right_shift(slots_ref[pl.ds(me_ref[0], 1), :], slots.bit_length() - 1)
    place = iota((rows, slots), 0) - target * cap
    marked = jnp.logical_and(place >= 0, place < cap)
    rank = dot(one_hot(marked), earlier(slots))
    chosen = one_hot(jnp.logical_and(marked, rank == place.astype(f32)))
    for x in range(0, BX, 2):
        pair = [wide_ref[pl.ds(x + n, slots, stride=BX), :].astype(bf16) for n in range(2)]
        out_ref[:, x * BY : (x + 2) * BY] = dot(chosen, jnp.concatenate(pair, axis=1)).astype(bf16)


def arrival_kernel(cap, me_ref, slots_ref, out_ref, table_ref, sem):
    rows, slots = slots_ref.shape
    item = slots_ref[...] - me_ref[0] * slots
    wanted = jnp.logical_and(item >= 0, item < slots)
    rank = dot(one_hot(wanted), earlier(slots))
    order = jnp.bitwise_and(iota((rows, slots), 0), cap - 1)
    found = jnp.logical_and(wanted, rank == order.astype(f32))
    item_of = jnp.sum(jnp.where(found, item + 1, 0).astype(f32), axis=1, keepdims=True) - 1.0
    table = jnp.where(item_of == iota((rows, slots), 1).astype(f32), 1.0, 0.0)
    table_ref[...] = table.T.astype(bf16)
    copy = pltpu.make_async_copy(table_ref, out_ref, sem)
    copy.start()
    copy.wait()


def toeplitz(row, count):
    spread = jnp.broadcast_to(row, (count, LANES))
    return pltpu.roll(spread, LANES - RADIUS, 1, stride=1, stride_axis=0)


def expand(table, selector):
    first = table.astype(bf16)
    rest = table - first.astype(f32)
    second = rest.astype(bf16)
    third = (rest - second.astype(f32)).astype(bf16)
    return dot(first, selector) + dot(second, selector) + dot(third, selector)


def selectors(width, count):
    lane = iota((LANES, width * count), 1)
    row = iota((LANES, width * count), 0)
    each = one_hot(row == jnp.right_shift(lane, width.bit_length() - 1))
    tiled = one_hot(row == jnp.bitwise_and(lane, width - 1))
    return each, tiled


def row_of(xr, yr, view, axis):
    return ((xr * ROLES + yr) * V + view) * 3 + axis


def kron_rows(out, outer, inner, count, width):
    for i in range(count):
        out[i * width : (i + 1) * width, :] = (inner * outer[i : i + 1, :]).astype(bf16)


def stack3(table):
    hi, lo = split(table)
    return jnp.concatenate([hi, hi, lo], axis=0)


def lanes3(table, width):
    inside = iota(table.shape, 1) < width
    kept = jnp.where(inside, table, 0.0)
    hi, lo = split(kept)
    hi, lo = hi.astype(f32), lo.astype(f32)
    return (hi + pltpu.roll(lo, width, 1) + pltpu.roll(hi, 2 * width, 1)).astype(bf16)


def banded_y(row):
    table = toeplitz(row, BY)
    off = iota((BY, BY), 0) - iota((BY, BY), 1)
    return jnp.where(jnp.abs(off) <= RADIUS, table, 0.0)


def build_forward_kernel(taps_ref, back_ref, *refs):
    held, out, sems = refs[8:16], refs[:8], refs[16]
    copies = [pltpu.make_async_copy(a, b, sems.at[n]) for n, (a, b) in enumerate(zip(held, out))]
    each, tiled = selectors(NZ, BX)
    each16, tiled16 = selectors(STRIP, BX)
    for xr in range(ROLES):
        k_ref, y_ref, xy_ref, z_ref = held[:4] if xr == 0 else held[4:]
        n = max(xr - 1, 0)
        for v in range(V):
            def fwd(yr, e):
                r = row_of(xr, yr, v, e)
                return taps_ref[r : r + 1, :]

            def bwd(yr, e):
                r = row_of(xr, yr, v, e)
                return back_ref[r : r + 1, :]

            outer = expand(toeplitz(fwd(0, 0), BX), each)
            inner = expand(toeplitz(fwd(0, 2), NZ), tiled)
            kron_rows(k_ref.at[n, v], outer, inner, BX, NZ)
            y_ref[n, :, v * BY : (v + 1) * BY] = stack3(banded_y(bwd(0, 1)))
            for yr in (1, 2):
                outer = expand(toeplitz(bwd(yr, 0), BX), each16)
                inner = expand(toeplitz(bwd(yr, 1), STRIP), tiled16)
                kron_rows(xy_ref.at[n, yr - 1, v], outer, inner, BX, STRIP)
                z_ref[n, yr - 1, v * NZ : (v + 1) * NZ, :] = lanes3(toeplitz(fwd(yr, 2), NZ), NZ)
        if xr == 0:
            for copy in copies[:4]:
                copy.start()
    for copy in copies[4:]:
        copy.start()
    for copy in copies:
        copy.wait()


def build_adjoint_kernel(taps_ref, back_ref, *refs):
    held, out, sems = refs[8:16], refs[:8], refs[16]
    copies = [pltpu.make_async_copy(a, b, sems.at[n]) for n, (a, b) in enumerate(zip(held, out))]
    each, tiled = selectors(NZ, BX)
    each16, tiled16 = selectors(STRIP, BX)
    for xr in range(ROLES):
        k_ref, y_ref, xy_ref, z_ref = held[:4] if xr == 0 else held[4:]
        n = max(xr - 1, 0)
        for v in range(V):
            def fwd(yr, e):
                r = row_of(xr, yr, v, e)
                return taps_ref[r : r + 1, :]

            def bwd(yr, e):
                r = row_of(xr, yr, v, e)
                return back_ref[r : r + 1, :]

            outer = expand(toeplitz(bwd(0, 0), BX), each)
            inner = expand(toeplitz(bwd(0, 2), NZ), tiled) * (1.0 / V)
            kron_rows(k_ref.at[n, v], outer, inner, BX, NZ)
            y_ref[v, :, n * BY : (n + 1) * BY] = stack3(banded_y(fwd(0, 1)))
            for yr in (1, 2):
                outer = expand(toeplitz(fwd(yr, 0), BX), each16)
                inner = expand(toeplitz(fwd(yr, 1), STRIP), tiled16)
                kron_rows(xy_ref.at[n, yr - 1, v], outer, inner, BX, STRIP)
                z_ref[n, yr - 1, :, v * LANES : (v + 1) * LANES] = lanes3(
                    toeplitz(bwd(yr, 2), NZ) * (1.0 / V), NZ
                )
        if xr == 0:
            for copy in copies[:4]:
                copy.start()
    for copy in copies[4:]:
        copy.start()
    for copy in copies:
        copy.wait()


def pack_strip(field, shift):
    lane = iota((NZ, LANES), 1)
    halves = []
    for half in range(2):
        total = jnp.zeros((NZ, LANES), f32)
        for j in range(8):
            x = half * 8 + j
            moved = pltpu.roll(field[x * NZ : (x + 1) * NZ, :], shift + STRIP * j, 1)
            inside = jnp.logical_and(lane >= STRIP * j, lane < STRIP * (j + 1))
            total = jnp.where(inside, moved, total)
        halves.append(total)
    return jnp.concatenate(halves, axis=0)


def unpack_strip(halves, shift):
    lane = iota((NZ, LANES), 1)
    first = jnp.where(shift > 0, BY - STRIP, 0)
    inside = jnp.logical_and(lane >= first, lane < first + STRIP)
    rows = []
    for x in range(BX):
        half, j = x // 8, x % 8
        moved = pltpu.roll(halves[half * NZ : (half + 1) * NZ, :], 2 * LANES - shift - STRIP * j, 1)
        rows.append(jnp.where(inside, moved, 0.0))
    return jnp.concatenate(rows, axis=0)


def wide(halves):
    return jnp.concatenate([halves[:NZ], halves[NZ:]], axis=1)


def tall(strip):
    return jnp.concatenate([strip[:, :LANES], strip[:, LANES:]], axis=0)


def column3(a):
    hi, lo = split(a)
    return jnp.concatenate([hi, hi, lo, jnp.zeros_like(hi)], axis=0)


def two_rows(a, matrix):
    hi, lo = split(a)
    both = dot(jnp.concatenate([hi, lo], axis=0), matrix)
    return both[: a.shape[0]] + both[a.shape[0] :]


def two_lanes(matrix, a):
    hi, lo = split(a)
    both = dot(matrix, jnp.concatenate([hi, lo], axis=1))
    return both[:, :LANES] + both[:, LANES:]


def three_lanes(a, stacked):
    hi, lo = split(a)
    return dot(jnp.concatenate([hi, lo, hi], axis=1), stacked)


def forward_parts(sources, shifts, add):
    for field, _, (k, y, _, _) in sources:
        spread = three_lanes(field, y[...])
        for v in range(V):
            add(v, two_lanes(k[v], spread[:, v * BY : (v + 1) * BY]))
    for yr in range(2):
        totals = [jnp.zeros((NZ, 2 * LANES), f32) for _ in range(V)]
        for _, strips, (_, _, xy, z) in sources:
            along = dot(z[yr], column3(wide(strips[yr])))
            for v in range(V):
                totals[v] += two_rows(along[v * NZ : (v + 1) * NZ], xy[yr, v])
        for v in range(V):
            add(v, unpack_strip(tall(totals[v]), shifts[yr]))


def brick(refs, n):
    k, y, xy, z = refs
    return k.at[n], y.at[n], xy.at[n], z.at[n]


def adjoint_parts(count, quotient_ref, edge_ref, refs, ready=lambda v: None):
    k_ref, y_ref, xy_ref, z_ref = refs
    totals = [jnp.zeros((FIELD, LANES), f32) for _ in range(count)]
    for v in range(V):
        spread = three_lanes(quotient_ref[v], y_ref[v])
        ready(v)
        for n in range(count):
            totals[n] += two_lanes(k_ref[n, v], spread[:, n * BY : (n + 1) * BY])
    ready(V)
    strips = [[], []]
    for yr in range(2):
        packed = [wide(edge_ref[v, yr]) for v in range(V)]
        for n in range(count):
            parts = [column3(two_rows(packed[v], xy_ref[n, yr, v])) for v in range(V)]
            strips[yr].append(tall(dot(z_ref[n, yr], jnp.concatenate(parts, axis=0))))
    return totals, strips


def write_message(ref, field, strips):
    ref[:FIELD] = field
    for n in range(2):
        ref[FIELD + n * 2 * NZ : FIELD + (n + 1) * 2 * NZ] = strips[n]


def write_scaled(ref, field, strips):
    peak = jnp.max(jnp.abs(field), axis=0, keepdims=True)
    for strip in strips:
        peak = jnp.maximum(peak, jnp.max(jnp.abs(strip), axis=0, keepdims=True))
    peak = jnp.maximum(jnp.max(peak, axis=1, keepdims=True), 1e-30)
    power = PEAK - jnp.ceil(jnp.log2(peak))
    scale = jnp.exp2(power)
    write_message(ref, field * scale, [strip * scale for strip in strips])
    ref[FIELD + 4 * NZ :] = jnp.broadcast_to(power, (STRIP, LANES))


def read_scaled(ref):
    scale = jnp.exp2(-ref[FIELD + 4 * NZ : FIELD + 4 * NZ + 1, :1])
    return ref[: FIELD + 4 * NZ] * scale


def message_parts(message):
    return message[:FIELD], [message[FIELD : FIELD + 2 * NZ], message[FIELD + 2 * NZ :]]


def start_kernel(info_ref, estimate_ref, field_ref, first_ref, second_ref):
    for x in range(BX):
        field_ref[x * NZ : (x + 1) * NZ, :] = estimate_ref[:, x, :]
    field = field_ref[...]
    first_ref[...] = pack_strip(field, info_ref[0])
    second_ref[...] = pack_strip(field, info_ref[1])


def forward_first_kernel(info_ref, own_ref, first_ref, second_ref, *rest):
    far, result_ref, held, out_ref, sems = rest[:8], rest[8], rest[9:17], rest[17], rest[18]
    copies = [pltpu.make_async_copy(a, b, sems.at[n]) for n, (a, b) in enumerate(zip(far, held))]
    for copy in copies:
        copy.start()
    for copy in copies:
        copy.wait()
    center, sides = held[:4], held[4:]
    shifts = (info_ref[0], info_ref[1])
    out_ref[...] = jnp.zeros_like(out_ref)

    def add(v, part):
        out_ref[v] += part

    bricks = (brick(center, 0), brick(sides, 0), brick(sides, 1))
    messages = (own_ref[...], first_ref[...], second_ref[...])
    sources = [(*message_parts(m), matrices) for m, matrices in zip(messages, bricks)]
    forward_parts(sources, shifts, add)
    for v in range(V):
        out_ref[v] = 1.0 / out_ref[v]
    copy = pltpu.make_async_copy(out_ref, result_ref, sems.at[len(copies)])
    copy.start()
    copy.wait()


def adjoint_sides(quotient_ref, edge_ref, shifts, refs, first_ref, second_ref, ready=lambda v: None):
    for v in range(V):
        for yr in range(2):
            edge_ref[v, yr] = pack_strip(quotient_ref[v], shifts[yr])
    totals, strips = adjoint_parts(2, quotient_ref, edge_ref, refs, ready)
    write_message(first_ref, totals[0], [strips[0][0], strips[1][0]])
    write_scaled(second_ref, totals[1], [strips[0][1], strips[1][1]])


def quotient_first_kernel(info_ref, *refs):
    far, (data_ref, quotient_ref, edge_ref, first_ref, second_ref), held, sems = (
        refs[:7], refs[7:12], refs[12:19], refs[19],
    )
    pairs = list(zip(far[:4], held[:4]))
    pairs += [(far[6].at[:, v], held[6].at[:, v]) for v in range(V)]
    pairs += list(zip(far[4:6], held[4:6]))
    copies = [pltpu.make_async_copy(a, b, sems.at[n]) for n, (a, b) in enumerate(pairs)]
    for copy in copies:
        copy.start()
    table_ref, arrived_ref, inverse_ref, y_ref, xy_ref, z_ref, k_ref = held
    shifts = (info_ref[0], info_ref[1])
    copies[0].wait()
    copies[1].wait()
    planes = dot(table_ref[...], arrived_ref[...])
    copies[2].wait()
    for v in range(V):
        for x in range(BX):
            rows = slice(x * NZ, (x + 1) * NZ)
            piece = planes[v * NZ : (v + 1) * NZ, x * BY : (x + 1) * BY]
            data_ref[v, rows, :] = piece.astype(bf16)
            quotient_ref[v, rows, :] = piece * inverse_ref[v, rows, :]
    copies[3].wait()

    def ready(v):
        for copy in copies[4 + v : 5 + v] if v < V else copies[4 + V :]:
            copy.wait()

    adjoint_sides(
        quotient_ref, edge_ref, shifts, (k_ref, y_ref, xy_ref, z_ref), first_ref, second_ref, ready
    )


def adjoint_center_kernel(quotient_ref, edge_ref, k_ref, y_ref, xy_ref, z_ref, field_ref, strips_ref):
    totals, strips = adjoint_parts(1, quotient_ref, edge_ref, (k_ref, y_ref, xy_ref, z_ref))
    field_ref[...] = totals[0]
    strips_ref[0] = strips[0][0]
    strips_ref[1] = strips[1][0]


def gather_kernel(info_ref, field_ref, strips_ref, first_ref, second_ref, total_ref, up_ref, down_ref):
    second = read_scaled(second_ref)
    total = field_ref[...] + first_ref[:FIELD] + second[:FIELD]
    total_ref[...] = total
    for n, ref in enumerate((up_ref, down_ref)):
        rows = slice(FIELD + n * 2 * NZ, FIELD + (n + 1) * 2 * NZ)
        ref[: 2 * NZ] = strips_ref[n] + first_ref[rows] + second[rows]
        ref[2 * NZ :] = pack_strip(total, info_ref[n])


def gather_last_kernel(field_ref, strips_ref, first_ref, second_ref, total_ref, up_ref, down_ref):
    second = read_scaled(second_ref)
    total_ref[...] = field_ref[...] + first_ref[:FIELD] + second[:FIELD]
    for n, ref in enumerate((up_ref, down_ref)):
        rows = slice(FIELD + n * 2 * NZ, FIELD + (n + 1) * 2 * NZ)
        ref[...] = strips_ref[n] + first_ref[rows] + second[rows]


def update_kernel(
    info_ref, old_ref, total_ref, up_ref, down_ref, up_in_ref, down_in_ref, new_ref, scaled_ref
):
    half = 2 * NZ
    correction = total_ref[...]
    for n, ref in enumerate((up_in_ref, down_in_ref)):
        correction += unpack_strip(ref[:half], info_ref[n])
    field = old_ref[:FIELD] * correction
    strips = []
    for n, (ref, own) in enumerate(((up_in_ref, up_ref), (down_in_ref, down_ref))):
        rows = slice(FIELD + n * half, FIELD + (n + 1) * half)
        strips.append(old_ref[rows] * (ref[half:] + own[:half]))
    write_message(new_ref, field, strips)
    write_scaled(scaled_ref, field, strips)


def forward_center_kernel(info_ref, own_ref, k_ref, y_ref, xy_ref, z_ref, out_ref):
    shifts = (info_ref[0], info_ref[1])
    out_ref[...] = jnp.zeros_like(out_ref)

    def add(v, part):
        out_ref[v] += part

    forward_parts([(*message_parts(own_ref[...]), brick((k_ref, y_ref, xy_ref, z_ref), 0))], shifts, add)


def middle_kernel(
    info_ref, data_ref, blurred_ref, from_first_ref, from_second_ref,
    k_ref, y_ref, xy_ref, z_ref, ka_ref, ya_ref, xya_ref, za_ref,
    quotient_ref, edge_ref, first_ref, second_ref,
):
    shifts = (info_ref[0], info_ref[1])
    quotient_ref[...] = blurred_ref[...]

    def add(v, part):
        quotient_ref[v] += part

    refs = (k_ref, y_ref, xy_ref, z_ref)
    sources = [
        (*message_parts(from_first_ref[...]), brick(refs, 0)),
        (*message_parts(read_scaled(from_second_ref)), brick(refs, 1)),
    ]
    forward_parts(sources, shifts, add)
    for v in range(V):
        quotient_ref[v] = data_ref[v].astype(f32) / quotient_ref[v]
    adjoint_sides(quotient_ref, edge_ref, shifts, (ka_ref, ya_ref, xya_ref, za_ref), first_ref, second_ref)


def final_kernel(info_ref, old_ref, total_ref, up_in_ref, down_in_ref, out_ref):
    correction = total_ref[...]
    for n, ref in enumerate((up_in_ref, down_in_ref)):
        correction += unpack_strip(ref[...], info_ref[n])
    result = old_ref[:FIELD] * correction
    for x in range(BX):
        out_ref[:, x, :] = result[x * NZ : (x + 1) * NZ]


SMEM, VMEM, HBM = pltpu.SMEM, pltpu.VMEM, pltpu.HBM


def call(kernel, outs, *args, scalars=0, far=(), out_place=VMEM, scratch=(), cost=1.0):
    arrays = [(a.size, a.dtype) for a in (*args[scalars:], *far)]
    arrays += [(math.prod(s), d) for s, d in outs]
    need = sum(count * jnp.dtype(d).itemsize for count, d in arrays)
    specs = [pl.BlockSpec(memory_space=SMEM)] * scalars
    specs += [pl.BlockSpec(memory_space=VMEM)] * (len(args) - scalars)
    specs += [pl.BlockSpec(memory_space=HBM)] * len(far)
    args += tuple(pltpu.with_memory_space_constraint(a, HBM) for a in far)
    return pl.pallas_call(
        kernel,
        out_shape=[HBM(s, d) if out_place is HBM else jax.ShapeDtypeStruct(s, d) for s, d in outs],
        in_specs=specs,
        out_specs=[pl.BlockSpec(memory_space=out_place)] * len(outs),
        scratch_shapes=list(scratch),
        compiler_params=pltpu.CompilerParams(vmem_limit_bytes=need + WORKSPACE),
        cost_estimate=pl.CostEstimate(flops=0, bytes_accessed=int(cost * 3.5e6), transcendentals=0),
    )(*args)


def held(shapes):
    return [pltpu.VMEM(s, d) for s, d in shapes]


def partner_swaps(axis):
    count_x, count_y = lax.axis_size("gx"), lax.axis_size("gy")
    near, far = [], []
    for x in range(count_x):
        for y in range(count_y):
            me = x * count_y + y
            across, along = x * count_y + (y ^ 1), (x ^ 1) * count_y + y
            if axis == "gx":
                other = x - 1 if x % 2 == 0 else x + 1
                near.append((me, along))
                far.append((me, other * count_y + y if 0 <= other < count_x else across))
            else:
                other = y - 1 if y % 2 == 0 else y + 1
                near.append((me, across))
                far.append((me, x * count_y + other if 0 <= other < count_y else along))
    return near, far


def swap(axis, near_value, far_value):
    near, far = partner_swaps(axis)
    far_in = lax.ppermute(far_value, ("gx", "gy"), far)
    near_in = lax.ppermute(near_value, ("gx", "gy"), near)
    return near_in, far_in


def swap_x(near_value, far_value):
    near_in, far_in = swap("gx", near_value, far_value.astype(jnp.float16))
    return near_in, far_in.astype(f32)


def tap_tables(psf_taps, kernel_index):
    gx, gy = lax.axis_index("gx"), lax.axis_index("gy")
    even_x, even_y = gx % 2 == 0, gy % 2 == 0
    anchor = jnp.zeros((), i32)
    bordered = jnp.pad(kernel_index, ((1, 1), (1, 1), (0, 0), (0, 0)), constant_values=-1)
    around = lax.dynamic_slice(
        bordered, (gx.astype(i32), gy.astype(i32), anchor, anchor), (ROLES, ROLES, V, 3)
    )
    low, middle, high = around[:1], around[1:2], around[2:]
    around = jnp.where(
        even_x, jnp.concatenate([middle, high, low]), jnp.concatenate([middle, low, high])
    )
    low, middle, high = around[:, :1], around[:, 1:2], around[:, 2:]
    around = jnp.where(
        even_y, jnp.concatenate([middle, high, low], 1), jnp.concatenate([middle, low, high], 1)
    )
    normal = psf_taps / jnp.sum(psf_taps, axis=-1, keepdims=True)
    chosen = (around.reshape(-1)[:, None] == jnp.arange(psf_taps.shape[0], dtype=i32)).astype(f32)
    kernels = jnp.dot(chosen, normal, precision=lax.Precision.HIGHEST)
    kernels = jnp.pad(kernels, ((0, 0), (0, LANES - TAPS)))
    backward = jnp.pad(kernels[:, :TAPS][:, ::-1], ((0, 0), (0, LANES - TAPS)))
    role = jnp.arange(kernels.shape[0])
    axis, yr, xr = role % 3, role // (3 * V) % ROLES, role // (3 * V * ROLES)
    step = jnp.where(axis == 0, jnp.where(xr == 1, 1, jnp.where(xr == 2, -1, 0)), 0)
    step = step * jnp.where(even_x, 1, -1)
    step_y = jnp.where(axis == 1, jnp.where(yr == 1, 1, jnp.where(yr == 2, -1, 0)), 0)
    step = (step + step_y * jnp.where(even_y, 1, -1))[:, None]

    def moved(a, sign):
        return jnp.where(
            step * sign > 0, jnp.roll(a, -STRIP, 1), jnp.where(step * sign < 0, jnp.roll(a, STRIP, 1), a)
        )

    return moved(kernels, 1), moved(backward, -1)


def shards(estimate, stored, placement, psf_taps, kernel_index):
    devices_y = lax.axis_size("gy")
    devices = lax.axis_size("gx") * devices_y
    slots = stored.shape[0]
    cap = 2 * slots // devices
    rows = devices * cap
    plane = BX * BY
    me = (lax.axis_index("gx") * devices_y + lax.axis_index("gy")).astype(i32)

    half, message = (2 * NZ, LANES), (FIELD + 4 * NZ, LANES)
    scaled = (FIELD + 4 * NZ + STRIP, LANES)
    one, every = (FIELD, LANES), (V, FIELD, LANES)
    even_y = lax.axis_index("gy") % 2 == 0
    info = jnp.stack([jnp.where(even_y, STRIP, 0), jnp.where(even_y, 0, STRIP)]).astype(i32)
    field, up, down = call(start_kernel, [(one, f32), (half, f32), (half, f32)], info, estimate, scalars=1)
    up_in, down_in = swap("gy", up, down)
    slots_of = placement.reshape(devices, slots)
    (outgoing,) = call(
        functools.partial(route_kernel, cap),
        [((rows, plane), bf16)],
        me.reshape(1), slots_of, stored,
        scalars=1, scratch=[pltpu.VMEM((slots * BX, BY), f32)],
    )
    outgoing, up_in, down_in, psf_taps, kernel_index, slots_of = lax.optimization_barrier(
        (outgoing, up_in, down_in, psf_taps, kernel_index, slots_of)
    )
    arrived = lax.all_to_all(
        outgoing.reshape(devices, cap, plane), ("gx", "gy"), split_axis=0, concat_axis=0, tiled=True
    ).reshape(rows, plane)

    old = jnp.concatenate([field, up_in, down_in], axis=0)
    narrow = old.astype(jnp.float16)
    first, second = (a.astype(f32) for a in swap("gx", narrow, narrow))
    taps, backward = tap_tables(psf_taps, kernel_index)

    def shapes(y_of, z_shape):
        return [
            shape
            for count in (1, ROLES - 1)
            for shape in (
                ((count, V, FIELD, FIELD), bf16),
                (y_of(count), bf16),
                ((count, 2, V, 2 * LANES, 2 * LANES), bf16),
                ((count, 2) + z_shape, bf16),
            )
        ]

    forward_shapes = shapes(lambda n: (n, 3 * BY, V * BY), (V * NZ, LANES))
    adjoint_shapes = shapes(lambda n: (V, 3 * BY, n * BY), (NZ, V * LANES))
    sems = [pltpu.SemaphoreType.DMA((8,))]
    forward = call(
        build_forward_kernel, forward_shapes, taps, backward,
        out_place=HBM, scratch=held(forward_shapes) + sems, cost=3.0,
    )
    adjoint = call(
        build_adjoint_kernel, adjoint_shapes, taps, backward,
        out_place=HBM, scratch=held(adjoint_shapes) + sems, cost=3.0,
    )
    forward_center, forward_sides = forward[:4], forward[4:]
    adjoint_center, adjoint_sides = adjoint[:4], adjoint[4:]
    (inverse,) = call(
        forward_first_kernel, [(every, f32)], info, old, first, second,
        scalars=1, far=forward, out_place=HBM,
        scratch=held(forward_shapes) + [pltpu.VMEM(every, f32), pltpu.SemaphoreType.DMA((9,))], cost=5.0,
    )
    repeated = jnp.repeat(slots_of, cap, axis=0)
    (table,) = call(
        functools.partial(arrival_kernel, cap), [((slots, rows), bf16)], me.reshape(1), repeated, scalars=1,
        out_place=HBM, scratch=[pltpu.VMEM((slots, rows), bf16), pltpu.SemaphoreType.DMA],
    )

    edges = ((V, 2) + half, f32)
    k, y, xy, z = adjoint_sides
    fetched = (table, arrived, inverse, y, xy, z, k)
    outs = [(every, bf16), (every, f32), edges, (message, f32), (scaled, f32)]
    data, quotient, edge, first, second = call(
        quotient_first_kernel, outs, info, scalars=1, far=fetched,
        scratch=held([(a.shape, a.dtype) for a in fetched]) + [pltpu.SemaphoreType.DMA((len(fetched) + V - 1,))],
    )
    first, second = swap_x(first, second)
    center = [(one, f32), ((2,) + half, f32)]
    field, strips = call(adjoint_center_kernel, center, quotient, edge, *adjoint_center)
    both = (4 * NZ, LANES)
    total, up, down = call(
        gather_kernel, [(one, f32), (both, f32), (both, f32)],
        info, field, strips, first, second, scalars=1,
    )
    up_in, down_in = swap("gy", up, down)
    new, new_scaled = call(
        update_kernel, [(message, f32), (scaled, f32)],
        info, old, total, up, down, up_in, down_in, scalars=1,
    )
    first, second = swap_x(new, new_scaled)
    (blurred,) = call(forward_center_kernel, [(every, f32)], info, new, *forward_center, scalars=1)
    quotient, edge, first, second = call(
        middle_kernel, [(every, f32), edges, (message, f32), (scaled, f32)],
        info, data, blurred, first, second, *forward_sides, *adjoint_sides, scalars=1,
    )
    first, second = swap_x(first, second)
    field, strips = call(adjoint_center_kernel, center, quotient, edge, *adjoint_center)
    total, up, down = call(
        gather_last_kernel, [(one, f32), (half, f32), (half, f32)], field, strips, first, second
    )
    up_in, down_in = swap("gy", up, down)
    (refined,) = call(final_kernel, [(estimate.shape, f32)], info, new, total, up_in, down_in, scalars=1)
    return refined


def solution(mesh):
    return jax.shard_map(
        shards,
        mesh=mesh,
        in_specs=(P(None, "gx", "gy"), P(("gx", "gy"), None, None), P(), P(), P()),
        out_specs=P(None, "gx", "gy"),
        check_vma=False,
    )
```

```python
import functools
import math

import jax
import jax.numpy as jnp
from jax import lax
from jax.experimental import pallas as pl
from jax.experimental.pallas import tpu as pltpu
from jax.sharding import PartitionSpec as P

f32 = jnp.float32
bf16 = jnp.bfloat16
i32 = jnp.int32

NZ = 32
BX = 16
BY = 128
V = 4
TAPS = 31
RADIUS = 15
FIELD = BX * NZ
STRIP = 16
LANES = 128
WORKSPACE = 8 * 2**20
PEAK = 14.0
QUICK = 0.02
ROLES = 3
CENTER, NEAR, FAR = range(ROLES)
ORDER = (FAR, NEAR, CENTER)


def iota(shape, axis):
    return lax.broadcasted_iota(i32, shape, axis)


def one_hot(mask):
    return jnp.where(mask, 1.0, 0.0).astype(bf16)


def split(a):
    hi = a.astype(bf16)
    return hi, (a - hi.astype(f32)).astype(bf16)


def dot(a, b):
    return jnp.dot(a, b, preferred_element_type=f32)


def earlier(count):
    return one_hot(iota((count, count), 0) < iota((count, count), 1))


def fetch(outside, held, sems):
    copies = [pltpu.make_async_copy(a, b, sems.at[n]) for n, (a, b) in enumerate(zip(outside, held))]
    for copy in copies:
        copy.start()
    return copies


def route_kernel(cap, me_ref, slots_ref, stored_ref, out_ref, wide_ref):
    rows, slots = out_ref.shape[0], stored_ref.shape[0]
    me = me_ref[0]
    wide_ref[...] = stored_ref[...].reshape(slots * BX, BY).astype(f32)
    target = jnp.right_shift(slots_ref[pl.ds(me, 1), :], slots.bit_length() - 1)
    place = iota((rows, slots), 0) - target * cap
    marked = jnp.logical_and(place >= 0, place < cap)
    rank = dot(one_hot(marked), earlier(slots))
    chosen = one_hot(jnp.logical_and(marked, rank == place.astype(f32)))
    for x in range(0, BX, 2):
        pair = [wide_ref[pl.ds(x + n, slots, stride=BX), :].astype(bf16) for n in range(2)]
        out_ref[:, x * BY : (x + 2) * BY] = dot(chosen, jnp.concatenate(pair, axis=1)).astype(bf16)


def arrival_kernel(cap, me_ref, slots_ref, out_ref, table_ref, sem):
    rows, slots = slots_ref.shape
    item = slots_ref[...] - me_ref[0] * slots
    wanted = jnp.logical_and(item >= 0, item < slots)
    rank = dot(one_hot(wanted), earlier(slots))
    order = jnp.bitwise_and(iota((rows, slots), 0), cap - 1)
    found = jnp.logical_and(wanted, rank == order.astype(f32))
    item_of = jnp.sum(jnp.where(found, item + 1, 0).astype(f32), axis=1, keepdims=True) - 1.0
    table = jnp.where(item_of == iota((rows, slots), 1).astype(f32), 1.0, 0.0)
    table_ref[...] = table.T.astype(bf16)
    copy = pltpu.make_async_copy(table_ref, out_ref, sem)
    copy.start()
    copy.wait()


def toeplitz(row, count):
    spread = jnp.broadcast_to(row, (count, LANES))
    return pltpu.roll(spread, LANES - RADIUS, 1, stride=1, stride_axis=0)


def expand(table, selector):
    first = table.astype(bf16)
    rest = table - first.astype(f32)
    second = rest.astype(bf16)
    third = (rest - second.astype(f32)).astype(bf16)
    return dot(first, selector) + dot(second, selector) + dot(third, selector)


def selectors(width, count):
    lane = iota((LANES, width * count), 1)
    row = iota((LANES, width * count), 0)
    each = one_hot(row == jnp.right_shift(lane, width.bit_length() - 1))
    tiled = one_hot(row == jnp.bitwise_and(lane, width - 1))
    return each, tiled


def row_of(xr, yr, view, axis):
    return ((xr * ROLES + yr) * V + view) * 3 + axis


def kron_rows(out, outer, inner, count, width):
    for i in range(count):
        out[i * width : (i + 1) * width, :] = (inner * outer[i : i + 1, :]).astype(bf16)


def stack3(table):
    hi, lo = split(table)
    return jnp.concatenate([hi, hi, lo], axis=0)


def lanes3(table, width):
    inside = iota(table.shape, 1) < width
    kept = jnp.where(inside, table, 0.0)
    hi, lo = split(kept)
    hi, lo = hi.astype(f32), lo.astype(f32)
    return (hi + pltpu.roll(lo, width, 1) + pltpu.roll(hi, 2 * width, 1)).astype(bf16)


def banded_y(row):
    table = toeplitz(row, BY)
    off = iota((BY, BY), 0) - iota((BY, BY), 1)
    return jnp.where(jnp.abs(off) <= RADIUS, table, 0.0)


def build_forward_kernel(taps_ref, back_ref, *held):
    each, tiled = selectors(NZ, BX)
    each16, tiled16 = selectors(STRIP, BX)
    for n, xr in enumerate(ORDER):
        k_ref, y_ref, xy_ref, z_ref = held[4 * n : 4 * n + 4]
        for v in range(V):
            def fwd(yr, e):
                r = row_of(xr, yr, v, e)
                return taps_ref[r : r + 1, :]

            def bwd(yr, e):
                r = row_of(xr, yr, v, e)
                return back_ref[r : r + 1, :]

            outer = expand(toeplitz(fwd(0, 0), BX), each)
            inner = expand(toeplitz(fwd(0, 2), NZ), tiled)
            kron_rows(k_ref.at[v], outer, inner, BX, NZ)
            y_ref[:, v * BY : (v + 1) * BY] = stack3(banded_y(bwd(0, 1)))
            for yr in (1, 2):
                outer = expand(toeplitz(bwd(yr, 0), BX), each16)
                inner = expand(toeplitz(bwd(yr, 1), STRIP), tiled16)
                kron_rows(xy_ref.at[yr - 1, v], outer, inner, BX, STRIP)
                z_ref[yr - 1, v * NZ : (v + 1) * NZ, :] = lanes3(toeplitz(fwd(yr, 2), NZ), NZ)


def build_adjoint_kernel(taps_ref, back_ref, *refs):
    out, held, sems = refs[:12], refs[12:24], refs[24]
    copies = [pltpu.make_async_copy(a, b, sems.at[n]) for n, (a, b) in enumerate(zip(held, out))]
    each, tiled = selectors(NZ, BX)
    each16, tiled16 = selectors(STRIP, BX)
    for n, xr in enumerate(ORDER):
        k_ref, y_ref, xy_ref, z_ref = held[4 * n : 4 * n + 4]
        for v in range(V):
            def fwd(yr, e):
                r = row_of(xr, yr, v, e)
                return taps_ref[r : r + 1, :]

            def bwd(yr, e):
                r = row_of(xr, yr, v, e)
                return back_ref[r : r + 1, :]

            outer = expand(toeplitz(bwd(0, 0), BX), each)
            inner = expand(toeplitz(bwd(0, 2), NZ), tiled) * (1.0 / V)
            kron_rows(k_ref.at[v], outer, inner, BX, NZ)
            hi, lo = split(banded_y(fwd(0, 1)))
            y_ref[v, :BY, :BY] = hi
            y_ref[v, :BY, BY:] = lo
            y_ref[v, BY:, :BY] = hi
            y_ref[v, BY:, BY:] = jnp.zeros_like(hi)
            for yr in (1, 2):
                outer = expand(toeplitz(fwd(yr, 0), BX), each16)
                inner = expand(toeplitz(fwd(yr, 1), STRIP), tiled16)
                kron_rows(xy_ref.at[yr - 1, v], outer, inner, BX, STRIP)
                z_ref[yr - 1, :, v * LANES : (v + 1) * LANES] = lanes3(
                    toeplitz(bwd(yr, 2), NZ) * (1.0 / V), NZ
                )
        for copy in copies[4 * n : 4 * n + 4]:
            copy.start()
    for copy in copies:
        copy.wait()


def pack_strip(field, shift):
    lane = iota((NZ, LANES), 1)
    halves = []
    for half in range(2):
        total = jnp.zeros((NZ, LANES), f32)
        for j in range(8):
            x = half * 8 + j
            moved = pltpu.roll(field[x * NZ : (x + 1) * NZ, :], shift + STRIP * j, 1)
            inside = jnp.logical_and(lane >= STRIP * j, lane < STRIP * (j + 1))
            total = jnp.where(inside, moved, total)
        halves.append(total)
    return jnp.concatenate(halves, axis=0)


def unpack_strip(halves, shift):
    lane = iota((NZ, LANES), 1)
    first = jnp.where(shift > 0, BY - STRIP, 0)
    inside = jnp.logical_and(lane >= first, lane < first + STRIP)
    rows = []
    for x in range(BX):
        half, j = x // 8, x % 8
        moved = pltpu.roll(halves[half * NZ : (half + 1) * NZ, :], 2 * LANES - shift - STRIP * j, 1)
        rows.append(jnp.where(inside, moved, 0.0))
    return jnp.concatenate(rows, axis=0)


def wide(halves):
    return jnp.concatenate([halves[:NZ], halves[NZ:]], axis=1)


def tall(strip):
    return jnp.concatenate([strip[:, :LANES], strip[:, LANES:]], axis=0)


def column3(a):
    hi, lo = split(a)
    return jnp.concatenate([hi, hi, lo, jnp.zeros_like(hi)], axis=0)


def two_rows(a, matrix):
    hi, lo = split(a)
    both = dot(jnp.concatenate([hi, lo], axis=0), matrix)
    return both[: a.shape[0]] + both[a.shape[0] :]


def two_lanes(matrix, a):
    hi, lo = split(a)
    both = dot(matrix, jnp.concatenate([hi, lo], axis=1))
    return both[:, :LANES] + both[:, LANES:]


def three_lanes(a, stacked):
    hi, lo = split(a)
    return dot(jnp.concatenate([hi, lo, hi], axis=1), stacked)


def forward_parts(sources, shifts, add):
    for field, _, (k, y, _, _) in sources:
        spread = three_lanes(field, y[...])
        for v in range(V):
            add(v, two_lanes(k[v], spread[:, v * BY : (v + 1) * BY]))
    for yr in range(2):
        totals = [jnp.zeros((NZ, 2 * LANES), f32) for _ in range(V)]
        for _, strips, (_, _, xy, z) in sources:
            along = dot(z[yr], column3(wide(strips[yr])))
            for v in range(V):
                totals[v] += two_rows(along[v * NZ : (v + 1) * NZ], xy[yr, v])
        for v in range(V):
            add(v, unpack_strip(tall(totals[v]), shifts[yr]))


def adjoint_parts(quotient_ref, edge_ref, refs, ready=lambda v: None):
    k_ref, y_ref, xy_ref, z_ref = refs
    total = jnp.zeros((FIELD, LANES), f32)
    for v in range(V):
        hi, lo = split(quotient_ref[v])
        both = dot(jnp.concatenate([hi, lo], axis=1), y_ref[v])
        spread = both[:, :BY] + both[:, BY:]
        ready(v)
        total += two_lanes(k_ref[v], spread)
    ready(V)
    strips = []
    for yr in range(2):
        parts = [column3(two_rows(wide(edge_ref[v, yr]), xy_ref[yr, v])) for v in range(V)]
        strips.append(tall(dot(z_ref[yr], jnp.concatenate(parts, axis=0))))
    return total, strips


def write_message(ref, field, strips):
    ref[:FIELD] = field
    for n in range(2):
        ref[FIELD + n * 2 * NZ : FIELD + (n + 1) * 2 * NZ] = strips[n]


def write_scaled(ref, field, strips):
    peak = jnp.max(jnp.abs(field), axis=0, keepdims=True)
    for strip in strips:
        peak = jnp.maximum(peak, jnp.max(jnp.abs(strip), axis=0, keepdims=True))
    peak = jnp.maximum(jnp.max(peak, axis=1, keepdims=True), 1e-30)
    power = PEAK - jnp.ceil(jnp.log2(peak))
    scale = jnp.exp2(power)
    write_message(ref, field * scale, [strip * scale for strip in strips])
    ref[FIELD + 4 * NZ :] = jnp.broadcast_to(power, (STRIP, LANES))


def read_scaled(ref):
    scale = jnp.exp2(-ref[FIELD + 4 * NZ : FIELD + 4 * NZ + 1, :1])
    return ref[: FIELD + 4 * NZ] * scale


def message_parts(message):
    return message[:FIELD], [message[FIELD : FIELD + 2 * NZ], message[FIELD + 2 * NZ :]]


def start_kernel(info_ref, *refs):
    outside, (field_ref, first_ref, second_ref), held, estimate_ref, sems = (
        refs[:3], refs[3:6], refs[6:8], refs[8], refs[9],
    )
    copies = fetch(outside, (estimate_ref, *held), sems)
    copies[0].wait()
    for x in range(BX):
        field_ref[x * NZ : (x + 1) * NZ, :] = estimate_ref[:, x, :]
    field = field_ref[...]
    first_ref[...] = pack_strip(field, info_ref[0])
    second_ref[...] = pack_strip(field, info_ref[1])
    for copy in copies[1:]:
        copy.wait()


def forward_first_kernel(last, info_ref, *refs):
    before = len(refs) - (13 if last else 12)
    message_ref, matrices, kept = refs[before], refs[before + 1 : before + 5], refs[before + 5 : before + 10]
    result_ref, out_ref, sems = refs[before + 10 :] if last else (None, *refs[before + 10 :])
    copies = fetch((*matrices, message_ref), kept, sems)
    shifts = (info_ref[0], info_ref[1])
    out_ref[...] = refs[0][...] if before else jnp.zeros_like(out_ref)

    def add(v, part):
        out_ref[v] += part

    forward_parts([(*message_parts(message_ref[...]), matrices)], shifts, add)
    if last:
        for v in range(V):
            out_ref[v] = 1.0 / out_ref[v]
        copies.append(pltpu.make_async_copy(out_ref, result_ref, sems.at[len(copies)]))
        copies[-1].start()
    for copy in copies:
        copy.wait()


def adjoint_far(quotient_ref, edge_ref, shifts, refs, far_ref, ready=lambda v: None):
    for v in range(V):
        for yr in range(2):
            edge_ref[v, yr] = pack_strip(quotient_ref[v], shifts[yr])
    write_scaled(far_ref, *adjoint_parts(quotient_ref, edge_ref, refs, ready))


def quotient_first_kernel(info_ref, *refs):
    outside, (data_ref, quotient_ref, edge_ref, far_ref), held, sems = (
        refs[:7], refs[7:11], refs[11:18], refs[18],
    )
    pairs = list(zip(outside[:4], held[:4]))
    pairs += [(outside[6].at[v], held[6].at[v]) for v in range(V)]
    pairs += list(zip(outside[4:6], held[4:6]))
    copies = [pltpu.make_async_copy(a, b, sems.at[n]) for n, (a, b) in enumerate(pairs)]
    for copy in copies:
        copy.start()
    table_ref, arrived_ref, inverse_ref, y_ref, xy_ref, z_ref, k_ref = held
    shifts = (info_ref[0], info_ref[1])
    copies[0].wait()
    copies[1].wait()
    planes = dot(table_ref[...], arrived_ref[...])
    copies[2].wait()
    for v in range(V):
        for x in range(BX):
            rows = slice(x * NZ, (x + 1) * NZ)
            piece = planes[v * NZ : (v + 1) * NZ, x * BY : (x + 1) * BY]
            data_ref[v, rows, :] = piece.astype(bf16)
            quotient_ref[v, rows, :] = piece * inverse_ref[v, rows, :]
    copies[3].wait()

    def ready(v):
        for copy in copies[4 + v : 5 + v] if v < V else copies[4 + V :]:
            copy.wait()

    adjoint_far(quotient_ref, edge_ref, shifts, (k_ref, y_ref, xy_ref, z_ref), far_ref, ready)


def adjoint_near_kernel(quotient_ref, edge_ref, k_ref, y_ref, xy_ref, z_ref, near_ref):
    write_scaled(near_ref, *adjoint_parts(quotient_ref, edge_ref, (k_ref, y_ref, xy_ref, z_ref)))


def adjoint_center_kernel(quotient_ref, edge_ref, k_ref, y_ref, xy_ref, z_ref, field_ref, strips_ref):
    field, strips = adjoint_parts(quotient_ref, edge_ref, (k_ref, y_ref, xy_ref, z_ref))
    field_ref[...] = field
    strips_ref[0] = strips[0]
    strips_ref[1] = strips[1]


def gather_kernel(info_ref, field_ref, strips_ref, near_ref, far_ref, total_ref, up_ref, down_ref):
    near, far = read_scaled(near_ref), read_scaled(far_ref)
    total = field_ref[...] + near[:FIELD] + far[:FIELD]
    total_ref[...] = total
    for n, ref in enumerate((up_ref, down_ref)):
        rows = slice(FIELD + n * 2 * NZ, FIELD + (n + 1) * 2 * NZ)
        ref[: 2 * NZ] = strips_ref[n] + near[rows] + far[rows]
        ref[2 * NZ :] = pack_strip(total, info_ref[n])


def gather_last_kernel(field_ref, strips_ref, near_ref, far_ref, total_ref, up_ref, down_ref):
    near, far = read_scaled(near_ref), read_scaled(far_ref)
    total_ref[...] = field_ref[...] + near[:FIELD] + far[:FIELD]
    for n, ref in enumerate((up_ref, down_ref)):
        rows = slice(FIELD + n * 2 * NZ, FIELD + (n + 1) * 2 * NZ)
        ref[...] = strips_ref[n] + near[rows] + far[rows]


def update_kernel(
    info_ref, old_ref, total_ref, up_ref, down_ref, up_in_ref, down_in_ref, new_ref, scaled_ref
):
    half = 2 * NZ
    correction = total_ref[...]
    for n, ref in enumerate((up_in_ref, down_in_ref)):
        correction += unpack_strip(ref[:half], info_ref[n])
    field = old_ref[:FIELD] * correction
    strips = []
    for n, (ref, own) in enumerate(((up_in_ref, up_ref), (down_in_ref, down_ref))):
        rows = slice(FIELD + n * half, FIELD + (n + 1) * half)
        strips.append(old_ref[rows] * (ref[half:] + own[:half]))
    write_message(new_ref, field, strips)
    write_scaled(scaled_ref, field, strips)


def forward_center_kernel(info_ref, own_ref, k_ref, y_ref, xy_ref, z_ref, out_ref):
    shifts = (info_ref[0], info_ref[1])
    out_ref[...] = jnp.zeros_like(out_ref)

    def add(v, part):
        out_ref[v] += part

    forward_parts([(*message_parts(own_ref[...]), (k_ref, y_ref, xy_ref, z_ref))], shifts, add)


def forward_near_kernel(info_ref, blurred_ref, near_ref, k_ref, y_ref, xy_ref, z_ref, out_ref):
    shifts = (info_ref[0], info_ref[1])
    out_ref[...] = blurred_ref[...]

    def add(v, part):
        out_ref[v] += part

    forward_parts([(*message_parts(read_scaled(near_ref)), (k_ref, y_ref, xy_ref, z_ref))], shifts, add)


def middle_kernel(
    info_ref, data_ref, blurred_ref, from_far_ref, k_ref, y_ref, xy_ref, z_ref,
    ka_ref, ya_ref, xya_ref, za_ref, quotient_ref, edge_ref, far_ref,
):
    shifts = (info_ref[0], info_ref[1])
    quotient_ref[...] = blurred_ref[...]

    def add(v, part):
        quotient_ref[v] += part

    sources = [(*message_parts(read_scaled(from_far_ref)), (k_ref, y_ref, xy_ref, z_ref))]
    forward_parts(sources, shifts, add)
    for v in range(V):
        quotient_ref[v] = data_ref[v].astype(f32) / quotient_ref[v]
    adjoint_far(quotient_ref, edge_ref, shifts, (ka_ref, ya_ref, xya_ref, za_ref), far_ref)


def final_kernel(info_ref, old_ref, total_ref, up_in_ref, down_in_ref, out_ref):
    correction = total_ref[...]
    for n, ref in enumerate((up_in_ref, down_in_ref)):
        correction += unpack_strip(ref[...], info_ref[n])
    result = old_ref[:FIELD] * correction
    for x in range(BX):
        out_ref[:, x, :] = result[x * NZ : (x + 1) * NZ]


SMEM, VMEM, HBM = pltpu.SMEM, pltpu.VMEM, pltpu.HBM


def call(kernel, outs, *args, scalars=0, far=(), out_place=VMEM, scratch=(), cost=QUICK):
    arrays = [(a.size, a.dtype) for a in (*args[scalars:], *far)]
    arrays += [(math.prod(s), d) for s, d in outs]
    need = sum(count * jnp.dtype(d).itemsize for count, d in arrays)
    places = out_place if isinstance(out_place, list) else [out_place] * len(outs)
    specs = [pl.BlockSpec(memory_space=SMEM)] * scalars
    specs += [pl.BlockSpec(memory_space=VMEM)] * (len(args) - scalars)
    specs += [pl.BlockSpec(memory_space=HBM)] * len(far)
    args += tuple(pltpu.with_memory_space_constraint(a, HBM) for a in far)
    return pl.pallas_call(
        kernel,
        out_shape=[
            HBM(s, d) if where is HBM else jax.ShapeDtypeStruct(s, d) for (s, d), where in zip(outs, places)
        ],
        in_specs=specs,
        out_specs=[pl.BlockSpec(memory_space=where) for where in places],
        scratch_shapes=list(scratch),
        compiler_params=pltpu.CompilerParams(vmem_limit_bytes=need + WORKSPACE),
        cost_estimate=pl.CostEstimate(flops=0, bytes_accessed=int(cost * 3.5e6), transcendentals=0),
    )(*args)


def held(shapes):
    return [pltpu.VMEM(s, d) for s, d in shapes]


def partner_swaps(axis):
    count_x, count_y = lax.axis_size("gx"), lax.axis_size("gy")
    near, far = [], []
    for x in range(count_x):
        for y in range(count_y):
            me = x * count_y + y
            across, along = x * count_y + (y ^ 1), (x ^ 1) * count_y + y
            if axis == "gx":
                other = x - 1 if x % 2 == 0 else x + 1
                near.append((me, along))
                far.append((me, other * count_y + y if 0 <= other < count_x else across))
            else:
                other = y - 1 if y % 2 == 0 else y + 1
                near.append((me, across))
                far.append((me, x * count_y + other if 0 <= other < count_y else along))
    return near, far


def swap_near(axis, value):
    return lax.ppermute(narrow(axis, value), ("gx", "gy"), partner_swaps(axis)[0])


def swap_far(axis, value):
    return lax.ppermute(narrow(axis, value), ("gx", "gy"), partner_swaps(axis)[1])


def narrow(axis, value):
    return value.astype(jnp.float16) if axis == "gx" else value


def swap(axis, near_value, far_value):
    far_in = swap_far(axis, far_value)
    return swap_near(axis, near_value), far_in


def tap_tables(psf_taps, kernel_index):
    gx, gy = lax.axis_index("gx"), lax.axis_index("gy")
    even_x, even_y = gx % 2 == 0, gy % 2 == 0
    anchor = jnp.zeros((), i32)
    bordered = jnp.pad(kernel_index, ((1, 1), (1, 1), (0, 0), (0, 0)), constant_values=-1)
    around = lax.dynamic_slice(
        bordered, (gx.astype(i32), gy.astype(i32), anchor, anchor), (ROLES, ROLES, V, 3)
    )
    low, middle, high = around[:1], around[1:2], around[2:]
    around = jnp.where(
        even_x, jnp.concatenate([middle, high, low]), jnp.concatenate([middle, low, high])
    )
    low, middle, high = around[:, :1], around[:, 1:2], around[:, 2:]
    around = jnp.where(
        even_y, jnp.concatenate([middle, high, low], 1), jnp.concatenate([middle, low, high], 1)
    )
    normal = psf_taps / jnp.sum(psf_taps, axis=-1, keepdims=True)
    chosen = (around.reshape(-1)[:, None] == jnp.arange(psf_taps.shape[0], dtype=i32)).astype(f32)
    kernels = jnp.dot(chosen, normal, precision=lax.Precision.HIGHEST)
    kernels = jnp.pad(kernels, ((0, 0), (0, LANES - TAPS)))
    backward = jnp.pad(kernels[:, :TAPS][:, ::-1], ((0, 0), (0, LANES - TAPS)))
    role = jnp.arange(kernels.shape[0])
    axis, yr, xr = role % 3, role // (3 * V) % ROLES, role // (3 * V * ROLES)
    step = jnp.where(axis == 0, jnp.where(xr == 1, 1, jnp.where(xr == 2, -1, 0)), 0)
    step = step * jnp.where(even_x, 1, -1)
    step_y = jnp.where(axis == 1, jnp.where(yr == 1, 1, jnp.where(yr == 2, -1, 0)), 0)
    step = (step + step_y * jnp.where(even_y, 1, -1))[:, None]

    def moved(a, sign):
        return jnp.where(
            step * sign > 0, jnp.roll(a, -STRIP, 1), jnp.where(step * sign < 0, jnp.roll(a, STRIP, 1), a)
        )

    return moved(kernels, 1), moved(backward, -1)


def shards(estimate, stored, placement, psf_taps, kernel_index):
    devices_y = lax.axis_size("gy")
    devices = lax.axis_size("gx") * devices_y
    slots = stored.shape[0]
    cap = 2 * slots // devices
    rows = devices * cap
    plane = BX * BY
    me = (lax.axis_index("gx") * devices_y + lax.axis_index("gy")).astype(i32)

    half, message = (2 * NZ, LANES), (FIELD + 4 * NZ, LANES)
    scaled = (FIELD + 4 * NZ + STRIP, LANES)
    one, every = (FIELD, LANES), (V, FIELD, LANES)
    even_y = lax.axis_index("gy") % 2 == 0
    info = jnp.stack([jnp.where(even_y, STRIP, 0), jnp.where(even_y, 0, STRIP)]).astype(i32)
    slots_of = placement.reshape(devices, slots)
    field, up, down, slots_near, stored_near = call(
        start_kernel,
        [(one, f32), (half, f32), (half, f32), (slots_of.shape, i32), (stored.shape, bf16)],
        info, scalars=1, far=(estimate, slots_of, stored),
        scratch=[pltpu.VMEM(estimate.shape, f32), pltpu.SemaphoreType.DMA((3,))],
    )
    up_in, down_in = swap("gy", up, down)
    (outgoing,) = call(
        functools.partial(route_kernel, cap), [((rows, plane), bf16)], me.reshape(1), slots_near, stored_near,
        scalars=1, scratch=[pltpu.VMEM((slots * BX, BY), f32)],
    )
    outgoing, up_in, down_in, psf_taps, kernel_index, slots_of = lax.optimization_barrier(
        (outgoing, up_in, down_in, psf_taps, kernel_index, slots_of)
    )
    arrived = lax.all_to_all(
        outgoing.reshape(devices, cap, plane), ("gx", "gy"), split_axis=0, concat_axis=0, tiled=True
    ).reshape(rows, plane)

    old = jnp.concatenate([field, up_in, down_in], axis=0)
    near, far = (a.astype(f32) for a in swap("gx", old, old))
    taps, backward = tap_tables(psf_taps, kernel_index)

    def shapes(y_shape, z_shape):
        return ROLES * [
            ((V, FIELD, FIELD), bf16),
            (y_shape, bf16),
            ((2, V, 2 * LANES, 2 * LANES), bf16),
            ((2,) + z_shape, bf16),
        ]

    forward_shapes = shapes((3 * BY, V * BY), (V * NZ, LANES))
    adjoint_shapes = shapes((V, 2 * BY, 2 * BY), (NZ, V * LANES))
    sems = [pltpu.SemaphoreType.DMA((4 * ROLES,))]
    forward = call(build_forward_kernel, forward_shapes, taps, backward, cost=3.0)
    adjoint = call(
        build_adjoint_kernel, adjoint_shapes, taps, backward,
        out_place=HBM, scratch=held(adjoint_shapes) + sems, cost=4.0,
    )
    forward_far, forward_near, forward_center = forward[:4], forward[4:8], forward[8:]

    def first_part(total, source, matrices, last=False):
        return call(
            functools.partial(forward_first_kernel, last), forward_shapes[:4] + [(message, f32), (every, f32)],
            info, *total, source, *matrices, scalars=1, out_place=[HBM] * 5 + [HBM if last else VMEM],
            scratch=[pltpu.VMEM(every, f32)] * last + [pltpu.SemaphoreType.DMA((6,))],
        )

    *forward_center, old, total = first_part((), old, forward_center)
    *forward_near, _, total = first_part((total,), near, forward_near)
    *forward_far, _, inverse = first_part((total,), far, forward_far, last=True)
    adjoint_of_far, adjoint_near, adjoint_center = adjoint[:4], adjoint[4:8], adjoint[8:]
    (table,) = call(
        functools.partial(arrival_kernel, cap), [((slots, rows), bf16)],
        me.reshape(1), jnp.repeat(slots_of, cap, axis=0), scalars=1,
        out_place=HBM, scratch=[pltpu.VMEM((slots, rows), bf16), pltpu.SemaphoreType.DMA],
    )

    edges = ((V, 2) + half, f32)
    k, y, xy, z = adjoint_of_far
    fetched = (table, arrived, inverse, y, xy, z, k)
    data, quotient, edge, far = call(
        quotient_first_kernel, [(every, bf16), (every, f32), edges, (scaled, f32)],
        info, scalars=1, far=fetched, cost=QUICK,
        scratch=held([(a.shape, a.dtype) for a in fetched]) + [pltpu.SemaphoreType.DMA((len(fetched) + V - 1,))],
    )

    def sides(quotient, edge, far):
        far = swap_far("gx", far)
        (near,) = call(adjoint_near_kernel, [(scaled, f32)], quotient, edge, *adjoint_near)
        near = swap_near("gx", near)
        center = [(one, f32), ((2,) + half, f32)]
        field, strips = call(adjoint_center_kernel, center, quotient, edge, *adjoint_center, cost=QUICK)
        return field, strips, near.astype(f32), far.astype(f32)

    both = (4 * NZ, LANES)
    total, up, down = call(
        gather_kernel, [(one, f32), (both, f32), (both, f32)], info, *sides(quotient, edge, far), scalars=1
    )
    up_in, down_in = swap("gy", up, down)
    new, new_scaled = call(
        update_kernel, [(message, f32), (scaled, f32)],
        info, old, total, up, down, up_in, down_in, scalars=1,
    )
    far = swap_far("gx", new_scaled)
    near = swap_near("gx", new_scaled)
    (blurred,) = call(forward_center_kernel, [(every, f32)], info, new, *forward_center, scalars=1, cost=QUICK)
    (blurred,) = call(
        forward_near_kernel, [(every, f32)], info, blurred, near.astype(f32), *forward_near, scalars=1, cost=QUICK
    )
    quotient, edge, far = call(
        middle_kernel, [(every, f32), edges, (scaled, f32)],
        info, data, blurred, far.astype(f32), *forward_far, *adjoint_of_far, scalars=1, cost=QUICK,
    )
    total, up, down = call(
        gather_last_kernel, [(one, f32), (half, f32), (half, f32)], *sides(quotient, edge, far)
    )
    up_in, down_in = swap("gy", up, down)
    (refined,) = call(final_kernel, [(estimate.shape, f32)], info, new, total, up_in, down_in, scalars=1)
    return refined


def solution(mesh):
    return jax.shard_map(
        shards,
        mesh=mesh,
        in_specs=(P(None, "gx", "gy"), P(("gx", "gy"), None, None), P(), P(), P()),
        out_specs=P(None, "gx", "gy"),
        check_vma=False,
    )
```

```python
import functools
import math

import jax
import jax.numpy as jnp
from jax import lax
from jax.experimental import pallas as pl
from jax.experimental.pallas import tpu as pltpu
from jax.sharding import PartitionSpec as P

f32 = jnp.float32
bf16 = jnp.bfloat16
i32 = jnp.int32

NZ = 32
BX = 16
BY = 128
V = 4
TAPS = 31
RADIUS = 15
FIELD = BX * NZ
STRIP = 16
LANES = 128
WORKSPACE = 8 * 2**20
PEAK = 14.0
QUICK = 0.02
ROLES = 3
CENTER, NEAR, FAR = range(ROLES)
ORDER = (FAR, NEAR, CENTER)


def iota(shape, axis):
    return lax.broadcasted_iota(i32, shape, axis)


def one_hot(mask):
    return jnp.where(mask, 1.0, 0.0).astype(bf16)


def split(a):
    hi = a.astype(bf16)
    return hi, (a - hi.astype(f32)).astype(bf16)


def dot(a, b):
    return jnp.dot(a, b, preferred_element_type=f32)


def earlier(count):
    return one_hot(iota((count, count), 0) < iota((count, count), 1))


def fetch(outside, held, sems):
    copies = [pltpu.make_async_copy(a, b, sems.at[n]) for n, (a, b) in enumerate(zip(outside, held))]
    for copy in copies:
        copy.start()
    return copies


def route_kernel(cap, me_ref, slots_ref, stored_ref, out_ref, wide_ref):
    rows, slots = out_ref.shape[0], stored_ref.shape[0]
    me = me_ref[0]
    wide_ref[...] = stored_ref[...].reshape(slots * BX, BY).astype(f32)
    target = jnp.right_shift(slots_ref[pl.ds(me, 1), :], slots.bit_length() - 1)
    place = iota((rows, slots), 0) - target * cap
    marked = jnp.logical_and(place >= 0, place < cap)
    rank = dot(one_hot(marked), earlier(slots))
    chosen = one_hot(jnp.logical_and(marked, rank == place.astype(f32)))
    for x in range(0, BX, 2):
        pair = [wide_ref[pl.ds(x + n, slots, stride=BX), :].astype(bf16) for n in range(2)]
        out_ref[:, x * BY : (x + 2) * BY] = dot(chosen, jnp.concatenate(pair, axis=1)).astype(bf16)


def arrival_kernel(cap, me_ref, slots_ref, out_ref, table_ref, sem):
    rows, slots = slots_ref.shape
    item = slots_ref[...] - me_ref[0] * slots
    wanted = jnp.logical_and(item >= 0, item < slots)
    rank = dot(one_hot(wanted), earlier(slots))
    order = jnp.bitwise_and(iota((rows, slots), 0), cap - 1)
    found = jnp.logical_and(wanted, rank == order.astype(f32))
    item_of = jnp.sum(jnp.where(found, item + 1, 0).astype(f32), axis=1, keepdims=True) - 1.0
    table = jnp.where(item_of == iota((rows, slots), 1).astype(f32), 1.0, 0.0)
    table_ref[...] = table.T.astype(bf16)
    copy = pltpu.make_async_copy(table_ref, out_ref, sem)
    copy.start()
    copy.wait()


def toeplitz(row, count):
    spread = jnp.broadcast_to(row, (count, LANES))
    return pltpu.roll(spread, LANES - RADIUS, 1, stride=1, stride_axis=0)


def expand(table, selector):
    first = table.astype(bf16)
    rest = table - first.astype(f32)
    second = rest.astype(bf16)
    third = (rest - second.astype(f32)).astype(bf16)
    return dot(first, selector) + dot(second, selector) + dot(third, selector)


def selectors(width, count):
    lane = iota((LANES, width * count), 1)
    row = iota((LANES, width * count), 0)
    each = one_hot(row == jnp.right_shift(lane, width.bit_length() - 1))
    tiled = one_hot(row == jnp.bitwise_and(lane, width - 1))
    return each, tiled


def row_of(xr, yr, view, axis):
    return ((xr * ROLES + yr) * V + view) * 3 + axis


def kron_rows(out, outer, inner, count, width):
    for i in range(count):
        out[i * width : (i + 1) * width, :] = (inner * outer[i : i + 1, :]).astype(bf16)


def stack3(table):
    hi, lo = split(table)
    return jnp.concatenate([hi, hi, lo], axis=0)


def lanes3(table, width):
    inside = iota(table.shape, 1) < width
    kept = jnp.where(inside, table, 0.0)
    hi, lo = split(kept)
    hi, lo = hi.astype(f32), lo.astype(f32)
    return (hi + pltpu.roll(lo, width, 1) + pltpu.roll(hi, 2 * width, 1)).astype(bf16)


def banded_y(row):
    table = toeplitz(row, BY)
    off = iota((BY, BY), 0) - iota((BY, BY), 1)
    return jnp.where(jnp.abs(off) <= RADIUS, table, 0.0)


def build_forward_kernel(taps_ref, back_ref, *held):
    each, tiled = selectors(NZ, BX)
    each16, tiled16 = selectors(STRIP, BX)
    for n, xr in enumerate(ORDER):
        k_ref, y_ref, xy_ref, z_ref = held[4 * n : 4 * n + 4]
        for v in range(V):
            def fwd(yr, e):
                r = row_of(xr, yr, v, e)
                return taps_ref[r : r + 1, :]

            def bwd(yr, e):
                r = row_of(xr, yr, v, e)
                return back_ref[r : r + 1, :]

            outer = expand(toeplitz(fwd(0, 0), BX), each)
            inner = expand(toeplitz(fwd(0, 2), NZ), tiled)
            kron_rows(k_ref.at[v], outer, inner, BX, NZ)
            y_ref[:, v * BY : (v + 1) * BY] = stack3(banded_y(bwd(0, 1)))
            for yr in (1, 2):
                outer = expand(toeplitz(bwd(yr, 0), BX), each16)
                inner = expand(toeplitz(bwd(yr, 1), STRIP), tiled16)
                kron_rows(xy_ref.at[yr - 1, v], outer, inner, BX, STRIP)
                z_ref[yr - 1, v * NZ : (v + 1) * NZ, :] = lanes3(toeplitz(fwd(yr, 2), NZ), NZ)


def build_adjoint_kernel(taps_ref, back_ref, *refs):
    out, held, sems = refs[:12], refs[12:24], refs[24]
    copies = [pltpu.make_async_copy(a, b, sems.at[n]) for n, (a, b) in enumerate(zip(held, out))]
    each, tiled = selectors(NZ, BX)
    each16, tiled16 = selectors(STRIP, BX)
    for n, xr in enumerate(ORDER):
        k_ref, y_ref, xy_ref, z_ref = held[4 * n : 4 * n + 4]
        for v in range(V):
            def fwd(yr, e):
                r = row_of(xr, yr, v, e)
                return taps_ref[r : r + 1, :]

            def bwd(yr, e):
                r = row_of(xr, yr, v, e)
                return back_ref[r : r + 1, :]

            outer = expand(toeplitz(bwd(0, 0), BX), each)
            inner = expand(toeplitz(bwd(0, 2), NZ), tiled) * (1.0 / V)
            kron_rows(k_ref.at[v], outer, inner, BX, NZ)
            hi, lo = split(banded_y(fwd(0, 1)))
            y_ref[v, :BY, :BY] = hi
            y_ref[v, :BY, BY:] = lo
            y_ref[v, BY:, :BY] = hi
            y_ref[v, BY:, BY:] = jnp.zeros_like(hi)
            for yr in (1, 2):
                outer = expand(toeplitz(fwd(yr, 0), BX), each16)
                inner = expand(toeplitz(fwd(yr, 1), STRIP), tiled16)
                kron_rows(xy_ref.at[yr - 1, v], outer, inner, BX, STRIP)
                z_ref[yr - 1, :, v * LANES : (v + 1) * LANES] = lanes3(
                    toeplitz(bwd(yr, 2), NZ) * (1.0 / V), NZ
                )
        for copy in copies[4 * n : 4 * n + 4]:
            copy.start()
    for copy in copies:
        copy.wait()


def pack_strip(field, shift):
    lane = iota((NZ, LANES), 1)
    halves = []
    for half in range(2):
        total = jnp.zeros((NZ, LANES), f32)
        for j in range(8):
            x = half * 8 + j
            moved = pltpu.roll(field[x * NZ : (x + 1) * NZ, :], shift + STRIP * j, 1)
            inside = jnp.logical_and(lane >= STRIP * j, lane < STRIP * (j + 1))
            total = jnp.where(inside, moved, total)
        halves.append(total)
    return jnp.concatenate(halves, axis=0)


def unpack_strip(halves, shift):
    lane = iota((NZ, LANES), 1)
    first = jnp.where(shift > 0, BY - STRIP, 0)
    inside = jnp.logical_and(lane >= first, lane < first + STRIP)
    rows = []
    for x in range(BX):
        half, j = x // 8, x % 8
        moved = pltpu.roll(halves[half * NZ : (half + 1) * NZ, :], 2 * LANES - shift - STRIP * j, 1)
        rows.append(jnp.where(inside, moved, 0.0))
    return jnp.concatenate(rows, axis=0)


def unpack_strips(up, down, shifts):
    lane = iota((NZ, LANES), 1)
    inside = []
    for shift in shifts:
        first = jnp.where(shift > 0, BY - STRIP, 0)
        inside.append(jnp.logical_and(lane >= first, lane < first + STRIP))
    rows = []
    for x in range(BX):
        half, j = x // 8, x % 8
        moved = [
            pltpu.roll(a[half * NZ : (half + 1) * NZ, :], 2 * LANES - shift - STRIP * j, 1)
            for a, shift in zip((up, down), shifts)
        ]
        rows.append(jnp.where(inside[0], moved[0], jnp.where(inside[1], moved[1], 0.0)))
    return jnp.concatenate(rows, axis=0)


def wide(halves):
    return jnp.concatenate([halves[:NZ], halves[NZ:]], axis=1)


def tall(strip):
    return jnp.concatenate([strip[:, :LANES], strip[:, LANES:]], axis=0)


def column3(a):
    hi, lo = split(a)
    return jnp.concatenate([hi, hi, lo, jnp.zeros_like(hi)], axis=0)


def two_rows(a, matrix):
    hi, lo = split(a)
    both = dot(jnp.concatenate([hi, lo], axis=0), matrix)
    return both[: a.shape[0]] + both[a.shape[0] :]


def two_lanes(matrix, a):
    hi, lo = split(a)
    both = dot(matrix, jnp.concatenate([hi, lo], axis=1))
    return both[:, :LANES] + both[:, LANES:]


def three_lanes(a, stacked):
    hi, lo = split(a)
    return dot(jnp.concatenate([hi, lo, hi], axis=1), stacked)


def forward_parts(message, matrices, shifts, add):
    k, y, xy, z = matrices
    field, strips = message_parts(message)
    totals = []
    for yr in range(2):
        along = dot(z[yr], column3(wide(strips[yr])))
        totals.append([tall(two_rows(along[v * NZ : (v + 1) * NZ], xy[yr, v])) for v in range(V)])
    spread = three_lanes(field, y[...])
    for v in range(V):
        center = two_lanes(k[v], spread[:, v * BY : (v + 1) * BY])
        add(v, center + unpack_strips(totals[0][v], totals[1][v], shifts))


def adjoint_parts(quotient_ref, edge_ref, refs):
    k_ref, y_ref, xy_ref, z_ref = refs
    total = jnp.zeros((FIELD, LANES), f32)
    for v in range(V):
        hi, lo = split(quotient_ref[v])
        both = dot(jnp.concatenate([hi, lo], axis=1), y_ref[v])
        spread = both[:, :BY] + both[:, BY:]
        total += two_lanes(k_ref[v], spread)
    strips = []
    for yr in range(2):
        parts = [column3(two_rows(wide(edge_ref[v, yr]), xy_ref[yr, v])) for v in range(V)]
        strips.append(tall(dot(z_ref[yr], jnp.concatenate(parts, axis=0))))
    return total, strips


def write_message(ref, field, strips):
    ref[:FIELD] = field
    for n in range(2):
        ref[FIELD + n * 2 * NZ : FIELD + (n + 1) * 2 * NZ] = strips[n]


def write_scaled(ref, field, strips):
    peak = jnp.max(jnp.abs(field), axis=0, keepdims=True)
    for strip in strips:
        peak = jnp.maximum(peak, jnp.max(jnp.abs(strip), axis=0, keepdims=True))
    peak = jnp.maximum(jnp.max(peak, axis=1, keepdims=True), 1e-30)
    power = PEAK - jnp.ceil(jnp.log2(peak))
    scale = jnp.exp2(power)
    write_message(ref, field * scale, [strip * scale for strip in strips])
    ref[FIELD + 4 * NZ :] = jnp.broadcast_to(power, (STRIP, LANES))


def read_scaled(ref):
    scale = jnp.exp2(-ref[FIELD + 4 * NZ : FIELD + 4 * NZ + 1, :1])
    return ref[: FIELD + 4 * NZ] * scale


def message_parts(message):
    return message[:FIELD], [message[FIELD : FIELD + 2 * NZ], message[FIELD + 2 * NZ :]]


def start_kernel(info_ref, *refs):
    outside, (field_ref, first_ref, second_ref), held, estimate_ref, sems = (
        refs[:3], refs[3:6], refs[6:8], refs[8], refs[9],
    )
    copies = fetch(outside, (estimate_ref, *held), sems)
    copies[0].wait()
    for x in range(BX):
        field_ref[x * NZ : (x + 1) * NZ, :] = estimate_ref[:, x, :]
    field = field_ref[...]
    first_ref[...] = pack_strip(field, info_ref[0])
    second_ref[...] = pack_strip(field, info_ref[1])
    for copy in copies[1:]:
        copy.wait()


def forward_first_kernel(info_ref, *refs):
    before = len(refs) - 6
    message_ref, matrices, out_ref = refs[before], refs[before + 1 : before + 5], refs[-1]
    shifts = (info_ref[0], info_ref[1])

    def add(v, part):
        out_ref[v] = part + refs[0][v] if before else part

    forward_parts(message_ref[...], matrices, shifts, add)


def forward_inverse_kernel(info_ref, blurred_ref, message_ref, k_ref, y_ref, xy_ref, z_ref, result_ref, out_ref, sem):
    shifts = (info_ref[0], info_ref[1])

    def add(v, part):
        out_ref[v] = 1.0 / (blurred_ref[v] + part)

    forward_parts(message_ref[...], (k_ref, y_ref, xy_ref, z_ref), shifts, add)
    copy = pltpu.make_async_copy(out_ref, result_ref, sem)
    copy.start()
    copy.wait()


def pack_edges(quotient_ref, edge_ref, shifts):
    for v in range(V):
        for yr in range(2):
            edge_ref[v, yr] = pack_strip(quotient_ref[v], shifts[yr])


def quotient_first_kernel(info_ref, arrived_ref, *refs):
    outside, (data_ref, quotient_ref, edge_ref, far_ref), held, sems = (
        refs[:6], refs[6:10], refs[10:16], refs[16],
    )
    copies = fetch(outside, held, sems)
    table_ref, inverse_ref, *matrices = held
    shifts = (info_ref[0], info_ref[1])
    copies[0].wait()
    copies[1].wait()

    @pl.when(shifts[0] >= 0)
    def _():
        planes = dot(table_ref[...], arrived_ref[...])
        for v in range(V):
            for x in range(BX):
                rows = slice(x * NZ, (x + 1) * NZ)
                piece = planes[v * NZ : (v + 1) * NZ, x * BY : (x + 1) * BY]
                data_ref[v, rows, :] = piece.astype(bf16)
                quotient_ref[v, rows, :] = piece * inverse_ref[v, rows, :]
        pack_edges(quotient_ref, edge_ref, shifts)

    for copy in copies[2:]:
        copy.wait()
    write_scaled(far_ref, *adjoint_parts(quotient_ref, edge_ref, matrices))


def adjoint_side_kernel(quotient_ref, edge_ref, k_ref, y_ref, xy_ref, z_ref, message_ref):
    write_scaled(message_ref, *adjoint_parts(quotient_ref, edge_ref, (k_ref, y_ref, xy_ref, z_ref)))


def adjoint_center_kernel(quotient_ref, edge_ref, k_ref, y_ref, xy_ref, z_ref, field_ref, strips_ref):
    field, strips = adjoint_parts(quotient_ref, edge_ref, (k_ref, y_ref, xy_ref, z_ref))
    field_ref[...] = field
    strips_ref[0] = strips[0]
    strips_ref[1] = strips[1]


def gather_kernel(info_ref, field_ref, strips_ref, near_ref, far_ref, total_ref, up_ref, down_ref):
    near, far = read_scaled(near_ref), read_scaled(far_ref)
    total = field_ref[...] + near[:FIELD] + far[:FIELD]
    total_ref[...] = total
    for n, ref in enumerate((up_ref, down_ref)):
        rows = slice(FIELD + n * 2 * NZ, FIELD + (n + 1) * 2 * NZ)
        ref[: 2 * NZ] = strips_ref[n] + near[rows] + far[rows]
        ref[2 * NZ :] = pack_strip(total, info_ref[n])


def gather_last_kernel(field_ref, strips_ref, near_ref, far_ref, total_ref, up_ref, down_ref):
    near, far = read_scaled(near_ref), read_scaled(far_ref)
    total_ref[...] = field_ref[...] + near[:FIELD] + far[:FIELD]
    for n, ref in enumerate((up_ref, down_ref)):
        rows = slice(FIELD + n * 2 * NZ, FIELD + (n + 1) * 2 * NZ)
        ref[...] = strips_ref[n] + near[rows] + far[rows]


def update_kernel(
    info_ref, old_ref, total_ref, up_ref, down_ref, up_in_ref, down_in_ref, new_ref, scaled_ref
):
    half = 2 * NZ
    correction = total_ref[...]
    for n, ref in enumerate((up_in_ref, down_in_ref)):
        correction += unpack_strip(ref[:half], info_ref[n])
    field = old_ref[:FIELD] * correction
    strips = []
    for n, (ref, own) in enumerate(((up_in_ref, up_ref), (down_in_ref, down_ref))):
        rows = slice(FIELD + n * half, FIELD + (n + 1) * half)
        strips.append(old_ref[rows] * (ref[half:] + own[:half]))
    write_message(new_ref, field, strips)
    write_scaled(scaled_ref, field, strips)


def forward_center_kernel(info_ref, own_ref, k_ref, y_ref, xy_ref, z_ref, out_ref):
    shifts = (info_ref[0], info_ref[1])

    def add(v, part):
        out_ref[v] = part

    forward_parts(own_ref[...], (k_ref, y_ref, xy_ref, z_ref), shifts, add)


def forward_near_kernel(info_ref, blurred_ref, near_ref, k_ref, y_ref, xy_ref, z_ref, out_ref):
    shifts = (info_ref[0], info_ref[1])

    def add(v, part):
        out_ref[v] = blurred_ref[v] + part

    forward_parts(read_scaled(near_ref), (k_ref, y_ref, xy_ref, z_ref), shifts, add)


def middle_kernel(
    info_ref, data_ref, blurred_ref, from_far_ref, k_ref, y_ref, xy_ref, z_ref,
    ka_ref, ya_ref, xya_ref, za_ref, quotient_ref, edge_ref, far_ref,
):
    shifts = (info_ref[0], info_ref[1])

    def add(v, part):
        quotient_ref[v] = data_ref[v].astype(f32) / (blurred_ref[v] + part)

    forward_parts(read_scaled(from_far_ref), (k_ref, y_ref, xy_ref, z_ref), shifts, add)
    pack_edges(quotient_ref, edge_ref, shifts)
    write_scaled(far_ref, *adjoint_parts(quotient_ref, edge_ref, (ka_ref, ya_ref, xya_ref, za_ref)))


def final_kernel(info_ref, old_ref, total_ref, up_in_ref, down_in_ref, out_ref):
    correction = total_ref[...]
    for n, ref in enumerate((up_in_ref, down_in_ref)):
        correction += unpack_strip(ref[...], info_ref[n])
    result = old_ref[:FIELD] * correction
    for x in range(BX):
        out_ref[:, x, :] = result[x * NZ : (x + 1) * NZ]


SMEM, VMEM, HBM = pltpu.SMEM, pltpu.VMEM, pltpu.HBM


def call(kernel, outs, *args, scalars=0, far=(), out_place=VMEM, scratch=(), cost=QUICK):
    arrays = [(a.size, a.dtype) for a in (*args[scalars:], *far)]
    arrays += [(math.prod(s), d) for s, d in outs]
    need = sum(count * jnp.dtype(d).itemsize for count, d in arrays)
    places = out_place if isinstance(out_place, list) else [out_place] * len(outs)
    specs = [pl.BlockSpec(memory_space=SMEM)] * scalars
    specs += [pl.BlockSpec(memory_space=VMEM)] * (len(args) - scalars)
    specs += [pl.BlockSpec(memory_space=HBM)] * len(far)
    args += tuple(pltpu.with_memory_space_constraint(a, HBM) for a in far)
    return pl.pallas_call(
        kernel,
        out_shape=[
            HBM(s, d) if where is HBM else jax.ShapeDtypeStruct(s, d) for (s, d), where in zip(outs, places)
        ],
        in_specs=specs,
        out_specs=[pl.BlockSpec(memory_space=where) for where in places],
        scratch_shapes=list(scratch),
        compiler_params=pltpu.CompilerParams(vmem_limit_bytes=need + WORKSPACE),
        cost_estimate=pl.CostEstimate(flops=0, bytes_accessed=int(cost * 3.5e6), transcendentals=0),
    )(*args)


def held(shapes):
    return [pltpu.VMEM(s, d) for s, d in shapes]


def partner_swaps(axis):
    count_x, count_y = lax.axis_size("gx"), lax.axis_size("gy")
    near, far = [], []
    for x in range(count_x):
        for y in range(count_y):
            me = x * count_y + y
            across, along = x * count_y + (y ^ 1), (x ^ 1) * count_y + y
            if axis == "gx":
                other = x - 1 if x % 2 == 0 else x + 1
                near.append((me, along))
                far.append((me, other * count_y + y if 0 <= other < count_x else across))
            else:
                other = y - 1 if y % 2 == 0 else y + 1
                near.append((me, across))
                far.append((me, x * count_y + other if 0 <= other < count_y else along))
    return near, far


def swap_near(axis, value):
    return lax.ppermute(narrow(axis, value), ("gx", "gy"), partner_swaps(axis)[0])


def swap_far(axis, value):
    return lax.ppermute(narrow(axis, value), ("gx", "gy"), partner_swaps(axis)[1])


def narrow(axis, value):
    return value.astype(jnp.float16) if axis == "gx" else value


def swap(axis, near_value, far_value):
    far_in = swap_far(axis, far_value)
    return swap_near(axis, near_value), far_in


def tap_tables(psf_taps, kernel_index):
    gx, gy = lax.axis_index("gx"), lax.axis_index("gy")
    even_x, even_y = gx % 2 == 0, gy % 2 == 0
    anchor = jnp.zeros((), i32)
    bordered = jnp.pad(kernel_index, ((1, 1), (1, 1), (0, 0), (0, 0)), constant_values=-1)
    around = lax.dynamic_slice(
        bordered, (gx.astype(i32), gy.astype(i32), anchor, anchor), (ROLES, ROLES, V, 3)
    )
    low, middle, high = around[:1], around[1:2], around[2:]
    around = jnp.where(
        even_x, jnp.concatenate([middle, high, low]), jnp.concatenate([middle, low, high])
    )
    low, middle, high = around[:, :1], around[:, 1:2], around[:, 2:]
    around = jnp.where(
        even_y, jnp.concatenate([middle, high, low], 1), jnp.concatenate([middle, low, high], 1)
    )
    normal = psf_taps / jnp.sum(psf_taps, axis=-1, keepdims=True)
    chosen = (around.reshape(-1)[:, None] == jnp.arange(psf_taps.shape[0], dtype=i32)).astype(f32)
    kernels = jnp.dot(chosen, normal, precision=lax.Precision.HIGHEST)
    kernels = jnp.pad(kernels, ((0, 0), (0, LANES - TAPS)))
    backward = jnp.pad(kernels[:, :TAPS][:, ::-1], ((0, 0), (0, LANES - TAPS)))
    role = jnp.arange(kernels.shape[0])
    axis, yr, xr = role % 3, role // (3 * V) % ROLES, role // (3 * V * ROLES)
    step = jnp.where(axis == 0, jnp.where(xr == 1, 1, jnp.where(xr == 2, -1, 0)), 0)
    step = step * jnp.where(even_x, 1, -1)
    step_y = jnp.where(axis == 1, jnp.where(yr == 1, 1, jnp.where(yr == 2, -1, 0)), 0)
    step = (step + step_y * jnp.where(even_y, 1, -1))[:, None]

    def moved(a, sign):
        return jnp.where(
            step * sign > 0, jnp.roll(a, -STRIP, 1), jnp.where(step * sign < 0, jnp.roll(a, STRIP, 1), a)
        )

    return moved(kernels, 1), moved(backward, -1)


def shards(estimate, stored, placement, psf_taps, kernel_index):
    devices_y = lax.axis_size("gy")
    devices = lax.axis_size("gx") * devices_y
    slots = stored.shape[0]
    cap = 2 * slots // devices
    rows = devices * cap
    plane = BX * BY
    me = (lax.axis_index("gx") * devices_y + lax.axis_index("gy")).astype(i32)

    half, message = (2 * NZ, LANES), (FIELD + 4 * NZ, LANES)
    scaled = (FIELD + 4 * NZ + STRIP, LANES)
    one, every = (FIELD, LANES), (V, FIELD, LANES)
    even_y = lax.axis_index("gy") % 2 == 0
    info = jnp.stack([jnp.where(even_y, STRIP, 0), jnp.where(even_y, 0, STRIP)]).astype(i32)
    slots_of = placement.reshape(devices, slots)
    field, up, down, slots_near, stored_near = call(
        start_kernel,
        [(one, f32), (half, f32), (half, f32), (slots_of.shape, i32), (stored.shape, bf16)],
        info, scalars=1, far=(estimate, slots_of, stored),
        scratch=[pltpu.VMEM(estimate.shape, f32), pltpu.SemaphoreType.DMA((3,))],
    )
    up_in, down_in = swap("gy", up, down)
    (outgoing,) = call(
        functools.partial(route_kernel, cap), [((rows, plane), bf16)], me.reshape(1), slots_near, stored_near,
        scalars=1, scratch=[pltpu.VMEM((slots * BX, BY), f32)],
    )
    outgoing, up_in, down_in, psf_taps, kernel_index, slots_of = lax.optimization_barrier(
        (outgoing, up_in, down_in, psf_taps, kernel_index, slots_of)
    )
    arrived = lax.all_to_all(
        outgoing.reshape(devices, cap, plane), ("gx", "gy"), split_axis=0, concat_axis=0, tiled=True
    ).reshape(rows, plane)

    old = jnp.concatenate([field, up_in, down_in], axis=0)
    near, far = (a.astype(f32) for a in swap("gx", old, old))
    taps, backward = tap_tables(psf_taps, kernel_index)

    def shapes(y_shape, z_shape):
        return ROLES * [
            ((V, FIELD, FIELD), bf16),
            (y_shape, bf16),
            ((2, V, 2 * LANES, 2 * LANES), bf16),
            ((2,) + z_shape, bf16),
        ]

    forward_shapes = shapes((3 * BY, V * BY), (V * NZ, LANES))
    adjoint_shapes = shapes((V, 2 * BY, 2 * BY), (NZ, V * LANES))
    sems = [pltpu.SemaphoreType.DMA((4 * ROLES,))]
    forward = call(build_forward_kernel, forward_shapes, taps, backward, cost=3.0)
    adjoint = call(
        build_adjoint_kernel, adjoint_shapes, taps, backward,
        out_place=HBM, scratch=held(adjoint_shapes) + sems, cost=4.0,
    )
    forward_far, forward_near, forward_center = forward[:4], forward[4:8], forward[8:]

    blurred = ()
    for message_in, matrices in ((old, forward_center), (near, forward_near)):
        blurred = call(
            forward_first_kernel, [(every, f32)], info, *blurred, message_in, *matrices, scalars=1
        )
    (inverse,) = call(
        forward_inverse_kernel, [(every, f32)], info, *blurred, far, *forward_far, scalars=1,
        out_place=HBM, scratch=[pltpu.VMEM(every, f32), pltpu.SemaphoreType.DMA],
    )
    adjoint_of_far, adjoint_near, adjoint_center = adjoint[:4], adjoint[4:8], adjoint[8:]
    (table,) = call(
        functools.partial(arrival_kernel, cap), [((slots, rows), bf16)],
        me.reshape(1), jnp.repeat(slots_of, cap, axis=0), scalars=1,
        out_place=HBM, scratch=[pltpu.VMEM((slots, rows), bf16), pltpu.SemaphoreType.DMA],
    )

    edges = ((V, 2) + half, f32)
    fetched = (table, inverse, *adjoint_of_far)
    data, quotient, edge, far = call(
        quotient_first_kernel, [(every, bf16), (every, f32), edges, (scaled, f32)],
        info, arrived, scalars=1, far=fetched,
        scratch=held([(a.shape, a.dtype) for a in fetched]) + [pltpu.SemaphoreType.DMA((len(fetched),))],
    )

    def sides(quotient, edge, far):
        far = swap_far("gx", far)
        (near,) = call(adjoint_side_kernel, [(scaled, f32)], quotient, edge, *adjoint_near)
        near = swap_near("gx", near)
        center = [(one, f32), ((2,) + half, f32)]
        field, strips = call(adjoint_center_kernel, center, quotient, edge, *adjoint_center, cost=QUICK)
        return field, strips, near.astype(f32), far.astype(f32)

    both = (4 * NZ, LANES)
    total, up, down = call(
        gather_kernel, [(one, f32), (both, f32), (both, f32)], info, *sides(quotient, edge, far), scalars=1
    )
    up_in, down_in = swap("gy", up, down)
    taps, backward, up, down = lax.optimization_barrier((taps, backward, up, down))
    forward = call(build_forward_kernel, forward_shapes, taps, backward)
    old, *forward = lax.optimization_barrier((old, *forward))
    forward_far, forward_near, forward_center = forward[:4], forward[4:8], forward[8:]
    new, new_scaled = call(
        update_kernel, [(message, f32), (scaled, f32)],
        info, old, total, up, down, up_in, down_in, scalars=1,
    )
    far = swap_far("gx", new_scaled)
    near = swap_near("gx", new_scaled)
    (blurred,) = call(forward_center_kernel, [(every, f32)], info, new, *forward_center, scalars=1, cost=QUICK)
    (blurred,) = call(
        forward_near_kernel, [(every, f32)], info, blurred, near.astype(f32), *forward_near, scalars=1, cost=QUICK
    )
    quotient, edge, far = call(
        middle_kernel, [(every, f32), edges, (scaled, f32)],
        info, data, blurred, far.astype(f32), *forward_far, *adjoint_of_far, scalars=1, cost=QUICK,
    )
    total, up, down = call(
        gather_last_kernel, [(one, f32), (half, f32), (half, f32)], *sides(quotient, edge, far)
    )
    up_in, down_in = swap("gy", up, down)
    (refined,) = call(final_kernel, [(estimate.shape, f32)], info, new, total, up_in, down_in, scalars=1)
    return refined


def solution(mesh):
    return jax.shard_map(
        shards,
        mesh=mesh,
        in_specs=(P(None, "gx", "gy"), P(("gx", "gy"), None, None), P(), P(), P()),
        out_specs=P(None, "gx", "gy"),
        check_vma=False,
    )
```

```python
import functools
import math

import jax
import jax.numpy as jnp
from jax import lax
from jax.experimental import pallas as pl
from jax.experimental.pallas import tpu as pltpu
from jax.sharding import PartitionSpec as P

f32 = jnp.float32
bf16 = jnp.bfloat16
i32 = jnp.int32

NZ = 32
BX = 16
BY = 128
V = 4
TAPS = 31
RADIUS = 15
FIELD = BX * NZ
STRIP = 16
LANES = 128
WORKSPACE = 8 * 2**20
PEAK = 14.0
QUICK = 0.02
ROLES = 3
CENTER, NEAR, FAR = range(ROLES)
ORDER = (FAR, NEAR, CENTER)


def iota(shape, axis):
    return lax.broadcasted_iota(i32, shape, axis)


def one_hot(mask):
    return jnp.where(mask, 1.0, 0.0).astype(bf16)


def split(a):
    hi = a.astype(bf16)
    return hi, (a - hi.astype(f32)).astype(bf16)


def dot(a, b):
    return jnp.dot(a, b, preferred_element_type=f32)


def earlier(count):
    return one_hot(iota((count, count), 0) < iota((count, count), 1))


def fetch(outside, held, sems):
    copies = [pltpu.make_async_copy(a, b, sems.at[n]) for n, (a, b) in enumerate(zip(outside, held))]
    for copy in copies:
        copy.start()
    return copies


def route_kernel(cap, me_ref, slots_ref, stored_ref, out_ref, wide_ref):
    rows, slots = out_ref.shape[0], stored_ref.shape[0]
    me = me_ref[0]
    wide_ref[...] = stored_ref[...].reshape(slots * BX, BY).astype(f32)
    target = jnp.right_shift(slots_ref[pl.ds(me, 1), :], slots.bit_length() - 1)
    place = iota((rows, slots), 0) - target * cap
    marked = jnp.logical_and(place >= 0, place < cap)
    rank = dot(one_hot(marked), earlier(slots))
    chosen = one_hot(jnp.logical_and(marked, rank == place.astype(f32)))
    for x in range(0, BX, 2):
        pair = [wide_ref[pl.ds(x + n, slots, stride=BX), :].astype(bf16) for n in range(2)]
        out_ref[:, x * BY : (x + 2) * BY] = dot(chosen, jnp.concatenate(pair, axis=1)).astype(bf16)


def arrival_kernel(cap, me_ref, slots_ref, out_ref, table_ref, sem):
    rows, slots = slots_ref.shape
    item = slots_ref[...] - me_ref[0] * slots
    wanted = jnp.logical_and(item >= 0, item < slots)
    rank = dot(one_hot(wanted), earlier(slots))
    order = jnp.bitwise_and(iota((rows, slots), 0), cap - 1)
    found = jnp.logical_and(wanted, rank == order.astype(f32))
    item_of = jnp.sum(jnp.where(found, item + 1, 0).astype(f32), axis=1, keepdims=True) - 1.0
    table = jnp.where(item_of == iota((rows, slots), 1).astype(f32), 1.0, 0.0)
    table_ref[...] = table.T.astype(bf16)
    copy = pltpu.make_async_copy(table_ref, out_ref, sem)
    copy.start()
    copy.wait()


def toeplitz(row, count):
    spread = jnp.broadcast_to(row, (count, LANES))
    return pltpu.roll(spread, LANES - RADIUS, 1, stride=1, stride_axis=0)


def expand(table, selector):
    first = table.astype(bf16)
    rest = table - first.astype(f32)
    second = rest.astype(bf16)
    third = (rest - second.astype(f32)).astype(bf16)
    return dot(first, selector) + dot(second, selector) + dot(third, selector)


def selectors(width, count):
    lane = iota((LANES, width * count), 1)
    row = iota((LANES, width * count), 0)
    each = one_hot(row == jnp.right_shift(lane, width.bit_length() - 1))
    tiled = one_hot(row == jnp.bitwise_and(lane, width - 1))
    return each, tiled


def row_of(xr, yr, view, axis):
    return ((xr * ROLES + yr) * V + view) * 3 + axis


def kron_rows(out, outer, inner, count, width):
    for i in range(count):
        out[i * width : (i + 1) * width, :] = (inner * outer[i : i + 1, :]).astype(bf16)


def stack3(table):
    hi, lo = split(table)
    return jnp.concatenate([hi, hi, lo], axis=0)


def lanes3(table, width):
    inside = iota(table.shape, 1) < width
    kept = jnp.where(inside, table, 0.0)
    hi, lo = split(kept)
    hi, lo = hi.astype(f32), lo.astype(f32)
    return (hi + pltpu.roll(lo, width, 1) + pltpu.roll(hi, 2 * width, 1)).astype(bf16)


def banded_y(row):
    table = toeplitz(row, BY)
    off = iota((BY, BY), 0) - iota((BY, BY), 1)
    return jnp.where(jnp.abs(off) <= RADIUS, table, 0.0)


def build_forward_kernel(taps_ref, back_ref, *held):
    each, tiled = selectors(NZ, BX)
    each16, tiled16 = selectors(STRIP, BX)
    for n, xr in enumerate(ORDER):
        k_ref, y_ref, xy_ref, z_ref = held[4 * n : 4 * n + 4]
        for v in range(V):
            def fwd(yr, e):
                r = row_of(xr, yr, v, e)
                return taps_ref[r : r + 1, :]

            def bwd(yr, e):
                r = row_of(xr, yr, v, e)
                return back_ref[r : r + 1, :]

            outer = expand(toeplitz(fwd(0, 0), BX), each)
            inner = expand(toeplitz(fwd(0, 2), NZ), tiled)
            kron_rows(k_ref.at[v], outer, inner, BX, NZ)
            y_ref[:, v * BY : (v + 1) * BY] = stack3(banded_y(bwd(0, 1)))
            for yr in (1, 2):
                outer = expand(toeplitz(bwd(yr, 0), BX), each16)
                inner = expand(toeplitz(bwd(yr, 1), STRIP), tiled16)
                kron_rows(xy_ref.at[yr - 1, v], outer, inner, BX, STRIP)
                z_ref[yr - 1, v * NZ : (v + 1) * NZ, :] = lanes3(toeplitz(fwd(yr, 2), NZ), NZ)


def build_adjoint_kernel(taps_ref, back_ref, *refs):
    out, held, sems = refs[:12], refs[12:24], refs[24]
    copies = [pltpu.make_async_copy(a, b, sems.at[n]) for n, (a, b) in enumerate(zip(held, out))]
    each, tiled = selectors(NZ, BX)
    each16, tiled16 = selectors(STRIP, BX)
    for n, xr in enumerate(ORDER):
        k_ref, y_ref, xy_ref, z_ref = held[4 * n : 4 * n + 4]
        for v in range(V):
            def fwd(yr, e):
                r = row_of(xr, yr, v, e)
                return taps_ref[r : r + 1, :]

            def bwd(yr, e):
                r = row_of(xr, yr, v, e)
                return back_ref[r : r + 1, :]

            outer = expand(toeplitz(bwd(0, 0), BX), each)
            inner = expand(toeplitz(bwd(0, 2), NZ), tiled) * (1.0 / V)
            kron_rows(k_ref.at[v], outer, inner, BX, NZ)
            hi, lo = split(banded_y(fwd(0, 1)))
            y_ref[v, :BY, :BY] = hi
            y_ref[v, :BY, BY:] = lo
            y_ref[v, BY:, :BY] = hi
            y_ref[v, BY:, BY:] = jnp.zeros_like(hi)
            for yr in (1, 2):
                outer = expand(toeplitz(fwd(yr, 0), BX), each16)
                inner = expand(toeplitz(fwd(yr, 1), STRIP), tiled16)
                kron_rows(xy_ref.at[yr - 1, v], outer, inner, BX, STRIP)
                z_ref[yr - 1, :, v * LANES : (v + 1) * LANES] = lanes3(
                    toeplitz(bwd(yr, 2), NZ) * (1.0 / V), NZ
                )
        for copy in copies[4 * n : 4 * n + 4]:
            copy.start()
    for copy in copies:
        copy.wait()


def pack_strip(field, shift):
    lane = iota((NZ, LANES), 1)
    halves = []
    for half in range(2):
        total = jnp.zeros((NZ, LANES), f32)
        for j in range(8):
            x = half * 8 + j
            moved = pltpu.roll(field[x * NZ : (x + 1) * NZ, :], shift + STRIP * j, 1)
            inside = jnp.logical_and(lane >= STRIP * j, lane < STRIP * (j + 1))
            total = jnp.where(inside, moved, total)
        halves.append(total)
    return jnp.concatenate(halves, axis=0)


def unpack_strip(halves, shift):
    lane = iota((NZ, LANES), 1)
    first = jnp.where(shift > 0, BY - STRIP, 0)
    inside = jnp.logical_and(lane >= first, lane < first + STRIP)
    rows = []
    for x in range(BX):
        half, j = x // 8, x % 8
        moved = pltpu.roll(halves[half * NZ : (half + 1) * NZ, :], 2 * LANES - shift - STRIP * j, 1)
        rows.append(jnp.where(inside, moved, 0.0))
    return jnp.concatenate(rows, axis=0)


def unpack_strips(up, down, shifts):
    lane = iota((NZ, LANES), 1)
    inside = []
    for shift in shifts:
        first = jnp.where(shift > 0, BY - STRIP, 0)
        inside.append(jnp.logical_and(lane >= first, lane < first + STRIP))
    rows = []
    for x in range(BX):
        half, j = x // 8, x % 8
        moved = [
            pltpu.roll(a[half * NZ : (half + 1) * NZ, :], 2 * LANES - shift - STRIP * j, 1)
            for a, shift in zip((up, down), shifts)
        ]
        rows.append(jnp.where(inside[0], moved[0], jnp.where(inside[1], moved[1], 0.0)))
    return jnp.concatenate(rows, axis=0)


def wide(halves):
    return jnp.concatenate([halves[:NZ], halves[NZ:]], axis=1)


def tall(strip):
    return jnp.concatenate([strip[:, :LANES], strip[:, LANES:]], axis=0)


def column3(a):
    hi, lo = split(a)
    return jnp.concatenate([hi, hi, lo, jnp.zeros_like(hi)], axis=0)


def two_rows(a, matrix):
    hi, lo = split(a)
    both = dot(jnp.concatenate([hi, lo], axis=0), matrix)
    return both[: a.shape[0]] + both[a.shape[0] :]


def two_lanes(matrix, a):
    hi, lo = split(a)
    both = dot(matrix, jnp.concatenate([hi, lo], axis=1))
    return both[:, :LANES] + both[:, LANES:]


def three_lanes(a, stacked):
    hi, lo = split(a)
    return dot(jnp.concatenate([hi, lo, hi], axis=1), stacked)


def forward_parts(message, matrices, shifts, add):
    k, y, xy, z = matrices
    field, strips = message_parts(message)
    totals = []
    for yr in range(2):
        along = dot(z[yr], column3(wide(strips[yr])))
        totals.append([tall(two_rows(along[v * NZ : (v + 1) * NZ], xy[yr, v])) for v in range(V)])
    spread = three_lanes(field, y[...])
    for v in range(V):
        center = two_lanes(k[v], spread[:, v * BY : (v + 1) * BY])
        add(v, center + unpack_strips(totals[0][v], totals[1][v], shifts))


def adjoint_parts(quotient_ref, edge_ref, refs):
    k_ref, y_ref, xy_ref, z_ref = refs
    total = jnp.zeros((FIELD, LANES), f32)
    for v in range(V):
        hi, lo = split(quotient_ref[v])
        both = dot(jnp.concatenate([hi, lo], axis=1), y_ref[v])
        spread = both[:, :BY] + both[:, BY:]
        total += two_lanes(k_ref[v], spread)
    strips = []
    for yr in range(2):
        parts = [column3(two_rows(wide(edge_ref[v, yr]), xy_ref[yr, v])) for v in range(V)]
        strips.append(tall(dot(z_ref[yr], jnp.concatenate(parts, axis=0))))
    return total, strips


def write_message(ref, field, strips):
    ref[:FIELD] = field
    for n in range(2):
        ref[FIELD + n * 2 * NZ : FIELD + (n + 1) * 2 * NZ] = strips[n]


def write_scaled(ref, field, strips):
    peak = jnp.max(jnp.abs(field), axis=0, keepdims=True)
    for strip in strips:
        peak = jnp.maximum(peak, jnp.max(jnp.abs(strip), axis=0, keepdims=True))
    peak = jnp.maximum(jnp.max(peak, axis=1, keepdims=True), 1e-30)
    power = PEAK - jnp.ceil(jnp.log2(peak))
    scale = jnp.exp2(power)
    write_message(ref, field * scale, [strip * scale for strip in strips])
    ref[FIELD + 4 * NZ :] = jnp.broadcast_to(power, (STRIP, LANES))


def read_scaled(ref):
    scale = jnp.exp2(-ref[FIELD + 4 * NZ : FIELD + 4 * NZ + 1, :1])
    return ref[: FIELD + 4 * NZ] * scale


def message_parts(message):
    return message[:FIELD], [message[FIELD : FIELD + 2 * NZ], message[FIELD + 2 * NZ :]]


def start_kernel(info_ref, *refs):
    outside, (field_ref, first_ref, second_ref), held, estimate_ref, sems = (
        refs[:3], refs[3:6], refs[6:8], refs[8], refs[9],
    )
    copies = fetch(outside, (estimate_ref, *held), sems)
    copies[0].wait()
    for x in range(BX):
        field_ref[x * NZ : (x + 1) * NZ, :] = estimate_ref[:, x, :]
    field = field_ref[...]
    first_ref[...] = pack_strip(field, info_ref[0])
    second_ref[...] = pack_strip(field, info_ref[1])
    for copy in copies[1:]:
        copy.wait()


def forward_first_kernel(info_ref, *refs):
    before = len(refs) - 6
    message_ref, matrices, out_ref = refs[before], refs[before + 1 : before + 5], refs[-1]
    shifts = (info_ref[0], info_ref[1])

    def add(v, part):
        out_ref[v] = part + refs[0][v] if before else part

    forward_parts(message_ref[...], matrices, shifts, add)


def forward_inverse_kernel(info_ref, blurred_ref, message_ref, k_ref, y_ref, xy_ref, z_ref, result_ref, out_ref, sem):
    shifts = (info_ref[0], info_ref[1])

    def add(v, part):
        out_ref[v] = 1.0 / (blurred_ref[v] + part)

    forward_parts(message_ref[...], (k_ref, y_ref, xy_ref, z_ref), shifts, add)
    copy = pltpu.make_async_copy(out_ref, result_ref, sem)
    copy.start()
    copy.wait()


def pack_edges(quotient_ref, edge_ref, shifts):
    for v in range(V):
        for yr in range(2):
            edge_ref[v, yr] = pack_strip(quotient_ref[v], shifts[yr])


def quotient_first_kernel(info_ref, arrived_ref, *refs):
    outside, (data_ref, quotient_ref, edge_ref, far_ref), held, sems = (
        refs[:6], refs[6:10], refs[10:16], refs[16],
    )
    copies = fetch(outside, held, sems)
    table_ref, inverse_ref, *matrices = held
    shifts = (info_ref[0], info_ref[1])
    copies[0].wait()
    copies[1].wait()

    @pl.when(shifts[0] >= 0)
    def _():
        planes = dot(table_ref[...], arrived_ref[...])
        for v in range(V):
            for x in range(BX):
                rows = slice(x * NZ, (x + 1) * NZ)
                piece = planes[v * NZ : (v + 1) * NZ, x * BY : (x + 1) * BY]
                data_ref[v, rows, :] = piece.astype(bf16)
                quotient_ref[v, rows, :] = piece * inverse_ref[v, rows, :]
        pack_edges(quotient_ref, edge_ref, shifts)

    for copy in copies[2:]:
        copy.wait()
    write_scaled(far_ref, *adjoint_parts(quotient_ref, edge_ref, matrices))


def adjoint_side_kernel(quotient_ref, edge_ref, k_ref, y_ref, xy_ref, z_ref, message_ref):
    write_scaled(message_ref, *adjoint_parts(quotient_ref, edge_ref, (k_ref, y_ref, xy_ref, z_ref)))


def adjoint_center_kernel(quotient_ref, edge_ref, k_ref, y_ref, xy_ref, z_ref, field_ref, strips_ref):
    field, strips = adjoint_parts(quotient_ref, edge_ref, (k_ref, y_ref, xy_ref, z_ref))
    field_ref[...] = field
    strips_ref[0] = strips[0]
    strips_ref[1] = strips[1]


def gather_kernel(info_ref, field_ref, strips_ref, near_ref, far_ref, total_ref, up_ref, down_ref):
    near, far = read_scaled(near_ref), read_scaled(far_ref)
    total = field_ref[...] + near[:FIELD] + far[:FIELD]
    total_ref[...] = total
    for n, ref in enumerate((up_ref, down_ref)):
        rows = slice(FIELD + n * 2 * NZ, FIELD + (n + 1) * 2 * NZ)
        ref[: 2 * NZ] = strips_ref[n] + near[rows] + far[rows]
        ref[2 * NZ :] = pack_strip(total, info_ref[n])


def gather_last_kernel(field_ref, strips_ref, near_ref, far_ref, total_ref, up_ref, down_ref):
    near, far = read_scaled(near_ref), read_scaled(far_ref)
    total_ref[...] = field_ref[...] + near[:FIELD] + far[:FIELD]
    for n, ref in enumerate((up_ref, down_ref)):
        rows = slice(FIELD + n * 2 * NZ, FIELD + (n + 1) * 2 * NZ)
        ref[...] = strips_ref[n] + near[rows] + far[rows]


def update_kernel(
    info_ref, old_ref, total_ref, up_ref, down_ref, up_in_ref, down_in_ref, new_ref, scaled_ref
):
    half = 2 * NZ
    correction = total_ref[...]
    for n, ref in enumerate((up_in_ref, down_in_ref)):
        correction += unpack_strip(ref[:half], info_ref[n])
    field = old_ref[:FIELD] * correction
    strips = []
    for n, (ref, own) in enumerate(((up_in_ref, up_ref), (down_in_ref, down_ref))):
        rows = slice(FIELD + n * half, FIELD + (n + 1) * half)
        strips.append(old_ref[rows] * (ref[half:] + own[:half]))
    write_message(new_ref, field, strips)
    write_scaled(scaled_ref, field, strips)


def forward_center_kernel(info_ref, own_ref, k_ref, y_ref, xy_ref, z_ref, out_ref):
    shifts = (info_ref[0], info_ref[1])

    def add(v, part):
        out_ref[v] = part

    forward_parts(own_ref[...], (k_ref, y_ref, xy_ref, z_ref), shifts, add)


def forward_near_kernel(info_ref, blurred_ref, near_ref, k_ref, y_ref, xy_ref, z_ref, out_ref):
    shifts = (info_ref[0], info_ref[1])

    def add(v, part):
        out_ref[v] = blurred_ref[v] + part

    forward_parts(read_scaled(near_ref), (k_ref, y_ref, xy_ref, z_ref), shifts, add)


def middle_kernel(
    info_ref, data_ref, blurred_ref, from_far_ref, k_ref, y_ref, xy_ref, z_ref,
    ka_ref, ya_ref, xya_ref, za_ref, quotient_ref, edge_ref, far_ref,
):
    shifts = (info_ref[0], info_ref[1])

    def add(v, part):
        quotient_ref[v] = data_ref[v].astype(f32) / (blurred_ref[v] + part)

    forward_parts(read_scaled(from_far_ref), (k_ref, y_ref, xy_ref, z_ref), shifts, add)
    pack_edges(quotient_ref, edge_ref, shifts)
    write_scaled(far_ref, *adjoint_parts(quotient_ref, edge_ref, (ka_ref, ya_ref, xya_ref, za_ref)))


def final_kernel(info_ref, old_ref, total_ref, up_in_ref, down_in_ref, out_ref):
    correction = total_ref[...]
    for n, ref in enumerate((up_in_ref, down_in_ref)):
        correction += unpack_strip(ref[...], info_ref[n])
    result = old_ref[:FIELD] * correction
    for x in range(BX):
        out_ref[:, x, :] = result[x * NZ : (x + 1) * NZ]


SMEM, VMEM, HBM = pltpu.SMEM, pltpu.VMEM, pltpu.HBM


def call(kernel, outs, *args, scalars=0, far=(), out_place=VMEM, scratch=(), cost=QUICK):
    arrays = [(a.size, a.dtype) for a in (*args[scalars:], *far)]
    arrays += [(math.prod(s), d) for s, d in outs]
    need = sum(count * jnp.dtype(d).itemsize for count, d in arrays)
    places = out_place if isinstance(out_place, list) else [out_place] * len(outs)
    specs = [pl.BlockSpec(memory_space=SMEM)] * scalars
    specs += [pl.BlockSpec(memory_space=VMEM)] * (len(args) - scalars)
    specs += [pl.BlockSpec(memory_space=HBM)] * len(far)
    args += tuple(pltpu.with_memory_space_constraint(a, HBM) for a in far)
    return pl.pallas_call(
        kernel,
        out_shape=[
            HBM(s, d) if where is HBM else jax.ShapeDtypeStruct(s, d) for (s, d), where in zip(outs, places)
        ],
        in_specs=specs,
        out_specs=[pl.BlockSpec(memory_space=where) for where in places],
        scratch_shapes=list(scratch),
        compiler_params=pltpu.CompilerParams(vmem_limit_bytes=need + WORKSPACE),
        cost_estimate=pl.CostEstimate(flops=0, bytes_accessed=int(cost * 3.5e6), transcendentals=0),
    )(*args)


def held(shapes):
    return [pltpu.VMEM(s, d) for s, d in shapes]


def partner_swaps(axis):
    count_x, count_y = lax.axis_size("gx"), lax.axis_size("gy")
    near, far = [], []
    for x in range(count_x):
        for y in range(count_y):
            me = x * count_y + y
            across, along = x * count_y + (y ^ 1), (x ^ 1) * count_y + y
            if axis == "gx":
                other = x - 1 if x % 2 == 0 else x + 1
                near.append((me, along))
                far.append((me, other * count_y + y if 0 <= other < count_x else across))
            else:
                other = y - 1 if y % 2 == 0 else y + 1
                near.append((me, across))
                far.append((me, x * count_y + other if 0 <= other < count_y else along))
    return near, far


def swap_near(axis, value):
    return lax.ppermute(narrow(axis, value), ("gx", "gy"), partner_swaps(axis)[0])


def swap_far(axis, value):
    return lax.ppermute(narrow(axis, value), ("gx", "gy"), partner_swaps(axis)[1])


def narrow(axis, value):
    return value.astype(jnp.float16) if axis == "gx" else value


def swap(axis, near_value, far_value):
    far_in = swap_far(axis, far_value)
    return swap_near(axis, near_value), far_in


def tap_tables(psf_taps, kernel_index):
    gx, gy = lax.axis_index("gx"), lax.axis_index("gy")
    even_x, even_y = gx % 2 == 0, gy % 2 == 0
    anchor = jnp.zeros((), i32)
    bordered = jnp.pad(kernel_index, ((1, 1), (1, 1), (0, 0), (0, 0)), constant_values=-1)
    around = lax.dynamic_slice(
        bordered, (gx.astype(i32), gy.astype(i32), anchor, anchor), (ROLES, ROLES, V, 3)
    )
    low, middle, high = around[:1], around[1:2], around[2:]
    around = jnp.where(
        even_x, jnp.concatenate([middle, high, low]), jnp.concatenate([middle, low, high])
    )
    low, middle, high = around[:, :1], around[:, 1:2], around[:, 2:]
    around = jnp.where(
        even_y, jnp.concatenate([middle, high, low], 1), jnp.concatenate([middle, low, high], 1)
    )
    normal = psf_taps / jnp.sum(psf_taps, axis=-1, keepdims=True)
    chosen = (around.reshape(-1)[:, None] == jnp.arange(psf_taps.shape[0], dtype=i32)).astype(f32)
    kernels = jnp.dot(chosen, normal, precision=lax.Precision.HIGHEST)
    kernels = jnp.pad(kernels, ((0, 0), (0, LANES - TAPS)))
    backward = jnp.pad(kernels[:, :TAPS][:, ::-1], ((0, 0), (0, LANES - TAPS)))
    role = jnp.arange(kernels.shape[0])
    axis, yr, xr = role % 3, role // (3 * V) % ROLES, role // (3 * V * ROLES)
    step = jnp.where(axis == 0, jnp.where(xr == 1, 1, jnp.where(xr == 2, -1, 0)), 0)
    step = step * jnp.where(even_x, 1, -1)
    step_y = jnp.where(axis == 1, jnp.where(yr == 1, 1, jnp.where(yr == 2, -1, 0)), 0)
    step = (step + step_y * jnp.where(even_y, 1, -1))[:, None]

    def moved(a, sign):
        return jnp.where(
            step * sign > 0, jnp.roll(a, -STRIP, 1), jnp.where(step * sign < 0, jnp.roll(a, STRIP, 1), a)
        )

    return moved(kernels, 1), moved(backward, -1)


def shards(estimate, stored, placement, psf_taps, kernel_index):
    devices_y = lax.axis_size("gy")
    devices = lax.axis_size("gx") * devices_y
    slots = stored.shape[0]
    cap = 2 * slots // devices
    rows = devices * cap
    plane = BX * BY
    me = (lax.axis_index("gx") * devices_y + lax.axis_index("gy")).astype(i32)

    half, message = (2 * NZ, LANES), (FIELD + 4 * NZ, LANES)
    scaled = (FIELD + 4 * NZ + STRIP, LANES)
    one, every = (FIELD, LANES), (V, FIELD, LANES)
    even_y = lax.axis_index("gy") % 2 == 0
    info = jnp.stack([jnp.where(even_y, STRIP, 0), jnp.where(even_y, 0, STRIP)]).astype(i32)
    slots_of = placement.reshape(devices, slots)
    field, up, down, slots_near, stored_near = call(
        start_kernel,
        [(one, f32), (half, f32), (half, f32), (slots_of.shape, i32), (stored.shape, bf16)],
        info, scalars=1, far=(estimate, slots_of, stored),
        scratch=[pltpu.VMEM(estimate.shape, f32), pltpu.SemaphoreType.DMA((3,))],
    )
    up_in, down_in = swap("gy", up, down)
    (outgoing,) = call(
        functools.partial(route_kernel, cap), [((rows, plane), bf16)], me.reshape(1), slots_near, stored_near,
        scalars=1, scratch=[pltpu.VMEM((slots * BX, BY), f32)],
    )
    outgoing, psf_taps, kernel_index, slots_of = lax.optimization_barrier(
        (outgoing, psf_taps, kernel_index, slots_of)
    )
    arrived = lax.all_to_all(
        outgoing.reshape(devices, cap, plane), ("gx", "gy"), split_axis=0, concat_axis=0, tiled=True
    ).reshape(rows, plane)

    old = jnp.concatenate([field, up_in, down_in], axis=0)
    near, far = (a.astype(f32) for a in swap("gx", old, old))
    taps, backward = tap_tables(psf_taps, kernel_index)

    def shapes(y_shape, z_shape):
        return ROLES * [
            ((V, FIELD, FIELD), bf16),
            (y_shape, bf16),
            ((2, V, 2 * LANES, 2 * LANES), bf16),
            ((2,) + z_shape, bf16),
        ]

    forward_shapes = shapes((3 * BY, V * BY), (V * NZ, LANES))
    adjoint_shapes = shapes((V, 2 * BY, 2 * BY), (NZ, V * LANES))
    sems = [pltpu.SemaphoreType.DMA((4 * ROLES,))]
    forward = call(build_forward_kernel, forward_shapes, taps, backward, cost=3.0)
    adjoint = call(
        build_adjoint_kernel, adjoint_shapes, taps, backward,
        out_place=HBM, scratch=held(adjoint_shapes) + sems, cost=4.0,
    )
    forward_far, forward_near, forward_center = forward[:4], forward[4:8], forward[8:]

    blurred = ()
    for message_in, matrices in ((old, forward_center), (near, forward_near)):
        blurred = call(
            forward_first_kernel, [(every, f32)], info, *blurred, message_in, *matrices, scalars=1
        )
    (inverse,) = call(
        forward_inverse_kernel, [(every, f32)], info, *blurred, far, *forward_far, scalars=1,
        out_place=HBM, scratch=[pltpu.VMEM(every, f32), pltpu.SemaphoreType.DMA],
    )
    adjoint_of_far, adjoint_near, adjoint_center = adjoint[:4], adjoint[4:8], adjoint[8:]
    (table,) = call(
        functools.partial(arrival_kernel, cap), [((slots, rows), bf16)],
        me.reshape(1), jnp.repeat(slots_of, cap, axis=0), scalars=1,
        out_place=HBM, scratch=[pltpu.VMEM((slots, rows), bf16), pltpu.SemaphoreType.DMA],
    )

    edges = ((V, 2) + half, f32)
    fetched = (table, inverse, *adjoint_of_far)
    data, quotient, edge, far = call(
        quotient_first_kernel, [(every, bf16), (every, f32), edges, (scaled, f32)],
        info, arrived, scalars=1, far=fetched,
        scratch=held([(a.shape, a.dtype) for a in fetched]) + [pltpu.SemaphoreType.DMA((len(fetched),))],
    )

    def sides(quotient, edge, far):
        far = swap_far("gx", far)
        (near,) = call(adjoint_side_kernel, [(scaled, f32)], quotient, edge, *adjoint_near)
        near = swap_near("gx", near)
        center = [(one, f32), ((2,) + half, f32)]
        field, strips = call(adjoint_center_kernel, center, quotient, edge, *adjoint_center, cost=QUICK)
        return field, strips, near.astype(f32), far.astype(f32)

    both = (4 * NZ, LANES)
    total, up, down = call(
        gather_kernel, [(one, f32), (both, f32), (both, f32)], info, *sides(quotient, edge, far), scalars=1
    )
    up_in, down_in = swap("gy", up, down)
    taps, backward, up, down = lax.optimization_barrier((taps, backward, up, down))
    forward = call(build_forward_kernel, forward_shapes, taps, backward)
    old, *forward = lax.optimization_barrier((old, *forward))
    forward_far, forward_near, forward_center = forward[:4], forward[4:8], forward[8:]
    new, new_scaled = call(
        update_kernel, [(message, f32), (scaled, f32)],
        info, old, total, up, down, up_in, down_in, scalars=1,
    )
    far = swap_far("gx", new_scaled)
    near = swap_near("gx", new_scaled)
    (blurred,) = call(forward_center_kernel, [(every, f32)], info, new, *forward_center, scalars=1, cost=QUICK)
    (blurred,) = call(
        forward_near_kernel, [(every, f32)], info, blurred, near.astype(f32), *forward_near, scalars=1, cost=QUICK
    )
    quotient, edge, far = call(
        middle_kernel, [(every, f32), edges, (scaled, f32)],
        info, data, blurred, far.astype(f32), *forward_far, *adjoint_of_far, scalars=1, cost=QUICK,
    )
    total, up, down = call(
        gather_last_kernel, [(one, f32), (half, f32), (half, f32)], *sides(quotient, edge, far)
    )
    up_in, down_in = swap("gy", up, down)
    (refined,) = call(final_kernel, [(estimate.shape, f32)], info, new, total, up_in, down_in, scalars=1)
    return refined


def solution(mesh):
    return jax.shard_map(
        shards,
        mesh=mesh,
        in_specs=(P(None, "gx", "gy"), P(("gx", "gy"), None, None), P(), P(), P()),
        out_specs=P(None, "gx", "gy"),
        check_vma=False,
    )
```

```python
import functools
import math

import jax
import jax.numpy as jnp
from jax import lax
from jax.experimental import pallas as pl
from jax.experimental.pallas import tpu as pltpu
from jax.sharding import PartitionSpec as P

f32 = jnp.float32
bf16 = jnp.bfloat16
i32 = jnp.int32

NZ = 32
BX = 16
BY = 128
V = 4
TAPS = 31
RADIUS = 15
FIELD = BX * NZ
STRIP = 16
LANES = 128
WORKSPACE = 8 * 2**20
PEAK = 14.0
QUICK = 0.02
ROLES = 3
CENTER, NEAR, FAR = range(ROLES)
ORDER = (FAR, NEAR, CENTER)


def iota(shape, axis):
    return lax.broadcasted_iota(i32, shape, axis)


def one_hot(mask):
    return jnp.where(mask, 1.0, 0.0).astype(bf16)


def split(a):
    hi = a.astype(bf16)
    return hi, (a - hi.astype(f32)).astype(bf16)


def dot(a, b):
    return jnp.dot(a, b, preferred_element_type=f32)


def earlier(count):
    return one_hot(iota((count, count), 0) < iota((count, count), 1))


def fetch(outside, held, sems):
    copies = [pltpu.make_async_copy(a, b, sems.at[n]) for n, (a, b) in enumerate(zip(outside, held))]
    for copy in copies:
        copy.start()
    return copies


def route_kernel(cap, me_ref, slots_ref, stored_ref, out_ref, wide_ref):
    rows, slots = out_ref.shape[0], stored_ref.shape[0]
    me = me_ref[0]
    wide_ref[...] = stored_ref[...].reshape(slots * BX, BY).astype(f32)
    target = jnp.right_shift(slots_ref[pl.ds(me, 1), :], slots.bit_length() - 1)
    place = iota((rows, slots), 0) - target * cap
    marked = jnp.logical_and(place >= 0, place < cap)
    rank = dot(one_hot(marked), earlier(slots))
    chosen = one_hot(jnp.logical_and(marked, rank == place.astype(f32)))
    for x in range(0, BX, 2):
        pair = [wide_ref[pl.ds(x + n, slots, stride=BX), :].astype(bf16) for n in range(2)]
        out_ref[:, x * BY : (x + 2) * BY] = dot(chosen, jnp.concatenate(pair, axis=1)).astype(bf16)


def arrival_kernel(cap, me_ref, slots_ref, out_ref, table_ref, sem):
    rows, slots = slots_ref.shape
    item = slots_ref[...] - me_ref[0] * slots
    wanted = jnp.logical_and(item >= 0, item < slots)
    rank = dot(one_hot(wanted), earlier(slots))
    order = jnp.bitwise_and(iota((rows, slots), 0), cap - 1)
    found = jnp.logical_and(wanted, rank == order.astype(f32))
    item_of = jnp.sum(jnp.where(found, item + 1, 0).astype(f32), axis=1, keepdims=True) - 1.0
    table = jnp.where(item_of == iota((rows, slots), 1).astype(f32), 1.0, 0.0)
    table_ref[...] = table.T.astype(bf16)
    copy = pltpu.make_async_copy(table_ref, out_ref, sem)
    copy.start()
    copy.wait()


def toeplitz(row, count):
    spread = jnp.broadcast_to(row, (count, LANES))
    return pltpu.roll(spread, LANES - RADIUS, 1, stride=1, stride_axis=0)


def expand(table, selector):
    first = table.astype(bf16)
    rest = table - first.astype(f32)
    second = rest.astype(bf16)
    third = (rest - second.astype(f32)).astype(bf16)
    return dot(first, selector) + dot(second, selector) + dot(third, selector)


def selectors(width, count):
    lane = iota((LANES, width * count), 1)
    row = iota((LANES, width * count), 0)
    each = one_hot(row == jnp.right_shift(lane, width.bit_length() - 1))
    tiled = one_hot(row == jnp.bitwise_and(lane, width - 1))
    return each, tiled


def row_of(xr, yr, view, axis):
    return ((xr * ROLES + yr) * V + view) * 3 + axis


def kron_rows(out, outer, inner, count, width):
    for i in range(count):
        out[i * width : (i + 1) * width, :] = (inner * outer[i : i + 1, :]).astype(bf16)


def stack3(table):
    hi, lo = split(table)
    return jnp.concatenate([hi, hi, lo], axis=0)


def lanes3(table, width):
    inside = iota(table.shape, 1) < width
    kept = jnp.where(inside, table, 0.0)
    hi, lo = split(kept)
    hi, lo = hi.astype(f32), lo.astype(f32)
    return (hi + pltpu.roll(lo, width, 1) + pltpu.roll(hi, 2 * width, 1)).astype(bf16)


def banded_y(row):
    table = toeplitz(row, BY)
    off = iota((BY, BY), 0) - iota((BY, BY), 1)
    return jnp.where(jnp.abs(off) <= RADIUS, table, 0.0)


def build_forward_kernel(taps_ref, back_ref, *held):
    each, tiled = selectors(NZ, BX)
    each16, tiled16 = selectors(STRIP, BX)
    for n, xr in enumerate(ORDER):
        k_ref, y_ref, xy_ref, z_ref = held[4 * n : 4 * n + 4]
        for v in range(V):
            def fwd(yr, e):
                r = row_of(xr, yr, v, e)
                return taps_ref[r : r + 1, :]

            def bwd(yr, e):
                r = row_of(xr, yr, v, e)
                return back_ref[r : r + 1, :]

            outer = expand(toeplitz(fwd(0, 0), BX), each)
            inner = expand(toeplitz(fwd(0, 2), NZ), tiled)
            kron_rows(k_ref.at[v], outer, inner, BX, NZ)
            y_ref[:, v * BY : (v + 1) * BY] = stack3(banded_y(bwd(0, 1)))
            for yr in (1, 2):
                outer = expand(toeplitz(bwd(yr, 0), BX), each16)
                inner = expand(toeplitz(bwd(yr, 1), STRIP), tiled16)
                kron_rows(xy_ref.at[yr - 1, v], outer, inner, BX, STRIP)
                z_ref[yr - 1, v * NZ : (v + 1) * NZ, :] = lanes3(toeplitz(fwd(yr, 2), NZ), NZ)


def build_adjoint_kernel(taps_ref, back_ref, *refs):
    out, held, sems = refs[:12], refs[12:24], refs[24]
    copies = [pltpu.make_async_copy(a, b, sems.at[n]) for n, (a, b) in enumerate(zip(held, out))]
    each, tiled = selectors(NZ, BX)
    each16, tiled16 = selectors(STRIP, BX)
    for n, xr in enumerate(ORDER):
        k_ref, y_ref, xy_ref, z_ref = held[4 * n : 4 * n + 4]
        for v in range(V):
            def fwd(yr, e):
                r = row_of(xr, yr, v, e)
                return taps_ref[r : r + 1, :]

            def bwd(yr, e):
                r = row_of(xr, yr, v, e)
                return back_ref[r : r + 1, :]

            outer = expand(toeplitz(bwd(0, 0), BX), each)
            inner = expand(toeplitz(bwd(0, 2), NZ), tiled) * (1.0 / V)
            kron_rows(k_ref.at[v], outer, inner, BX, NZ)
            hi, lo = split(banded_y(fwd(0, 1)))
            y_ref[v, :BY, :BY] = hi
            y_ref[v, :BY, BY:] = lo
            y_ref[v, BY:, :BY] = hi
            y_ref[v, BY:, BY:] = jnp.zeros_like(hi)
            for yr in (1, 2):
                outer = expand(toeplitz(fwd(yr, 0), BX), each16)
                inner = expand(toeplitz(fwd(yr, 1), STRIP), tiled16)
                kron_rows(xy_ref.at[yr - 1, v], outer, inner, BX, STRIP)
                z_ref[yr - 1, :, v * LANES : (v + 1) * LANES] = lanes3(
                    toeplitz(bwd(yr, 2), NZ) * (1.0 / V), NZ
                )
        for copy in copies[4 * n : 4 * n + 4]:
            copy.start()
    for copy in copies:
        copy.wait()


def pack_strip(field, shift):
    lane = iota((NZ, LANES), 1)
    halves = []
    for half in range(2):
        total = jnp.zeros((NZ, LANES), f32)
        for j in range(8):
            x = half * 8 + j
            moved = pltpu.roll(field[x * NZ : (x + 1) * NZ, :], shift + STRIP * j, 1)
            inside = jnp.logical_and(lane >= STRIP * j, lane < STRIP * (j + 1))
            total = jnp.where(inside, moved, total)
        halves.append(total)
    return jnp.concatenate(halves, axis=0)


def unpack_strips(up, down, shifts, planes=slice(0, NZ)):
    first, last = planes.start, planes.stop
    lane = iota((last - first, LANES), 1)
    inside = []
    for shift in shifts:
        edge = jnp.where(shift > 0, BY - STRIP, 0)
        inside.append(jnp.logical_and(lane >= edge, lane < edge + STRIP))
    rows = []
    for x in range(BX):
        half, j = x // 8, x % 8
        moved = [
            pltpu.roll(a[half * NZ + first : half * NZ + last, :], 2 * LANES - shift - STRIP * j, 1)
            for a, shift in zip((up, down), shifts)
        ]
        rows.append(jnp.where(inside[0], moved[0], jnp.where(inside[1], moved[1], 0.0)))
    return jnp.concatenate(rows, axis=0)


def wide(halves):
    return jnp.concatenate([halves[:NZ], halves[NZ:]], axis=1)


def tall(strip):
    return jnp.concatenate([strip[:, :LANES], strip[:, LANES:]], axis=0)


def column3(a):
    hi, lo = split(a)
    return jnp.concatenate([hi, hi, lo, jnp.zeros_like(hi)], axis=0)


def two_rows(a, matrix):
    hi, lo = split(a)
    both = dot(jnp.concatenate([hi, lo], axis=0), matrix)
    return both[: a.shape[0]] + both[a.shape[0] :]


def two_lanes(matrix, a):
    hi, lo = split(a)
    both = dot(matrix, jnp.concatenate([hi, lo], axis=1))
    return both[:, :LANES] + both[:, LANES:]


def three_lanes(a, stacked):
    hi, lo = split(a)
    return dot(jnp.concatenate([hi, lo, hi], axis=1), stacked)


def forward_parts(message, matrices, shifts, add):
    k, y, xy, z = matrices
    field, strips = message_parts(message)
    spread = three_lanes(field, y[...])
    alongs = [dot(z[yr], column3(wide(strips[yr]))) for yr in range(2)]
    for v in range(V):
        center = two_lanes(k[v], spread[:, v * BY : (v + 1) * BY])
        rows = slice(v * NZ, (v + 1) * NZ)
        up, down = [tall(two_rows(alongs[yr][rows], xy[yr, v])) for yr in range(2)]
        add(v, center + unpack_strips(up, down, shifts))


def adjoint_parts(quotient_ref, edge_ref, refs):
    k_ref, y_ref, xy_ref, z_ref = refs
    columns = []
    for v in range(V):
        hi, lo = split(quotient_ref[v])
        both = dot(jnp.concatenate([hi, lo], axis=1), y_ref[v])
        columns.append(jnp.concatenate(split(both[:, :BY] + both[:, BY:]), axis=1))
    both = dot(
        jnp.concatenate([k_ref[v] for v in range(V)], axis=1), jnp.concatenate(columns, axis=0)
    )
    strips = []
    for yr in range(2):
        parts = [column3(two_rows(wide(edge_ref[v, yr]), xy_ref[yr, v])) for v in range(V)]
        strips.append(tall(dot(z_ref[yr], jnp.concatenate(parts, axis=0))))
    return both[:, :BY] + both[:, BY:], strips


def write_message(ref, field, strips):
    ref[:FIELD] = field
    for n in range(2):
        ref[FIELD + n * 2 * NZ : FIELD + (n + 1) * 2 * NZ] = strips[n]


def write_scaled(ref, field, strips):
    peak = jnp.max(jnp.abs(field), axis=0, keepdims=True)
    for strip in strips:
        peak = jnp.maximum(peak, jnp.max(jnp.abs(strip), axis=0, keepdims=True))
    peak = jnp.maximum(jnp.max(peak, axis=1, keepdims=True), 1e-30)
    power = PEAK - jnp.ceil(jnp.log2(peak))
    scale = jnp.exp2(power)
    write_message(ref, field * scale, [strip * scale for strip in strips])
    ref[FIELD + 4 * NZ :] = jnp.broadcast_to(power, (STRIP, LANES))


def read_scaled(ref):
    scale = jnp.exp2(-ref[FIELD + 4 * NZ : FIELD + 4 * NZ + 1, :1])
    return ref[: FIELD + 4 * NZ] * scale


def message_parts(message):
    return message[:FIELD], [message[FIELD : FIELD + 2 * NZ], message[FIELD + 2 * NZ :]]


def start_kernel(info_ref, *refs):
    outside, (field_ref, first_ref, second_ref), held, estimate_ref, sems = (
        refs[:3], refs[3:6], refs[6:8], refs[8], refs[9],
    )
    copies = fetch(outside, (estimate_ref, *held), sems)
    copies[0].wait()

    @pl.when(info_ref[0] >= 0)
    def _():
        for x in range(BX):
            field_ref[x * NZ : (x + 1) * NZ, :] = estimate_ref[:, x, :]
        field = field_ref[...]
        first_ref[...] = pack_strip(field, info_ref[0])
        second_ref[...] = pack_strip(field, info_ref[1])

    for copy in copies[1:]:
        copy.wait()


def forward_first_kernel(info_ref, *refs):
    before = len(refs) - 6
    message_ref, matrices, out_ref = refs[before], refs[before + 1 : before + 5], refs[-1]
    shifts = (info_ref[0], info_ref[1])

    def add(v, part):
        out_ref[v] = part + refs[0][v] if before else part

    forward_parts(message_ref[...], matrices, shifts, add)


def forward_inverse_kernel(info_ref, blurred_ref, message_ref, k_ref, y_ref, xy_ref, z_ref, result_ref, out_ref, sem):
    shifts = (info_ref[0], info_ref[1])

    def add(v, part):
        out_ref[v] = 1.0 / (blurred_ref[v] + part)

    forward_parts(message_ref[...], (k_ref, y_ref, xy_ref, z_ref), shifts, add)
    copy = pltpu.make_async_copy(out_ref, result_ref, sem)
    copy.start()
    copy.wait()


def pack_edges(quotient_ref, edge_ref, shifts):
    for v in range(V):
        for yr in range(2):
            edge_ref[v, yr] = pack_strip(quotient_ref[v], shifts[yr])


def quotient_first_kernel(info_ref, arrived_ref, *refs):
    outside, (data_ref, quotient_ref, edge_ref, far_ref), held, planes_ref, sems = (
        refs[:6], refs[6:10], refs[10:16], refs[16], refs[17],
    )
    parts = [(outside[0], held[0])] + [(outside[1].at[v], held[1].at[v]) for v in range(V)]
    parts += list(zip(outside[2:], held[2:]))
    copies = fetch(*zip(*parts), sems)
    table_ref, inverse_ref, *matrices = held
    shifts = (info_ref[0], info_ref[1])
    copies[0].wait()

    @pl.when(shifts[0] >= 0)
    def _():
        planes_ref[...] = dot(table_ref[...], arrived_ref[...])

    for v in range(V):
        copies[1 + v].wait()

        @pl.when(shifts[0] >= 0)
        def _():
            for x in range(BX):
                rows = slice(x * NZ, (x + 1) * NZ)
                piece = planes_ref[v * NZ : (v + 1) * NZ, x * BY : (x + 1) * BY]
                data_ref[v, rows, :] = piece.astype(bf16)
                quotient_ref[v, rows, :] = piece * inverse_ref[v, rows, :]
            for yr in range(2):
                edge_ref[v, yr] = pack_strip(quotient_ref[v], shifts[yr])

    for copy in copies[1 + V :]:
        copy.wait()
    write_scaled(far_ref, *adjoint_parts(quotient_ref, edge_ref, matrices))


def adjoint_side_kernel(quotient_ref, edge_ref, k_ref, y_ref, xy_ref, z_ref, message_ref):
    write_scaled(message_ref, *adjoint_parts(quotient_ref, edge_ref, (k_ref, y_ref, xy_ref, z_ref)))


def adjoint_center_kernel(quotient_ref, edge_ref, k_ref, y_ref, xy_ref, z_ref, field_ref, strips_ref):
    field, strips = adjoint_parts(quotient_ref, edge_ref, (k_ref, y_ref, xy_ref, z_ref))
    field_ref[...] = field
    strips_ref[0] = strips[0]
    strips_ref[1] = strips[1]


def gather_kernel(info_ref, field_ref, strips_ref, near_ref, far_ref, total_ref, up_ref, down_ref):
    near, far = read_scaled(near_ref), read_scaled(far_ref)
    total = field_ref[...] + near[:FIELD] + far[:FIELD]
    total_ref[...] = total
    for n, ref in enumerate((up_ref, down_ref)):
        rows = slice(FIELD + n * 2 * NZ, FIELD + (n + 1) * 2 * NZ)
        ref[: 2 * NZ] = strips_ref[n] + near[rows] + far[rows]
        ref[2 * NZ :] = pack_strip(total, info_ref[n])


def gather_last_kernel(field_ref, strips_ref, near_ref, far_ref, total_ref, up_ref, down_ref):
    near, far = read_scaled(near_ref), read_scaled(far_ref)
    total_ref[...] = field_ref[...] + near[:FIELD] + far[:FIELD]
    for n, ref in enumerate((up_ref, down_ref)):
        rows = slice(FIELD + n * 2 * NZ, FIELD + (n + 1) * 2 * NZ)
        ref[...] = strips_ref[n] + near[rows] + far[rows]


def update_kernel(
    info_ref, old_ref, total_ref, up_ref, down_ref, up_in_ref, down_in_ref, new_ref, scaled_ref
):
    half = 2 * NZ
    shifts = (info_ref[0], info_ref[1])
    field = old_ref[:FIELD] * (total_ref[...] + unpack_strips(up_in_ref[:half], down_in_ref[:half], shifts))
    strips = []
    for n, (ref, own) in enumerate(((up_in_ref, up_ref), (down_in_ref, down_ref))):
        rows = slice(FIELD + n * half, FIELD + (n + 1) * half)
        strips.append(old_ref[rows] * (ref[half:] + own[:half]))
    write_message(new_ref, field, strips)
    write_scaled(scaled_ref, field, strips)


def forward_center_kernel(info_ref, own_ref, k_ref, y_ref, xy_ref, z_ref, out_ref):
    shifts = (info_ref[0], info_ref[1])

    def add(v, part):
        out_ref[v] = part

    forward_parts(own_ref[...], (k_ref, y_ref, xy_ref, z_ref), shifts, add)


def forward_near_kernel(info_ref, blurred_ref, near_ref, k_ref, y_ref, xy_ref, z_ref, out_ref):
    shifts = (info_ref[0], info_ref[1])

    def add(v, part):
        out_ref[v] = blurred_ref[v] + part

    forward_parts(read_scaled(near_ref), (k_ref, y_ref, xy_ref, z_ref), shifts, add)


def middle_kernel(
    info_ref, data_ref, blurred_ref, from_far_ref, k_ref, y_ref, xy_ref, z_ref,
    ka_ref, ya_ref, xya_ref, za_ref, quotient_ref, edge_ref, far_ref,
):
    shifts = (info_ref[0], info_ref[1])

    def add(v, part):
        quotient_ref[v] = data_ref[v].astype(f32) / (blurred_ref[v] + part)

    forward_parts(read_scaled(from_far_ref), (k_ref, y_ref, xy_ref, z_ref), shifts, add)
    pack_edges(quotient_ref, edge_ref, shifts)
    write_scaled(far_ref, *adjoint_parts(quotient_ref, edge_ref, (ka_ref, ya_ref, xya_ref, za_ref)))


def final_kernel(info_ref, old_ref, total_ref, up_in_ref, down_in_ref, out_ref, held_ref, sems):
    shifts = (info_ref[0], info_ref[1])
    half = NZ // 2
    copies = []
    for n in range(2):

        @pl.when(shifts[0] >= 0)
        def _():
            edges = unpack_strips(up_in_ref[...], down_in_ref[...], shifts, slice(n * half, (n + 1) * half))
            for x in range(BX):
                rows = slice(x * NZ + n * half, x * NZ + (n + 1) * half)
                correction = total_ref[rows] + edges[x * half : (x + 1) * half]
                held_ref[n * half : (n + 1) * half, x, :] = old_ref[rows] * correction

        part = slice(n * half, (n + 1) * half)
        copies.append(pltpu.make_async_copy(held_ref.at[part], out_ref.at[part], sems.at[n]))
        copies[-1].start()
    for copy in copies:
        copy.wait()


SMEM, VMEM, HBM = pltpu.SMEM, pltpu.VMEM, pltpu.HBM


def call(kernel, outs, *args, scalars=0, far=(), out_place=VMEM, scratch=(), cost=QUICK):
    arrays = [(a.size, a.dtype) for a in (*args[scalars:], *far)]
    arrays += [(math.prod(s), d) for s, d in outs]
    need = sum(count * jnp.dtype(d).itemsize for count, d in arrays)
    places = out_place if isinstance(out_place, list) else [out_place] * len(outs)
    specs = [pl.BlockSpec(memory_space=SMEM)] * scalars
    specs += [pl.BlockSpec(memory_space=VMEM)] * (len(args) - scalars)
    specs += [pl.BlockSpec(memory_space=HBM)] * len(far)
    args += tuple(pltpu.with_memory_space_constraint(a, HBM) for a in far)
    return pl.pallas_call(
        kernel,
        out_shape=[
            HBM(s, d) if where is HBM else jax.ShapeDtypeStruct(s, d) for (s, d), where in zip(outs, places)
        ],
        in_specs=specs,
        out_specs=[pl.BlockSpec(memory_space=where) for where in places],
        scratch_shapes=list(scratch),
        compiler_params=pltpu.CompilerParams(vmem_limit_bytes=need + WORKSPACE),
        cost_estimate=pl.CostEstimate(flops=0, bytes_accessed=int(cost * 3.5e6), transcendentals=0),
    )(*args)


def held(shapes):
    return [pltpu.VMEM(s, d) for s, d in shapes]


def partner_swaps(axis):
    count_x, count_y = lax.axis_size("gx"), lax.axis_size("gy")
    near, far = [], []
    for x in range(count_x):
        for y in range(count_y):
            me = x * count_y + y
            across, along = x * count_y + (y ^ 1), (x ^ 1) * count_y + y
            if axis == "gx":
                other = x - 1 if x % 2 == 0 else x + 1
                near.append((me, along))
                far.append((me, other * count_y + y if 0 <= other < count_x else across))
            else:
                other = y - 1 if y % 2 == 0 else y + 1
                near.append((me, across))
                far.append((me, x * count_y + other if 0 <= other < count_y else along))
    return near, far


def swap_near(axis, value):
    return lax.ppermute(narrow(axis, value), ("gx", "gy"), partner_swaps(axis)[0])


def swap_far(axis, value):
    return lax.ppermute(narrow(axis, value), ("gx", "gy"), partner_swaps(axis)[1])


def narrow(axis, value):
    return value.astype(jnp.float16) if axis == "gx" else value


def swap(axis, near_value, far_value):
    far_in = swap_far(axis, far_value)
    return swap_near(axis, near_value), far_in


def tap_tables(psf_taps, kernel_index):
    gx, gy = lax.axis_index("gx"), lax.axis_index("gy")
    even_x, even_y = gx % 2 == 0, gy % 2 == 0
    anchor = jnp.zeros((), i32)
    bordered = jnp.pad(kernel_index, ((1, 1), (1, 1), (0, 0), (0, 0)), constant_values=-1)
    around = lax.dynamic_slice(
        bordered, (gx.astype(i32), gy.astype(i32), anchor, anchor), (ROLES, ROLES, V, 3)
    )
    low, middle, high = around[:1], around[1:2], around[2:]
    around = jnp.where(
        even_x, jnp.concatenate([middle, high, low]), jnp.concatenate([middle, low, high])
    )
    low, middle, high = around[:, :1], around[:, 1:2], around[:, 2:]
    around = jnp.where(
        even_y, jnp.concatenate([middle, high, low], 1), jnp.concatenate([middle, low, high], 1)
    )
    normal = psf_taps / jnp.sum(psf_taps, axis=-1, keepdims=True)
    chosen = (around.reshape(-1)[:, None] == jnp.arange(psf_taps.shape[0], dtype=i32)).astype(f32)
    kernels = jnp.dot(chosen, normal, precision=lax.Precision.HIGHEST)
    kernels = jnp.pad(kernels, ((0, 0), (0, LANES - TAPS)))
    backward = jnp.pad(kernels[:, :TAPS][:, ::-1], ((0, 0), (0, LANES - TAPS)))
    role = jnp.arange(kernels.shape[0])
    axis, yr, xr = role % 3, role // (3 * V) % ROLES, role // (3 * V * ROLES)
    step = jnp.where(axis == 0, jnp.where(xr == 1, 1, jnp.where(xr == 2, -1, 0)), 0)
    step = step * jnp.where(even_x, 1, -1)
    step_y = jnp.where(axis == 1, jnp.where(yr == 1, 1, jnp.where(yr == 2, -1, 0)), 0)
    step = (step + step_y * jnp.where(even_y, 1, -1))[:, None]

    def moved(a, sign):
        return jnp.where(
            step * sign > 0, jnp.roll(a, -STRIP, 1), jnp.where(step * sign < 0, jnp.roll(a, STRIP, 1), a)
        )

    return moved(kernels, 1), moved(backward, -1)


def shards(estimate, stored, placement, psf_taps, kernel_index):
    devices_y = lax.axis_size("gy")
    devices = lax.axis_size("gx") * devices_y
    slots = stored.shape[0]
    cap = 2 * slots // devices
    rows = devices * cap
    plane = BX * BY
    me = (lax.axis_index("gx") * devices_y + lax.axis_index("gy")).astype(i32)

    half, message = (2 * NZ, LANES), (FIELD + 4 * NZ, LANES)
    scaled = (FIELD + 4 * NZ + STRIP, LANES)
    one, every = (FIELD, LANES), (V, FIELD, LANES)
    even_y = lax.axis_index("gy") % 2 == 0
    info = jnp.stack([jnp.where(even_y, STRIP, 0), jnp.where(even_y, 0, STRIP)]).astype(i32)
    slots_of = placement.reshape(devices, slots)
    field, up, down, slots_near, stored_near = call(
        start_kernel,
        [(one, f32), (half, f32), (half, f32), (slots_of.shape, i32), (stored.shape, bf16)],
        info, scalars=1, far=(estimate, slots_of, stored),
        scratch=[pltpu.VMEM(estimate.shape, f32), pltpu.SemaphoreType.DMA((3,))],
    )
    up_in, down_in = swap("gy", up, down)
    (outgoing,) = call(
        functools.partial(route_kernel, cap), [((rows, plane), bf16)], me.reshape(1), slots_near, stored_near,
        scalars=1, scratch=[pltpu.VMEM((slots * BX, BY), f32)],
    )
    outgoing, psf_taps, kernel_index, slots_of = lax.optimization_barrier(
        (outgoing, psf_taps, kernel_index, slots_of)
    )
    arrived = lax.all_to_all(
        outgoing.reshape(devices, cap, plane), ("gx", "gy"), split_axis=0, concat_axis=0, tiled=True
    ).reshape(rows, plane)

    old = jnp.concatenate([field, up_in, down_in], axis=0)
    near, far = (a.astype(f32) for a in swap("gx", old, old))
    taps, backward = tap_tables(psf_taps, kernel_index)

    def shapes(y_shape, z_shape):
        return ROLES * [
            ((V, FIELD, FIELD), bf16),
            (y_shape, bf16),
            ((2, V, 2 * LANES, 2 * LANES), bf16),
            ((2,) + z_shape, bf16),
        ]

    forward_shapes = shapes((3 * BY, V * BY), (V * NZ, LANES))
    adjoint_shapes = shapes((V, 2 * BY, 2 * BY), (NZ, V * LANES))
    sems = [pltpu.SemaphoreType.DMA((4 * ROLES,))]
    forward = call(build_forward_kernel, forward_shapes, taps, backward, cost=3.0)
    adjoint = call(
        build_adjoint_kernel, adjoint_shapes, taps, backward,
        out_place=HBM, scratch=held(adjoint_shapes) + sems, cost=4.0,
    )
    forward_far, forward_near, forward_center = forward[:4], forward[4:8], forward[8:]

    blurred = ()
    for message_in, matrices in ((old, forward_center), (near, forward_near)):
        blurred = call(
            forward_first_kernel, [(every, f32)], info, *blurred, message_in, *matrices, scalars=1
        )
    (inverse,) = call(
        forward_inverse_kernel, [(every, f32)], info, *blurred, far, *forward_far, scalars=1,
        out_place=HBM, scratch=[pltpu.VMEM(every, f32), pltpu.SemaphoreType.DMA],
    )
    adjoint_of_far, adjoint_near, adjoint_center = adjoint[:4], adjoint[4:8], adjoint[8:]
    (table,) = call(
        functools.partial(arrival_kernel, cap), [((slots, rows), bf16)],
        me.reshape(1), jnp.repeat(slots_of, cap, axis=0), scalars=1,
        out_place=HBM, scratch=[pltpu.VMEM((slots, rows), bf16), pltpu.SemaphoreType.DMA],
    )

    edges = ((V, 2) + half, f32)
    fetched = (table, inverse, *adjoint_of_far)
    data, quotient, edge, far = call(
        quotient_first_kernel, [(every, bf16), (every, f32), edges, (scaled, f32)],
        info, arrived, scalars=1, far=fetched,
        scratch=held([(a.shape, a.dtype) for a in fetched])
        + [pltpu.VMEM((slots, plane), f32), pltpu.SemaphoreType.DMA((len(fetched) + V - 1,))],
    )

    def sides(quotient, edge, far):
        far = swap_far("gx", far)
        (near,) = call(adjoint_side_kernel, [(scaled, f32)], quotient, edge, *adjoint_near)
        near = swap_near("gx", near)
        center = [(one, f32), ((2,) + half, f32)]
        field, strips = call(adjoint_center_kernel, center, quotient, edge, *adjoint_center, cost=QUICK)
        return field, strips, near.astype(f32), far.astype(f32)

    both = (4 * NZ, LANES)
    total, up, down = call(
        gather_kernel, [(one, f32), (both, f32), (both, f32)], info, *sides(quotient, edge, far), scalars=1
    )
    up_in, down_in = swap("gy", up, down)
    taps, backward, up, down = lax.optimization_barrier((taps, backward, up, down))
    forward = call(build_forward_kernel, forward_shapes, taps, backward)
    old, *forward = lax.optimization_barrier((old, *forward))
    forward_far, forward_near, forward_center = forward[:4], forward[4:8], forward[8:]
    new, new_scaled = call(
        update_kernel, [(message, f32), (scaled, f32)],
        info, old, total, up, down, up_in, down_in, scalars=1,
    )
    far = swap_far("gx", new_scaled)
    near = swap_near("gx", new_scaled)
    (blurred,) = call(forward_center_kernel, [(every, f32)], info, new, *forward_center, scalars=1, cost=QUICK)
    (blurred,) = call(
        forward_near_kernel, [(every, f32)], info, blurred, near.astype(f32), *forward_near, scalars=1, cost=QUICK
    )
    quotient, edge, far = call(
        middle_kernel, [(every, f32), edges, (scaled, f32)],
        info, data, blurred, far.astype(f32), *forward_far, *adjoint_of_far, scalars=1, cost=QUICK,
    )
    total, up, down = call(
        gather_last_kernel, [(one, f32), (half, f32), (half, f32)], *sides(quotient, edge, far)
    )
    up_in, down_in = swap("gy", up, down)
    (refined,) = call(
        final_kernel, [(estimate.shape, f32)], info, new, total, up_in, down_in, scalars=1, out_place=HBM,
        scratch=[pltpu.VMEM(estimate.shape, f32), pltpu.SemaphoreType.DMA((2,))],
    )
    return refined


def solution(mesh):
    return jax.shard_map(
        shards,
        mesh=mesh,
        in_specs=(P(None, "gx", "gy"), P(("gx", "gy"), None, None), P(), P(), P()),
        out_specs=P(None, "gx", "gy"),
        check_vma=False,
    )
```

```python
import functools
import math

import jax
import jax.numpy as jnp
from jax import lax
from jax.experimental import pallas as pl
from jax.experimental.pallas import tpu as pltpu
from jax.sharding import PartitionSpec as P

f32 = jnp.float32
bf16 = jnp.bfloat16
i32 = jnp.int32

NZ = 32
BX = 16
BY = 128
V = 4
TAPS = 31
RADIUS = 15
FIELD = BX * NZ
STRIP = 16
LANES = 128
WORKSPACE = 8 * 2**20
PEAK = 14.0
QUICK = 0.02
ROLES = 3
CENTER, NEAR, FAR = range(ROLES)
ORDER = (FAR, NEAR, CENTER)


def iota(shape, axis):
    return lax.broadcasted_iota(i32, shape, axis)


def one_hot(mask):
    return jnp.where(mask, 1.0, 0.0).astype(bf16)


def split(a):
    hi = a.astype(bf16)
    return hi, (a - hi.astype(f32)).astype(bf16)


def dot(a, b):
    return jnp.dot(a, b, preferred_element_type=f32)


def earlier(count):
    return one_hot(iota((count, count), 0) < iota((count, count), 1))


def fetch(outside, held, sems):
    copies = [pltpu.make_async_copy(a, b, sems.at[n]) for n, (a, b) in enumerate(zip(outside, held))]
    for copy in copies:
        copy.start()
    return copies


def route_kernel(cap, me_ref, slots_ref, stored_ref, out_ref, wide_ref):
    rows, slots = out_ref.shape[0], stored_ref.shape[0]
    me = me_ref[0]
    wide_ref[...] = stored_ref[...].reshape(slots * BX, BY).astype(f32)
    target = jnp.right_shift(slots_ref[pl.ds(me, 1), :], slots.bit_length() - 1)
    place = iota((rows, slots), 0) - target * cap
    marked = jnp.logical_and(place >= 0, place < cap)
    rank = dot(one_hot(marked), earlier(slots))
    chosen = one_hot(jnp.logical_and(marked, rank == place.astype(f32)))
    for x in range(0, BX, 2):
        pair = [wide_ref[pl.ds(x + n, slots, stride=BX), :].astype(bf16) for n in range(2)]
        out_ref[:, x * BY : (x + 2) * BY] = dot(chosen, jnp.concatenate(pair, axis=1)).astype(bf16)


def arrival_kernel(cap, me_ref, slots_ref, out_ref, table_ref, sem):
    rows, slots = slots_ref.shape
    item = slots_ref[...] - me_ref[0] * slots
    wanted = jnp.logical_and(item >= 0, item < slots)
    rank = dot(one_hot(wanted), earlier(slots))
    order = jnp.bitwise_and(iota((rows, slots), 0), cap - 1)
    found = jnp.logical_and(wanted, rank == order.astype(f32))
    item_of = jnp.sum(jnp.where(found, item + 1, 0).astype(f32), axis=1, keepdims=True) - 1.0
    table = jnp.where(item_of == iota((rows, slots), 1).astype(f32), 1.0, 0.0)
    table_ref[...] = table.T.astype(bf16)
    copy = pltpu.make_async_copy(table_ref, out_ref, sem)
    copy.start()
    copy.wait()


def toeplitz(row, count):
    spread = jnp.broadcast_to(row, (count, LANES))
    return pltpu.roll(spread, LANES - RADIUS, 1, stride=1, stride_axis=0)


def expand(table, selector):
    first = table.astype(bf16)
    rest = table - first.astype(f32)
    second = rest.astype(bf16)
    third = (rest - second.astype(f32)).astype(bf16)
    return dot(first, selector) + dot(second, selector) + dot(third, selector)


def selectors(width, count):
    lane = iota((LANES, width * count), 1)
    row = iota((LANES, width * count), 0)
    each = one_hot(row == jnp.right_shift(lane, width.bit_length() - 1))
    tiled = one_hot(row == jnp.bitwise_and(lane, width - 1))
    return each, tiled


def row_of(xr, yr, view, axis):
    return ((xr * ROLES + yr) * V + view) * 3 + axis


def kron_rows(out, outer, inner, count, width):
    for i in range(count):
        out[i * width : (i + 1) * width, :] = (inner * outer[i : i + 1, :]).astype(bf16)


def stack3(table):
    hi, lo = split(table)
    return jnp.concatenate([hi, hi, lo], axis=0)


def lanes3(table, width):
    inside = iota(table.shape, 1) < width
    kept = jnp.where(inside, table, 0.0)
    hi, lo = split(kept)
    hi, lo = hi.astype(f32), lo.astype(f32)
    return (hi + pltpu.roll(lo, width, 1) + pltpu.roll(hi, 2 * width, 1)).astype(bf16)


def banded_y(row):
    table = toeplitz(row, BY)
    off = iota((BY, BY), 0) - iota((BY, BY), 1)
    return jnp.where(jnp.abs(off) <= RADIUS, table, 0.0)


def build_forward_kernel(order, taps_ref, back_ref, *held):
    each, tiled = selectors(NZ, BX)
    each16, tiled16 = selectors(STRIP, BX)
    for n, xr in enumerate(order):
        k_ref, y_ref, xy_ref, z_ref = held[4 * n : 4 * n + 4]
        for v in range(V):
            def fwd(yr, e):
                r = row_of(xr, yr, v, e)
                return taps_ref[r : r + 1, :]

            def bwd(yr, e):
                r = row_of(xr, yr, v, e)
                return back_ref[r : r + 1, :]

            outer = expand(toeplitz(fwd(0, 0), BX), each)
            inner = expand(toeplitz(fwd(0, 2), NZ), tiled)
            kron_rows(k_ref.at[v], outer, inner, BX, NZ)
            y_ref[:, v * BY : (v + 1) * BY] = stack3(banded_y(bwd(0, 1)))
            for yr in (1, 2):
                outer = expand(toeplitz(bwd(yr, 0), BX), each16)
                inner = expand(toeplitz(bwd(yr, 1), STRIP), tiled16)
                kron_rows(xy_ref.at[yr - 1, v], outer, inner, BX, STRIP)
                z_ref[yr - 1, v * NZ : (v + 1) * NZ, :] = lanes3(toeplitz(fwd(yr, 2), NZ), NZ)


def build_adjoint_kernel(taps_ref, back_ref, *refs):
    out, held, sems = refs[:12], refs[12:24], refs[24]
    copies = [pltpu.make_async_copy(a, b, sems.at[n]) for n, (a, b) in enumerate(zip(held, out))]
    each, tiled = selectors(NZ, BX)
    each16, tiled16 = selectors(STRIP, BX)
    for n, xr in enumerate(ORDER):
        k_ref, y_ref, xy_ref, z_ref = held[4 * n : 4 * n + 4]
        for v in range(V):
            def fwd(yr, e):
                r = row_of(xr, yr, v, e)
                return taps_ref[r : r + 1, :]

            def bwd(yr, e):
                r = row_of(xr, yr, v, e)
                return back_ref[r : r + 1, :]

            outer = expand(toeplitz(bwd(0, 0), BX), each)
            inner = expand(toeplitz(bwd(0, 2), NZ), tiled) * (1.0 / V)
            kron_rows(k_ref.at[v], outer, inner, BX, NZ)
            hi, lo = split(banded_y(fwd(0, 1)))
            y_ref[v, :BY, :BY] = hi
            y_ref[v, :BY, BY:] = lo
            y_ref[v, BY:, :BY] = hi
            y_ref[v, BY:, BY:] = jnp.zeros_like(hi)
            for yr in (1, 2):
                outer = expand(toeplitz(fwd(yr, 0), BX), each16)
                inner = expand(toeplitz(fwd(yr, 1), STRIP), tiled16)
                kron_rows(xy_ref.at[yr - 1, v], outer, inner, BX, STRIP)
                z_ref[yr - 1, :, v * LANES : (v + 1) * LANES] = lanes3(
                    toeplitz(bwd(yr, 2), NZ) * (1.0 / V), NZ
                )
        for copy in copies[4 * n : 4 * n + 4]:
            copy.start()
    for copy in copies:
        copy.wait()


def pack_strip(field, shift):
    lane = iota((NZ, LANES), 1)
    halves = []
    for half in range(2):
        total = jnp.zeros((NZ, LANES), f32)
        for j in range(8):
            x = half * 8 + j
            moved = pltpu.roll(field[x * NZ : (x + 1) * NZ, :], shift + STRIP * j, 1)
            inside = jnp.logical_and(lane >= STRIP * j, lane < STRIP * (j + 1))
            total = jnp.where(inside, moved, total)
        halves.append(total)
    return jnp.concatenate(halves, axis=0)


def unpack_strips(up, down, shifts, planes=slice(0, NZ)):
    first, last = planes.start, planes.stop
    lane = iota((last - first, LANES), 1)
    inside = []
    for shift in shifts:
        edge = jnp.where(shift > 0, BY - STRIP, 0)
        inside.append(jnp.logical_and(lane >= edge, lane < edge + STRIP))
    rows = []
    for x in range(BX):
        half, j = x // 8, x % 8
        moved = [
            pltpu.roll(a[half * NZ + first : half * NZ + last, :], 2 * LANES - shift - STRIP * j, 1)
            for a, shift in zip((up, down), shifts)
        ]
        rows.append(jnp.where(inside[0], moved[0], jnp.where(inside[1], moved[1], 0.0)))
    return jnp.concatenate(rows, axis=0)


def wide(halves):
    return jnp.concatenate([halves[:NZ], halves[NZ:]], axis=1)


def tall(strip):
    return jnp.concatenate([strip[:, :LANES], strip[:, LANES:]], axis=0)


def column3(a):
    hi, lo = split(a)
    return jnp.concatenate([hi, hi, lo, jnp.zeros_like(hi)], axis=0)


def two_rows(a, matrix):
    hi, lo = split(a)
    both = dot(jnp.concatenate([hi, lo], axis=0), matrix)
    return both[: a.shape[0]] + both[a.shape[0] :]


def two_lanes(matrix, a):
    hi, lo = split(a)
    both = dot(matrix, jnp.concatenate([hi, lo], axis=1))
    return both[:, :LANES] + both[:, LANES:]


def three_lanes(a, stacked):
    hi, lo = split(a)
    return dot(jnp.concatenate([hi, lo, hi], axis=1), stacked)


def forward_parts(message, matrices, shifts, add):
    k, y, xy, z = matrices
    field, strips = message_parts(message)
    spread = three_lanes(field, y[...])
    alongs = [dot(z[yr], column3(wide(strips[yr]))) for yr in range(2)]
    for v in range(V):
        center = two_lanes(k[v], spread[:, v * BY : (v + 1) * BY])
        rows = slice(v * NZ, (v + 1) * NZ)
        up, down = [tall(two_rows(alongs[yr][rows], xy[yr, v])) for yr in range(2)]
        add(v, center + unpack_strips(up, down, shifts))


def adjoint_parts(quotient_ref, edge_ref, refs):
    k_ref, y_ref, xy_ref, z_ref = refs
    columns = []
    for v in range(V):
        hi, lo = split(quotient_ref[v])
        both = dot(jnp.concatenate([hi, lo], axis=1), y_ref[v])
        columns.append(jnp.concatenate(split(both[:, :BY] + both[:, BY:]), axis=1))
    both = dot(
        jnp.concatenate([k_ref[v] for v in range(V)], axis=1), jnp.concatenate(columns, axis=0)
    )
    strips = []
    for yr in range(2):
        parts = [column3(two_rows(wide(edge_ref[v, yr]), xy_ref[yr, v])) for v in range(V)]
        strips.append(tall(dot(z_ref[yr], jnp.concatenate(parts, axis=0))))
    return both[:, :BY] + both[:, BY:], strips


def write_message(ref, field, strips):
    ref[:FIELD] = field
    for n in range(2):
        ref[FIELD + n * 2 * NZ : FIELD + (n + 1) * 2 * NZ] = strips[n]


def write_scaled(ref, field, strips):
    peak = jnp.max(jnp.abs(field), axis=0, keepdims=True)
    for strip in strips:
        peak = jnp.maximum(peak, jnp.max(jnp.abs(strip), axis=0, keepdims=True))
    peak = jnp.maximum(jnp.max(peak, axis=1, keepdims=True), 1e-30)
    power = PEAK - jnp.ceil(jnp.log2(peak))
    scale = jnp.exp2(power)
    write_message(ref, field * scale, [strip * scale for strip in strips])
    ref[FIELD + 4 * NZ :] = jnp.broadcast_to(power, (STRIP, LANES))


def read_scaled(ref):
    scale = jnp.exp2(-ref[FIELD + 4 * NZ : FIELD + 4 * NZ + 1, :1])
    return ref[: FIELD + 4 * NZ] * scale


def message_parts(message):
    return message[:FIELD], [message[FIELD : FIELD + 2 * NZ], message[FIELD + 2 * NZ :]]


def start_kernel(info_ref, *refs):
    outside, (field_ref, first_ref, second_ref), held, estimate_ref, sems = (
        refs[:3], refs[3:6], refs[6:8], refs[8], refs[9],
    )
    copies = fetch(outside, (estimate_ref, *held), sems)
    copies[0].wait()

    @pl.when(info_ref[0] >= 0)
    def _():
        for x in range(BX):
            field_ref[x * NZ : (x + 1) * NZ, :] = estimate_ref[:, x, :]
        field = field_ref[...]
        first_ref[...] = pack_strip(field, info_ref[0])
        second_ref[...] = pack_strip(field, info_ref[1])

    for copy in copies[1:]:
        copy.wait()


def forward_first_kernel(info_ref, *refs):
    before = len(refs) - 6
    message_ref, matrices, out_ref = refs[before], refs[before + 1 : before + 5], refs[-1]
    shifts = (info_ref[0], info_ref[1])

    def add(v, part):
        out_ref[v] = part + refs[0][v] if before else part

    forward_parts(message_ref[...], matrices, shifts, add)


def forward_inverse_kernel(info_ref, blurred_ref, message_ref, k_ref, y_ref, xy_ref, z_ref, result_ref, out_ref, sem):
    shifts = (info_ref[0], info_ref[1])

    def add(v, part):
        out_ref[v] = 1.0 / (blurred_ref[v] + part)

    forward_parts(message_ref[...], (k_ref, y_ref, xy_ref, z_ref), shifts, add)
    copy = pltpu.make_async_copy(out_ref, result_ref, sem)
    copy.start()
    copy.wait()


def pack_edges(quotient_ref, edge_ref, shifts):
    for v in range(V):
        for yr in range(2):
            edge_ref[v, yr] = pack_strip(quotient_ref[v], shifts[yr])


def quotient_first_kernel(info_ref, arrived_ref, *refs):
    outside, (data_ref, quotient_ref, edge_ref, far_ref), held, planes_ref, sems = (
        refs[:6], refs[6:10], refs[10:16], refs[16], refs[17],
    )
    parts = [(outside[0], held[0])] + [(outside[1].at[v], held[1].at[v]) for v in range(V)]
    parts += list(zip(outside[2:], held[2:]))
    copies = fetch(*zip(*parts), sems)
    table_ref, inverse_ref, *matrices = held
    shifts = (info_ref[0], info_ref[1])
    copies[0].wait()

    @pl.when(shifts[0] >= 0)
    def _():
        planes_ref[...] = dot(table_ref[...], arrived_ref[...])

    for v in range(V):
        copies[1 + v].wait()

        @pl.when(shifts[0] >= 0)
        def _():
            for x in range(BX):
                rows = slice(x * NZ, (x + 1) * NZ)
                piece = planes_ref[v * NZ : (v + 1) * NZ, x * BY : (x + 1) * BY]
                data_ref[v, rows, :] = piece.astype(bf16)
                quotient_ref[v, rows, :] = piece * inverse_ref[v, rows, :]
            for yr in range(2):
                edge_ref[v, yr] = pack_strip(quotient_ref[v], shifts[yr])

    for copy in copies[1 + V :]:
        copy.wait()
    write_scaled(far_ref, *adjoint_parts(quotient_ref, edge_ref, matrices))


def adjoint_side_kernel(quotient_ref, edge_ref, k_ref, y_ref, xy_ref, z_ref, message_ref):
    write_scaled(message_ref, *adjoint_parts(quotient_ref, edge_ref, (k_ref, y_ref, xy_ref, z_ref)))


def adjoint_center_kernel(quotient_ref, edge_ref, k_ref, y_ref, xy_ref, z_ref, field_ref, strips_ref):
    field, strips = adjoint_parts(quotient_ref, edge_ref, (k_ref, y_ref, xy_ref, z_ref))
    field_ref[...] = field
    strips_ref[0] = strips[0]
    strips_ref[1] = strips[1]


def gather_kernel(info_ref, field_ref, strips_ref, near_ref, far_ref, total_ref, up_ref, down_ref):
    near, far = read_scaled(near_ref), read_scaled(far_ref)
    total = field_ref[...] + near[:FIELD] + far[:FIELD]
    total_ref[...] = total
    for n, ref in enumerate((up_ref, down_ref)):
        rows = slice(FIELD + n * 2 * NZ, FIELD + (n + 1) * 2 * NZ)
        ref[: 2 * NZ] = strips_ref[n] + near[rows] + far[rows]
        ref[2 * NZ :] = pack_strip(total, info_ref[n])


def gather_last_kernel(field_ref, strips_ref, near_ref, far_ref, total_ref, up_ref, down_ref):
    near, far = read_scaled(near_ref), read_scaled(far_ref)
    total_ref[...] = field_ref[...] + near[:FIELD] + far[:FIELD]
    for n, ref in enumerate((up_ref, down_ref)):
        rows = slice(FIELD + n * 2 * NZ, FIELD + (n + 1) * 2 * NZ)
        ref[...] = strips_ref[n] + near[rows] + far[rows]


def update_kernel(
    info_ref, old_ref, total_ref, up_ref, down_ref, up_in_ref, down_in_ref, new_ref, scaled_ref
):
    half = 2 * NZ
    shifts = (info_ref[0], info_ref[1])
    field = old_ref[:FIELD] * (total_ref[...] + unpack_strips(up_in_ref[:half], down_in_ref[:half], shifts))
    strips = []
    for n, (ref, own) in enumerate(((up_in_ref, up_ref), (down_in_ref, down_ref))):
        rows = slice(FIELD + n * half, FIELD + (n + 1) * half)
        strips.append(old_ref[rows] * (ref[half:] + own[:half]))
    write_message(new_ref, field, strips)
    write_scaled(scaled_ref, field, strips)


def forward_center_kernel(info_ref, own_ref, k_ref, y_ref, xy_ref, z_ref, out_ref):
    shifts = (info_ref[0], info_ref[1])

    def add(v, part):
        out_ref[v] = part

    forward_parts(own_ref[...], (k_ref, y_ref, xy_ref, z_ref), shifts, add)


def forward_near_kernel(info_ref, blurred_ref, near_ref, k_ref, y_ref, xy_ref, z_ref, out_ref):
    shifts = (info_ref[0], info_ref[1])

    def add(v, part):
        out_ref[v] = blurred_ref[v] + part

    forward_parts(read_scaled(near_ref), (k_ref, y_ref, xy_ref, z_ref), shifts, add)


def middle_kernel(
    info_ref, data_ref, blurred_ref, from_far_ref, k_ref, y_ref, xy_ref, z_ref,
    ka_ref, ya_ref, xya_ref, za_ref, quotient_ref, edge_ref, far_ref,
):
    shifts = (info_ref[0], info_ref[1])

    def add(v, part):
        quotient_ref[v] = data_ref[v].astype(f32) / (blurred_ref[v] + part)

    forward_parts(read_scaled(from_far_ref), (k_ref, y_ref, xy_ref, z_ref), shifts, add)
    pack_edges(quotient_ref, edge_ref, shifts)
    write_scaled(far_ref, *adjoint_parts(quotient_ref, edge_ref, (ka_ref, ya_ref, xya_ref, za_ref)))


def final_kernel(info_ref, old_ref, total_ref, up_in_ref, down_in_ref, out_ref, held_ref, sems):
    shifts = (info_ref[0], info_ref[1])
    half = NZ // 2
    copies = []
    for n in range(2):

        @pl.when(shifts[0] >= 0)
        def _():
            edges = unpack_strips(up_in_ref[...], down_in_ref[...], shifts, slice(n * half, (n + 1) * half))
            for x in range(BX):
                rows = slice(x * NZ + n * half, x * NZ + (n + 1) * half)
                correction = total_ref[rows] + edges[x * half : (x + 1) * half]
                held_ref[n * half : (n + 1) * half, x, :] = old_ref[rows] * correction

        part = slice(n * half, (n + 1) * half)
        copies.append(pltpu.make_async_copy(held_ref.at[part], out_ref.at[part], sems.at[n]))
        copies[-1].start()
    for copy in copies:
        copy.wait()


SMEM, VMEM, HBM = pltpu.SMEM, pltpu.VMEM, pltpu.HBM


def call(kernel, outs, *args, scalars=0, far=(), out_place=VMEM, scratch=(), cost=QUICK):
    arrays = [(a.size, a.dtype) for a in (*args[scalars:], *far)]
    arrays += [(math.prod(s), d) for s, d in outs]
    need = sum(count * jnp.dtype(d).itemsize for count, d in arrays)
    places = out_place if isinstance(out_place, list) else [out_place] * len(outs)
    specs = [pl.BlockSpec(memory_space=SMEM)] * scalars
    specs += [pl.BlockSpec(memory_space=VMEM)] * (len(args) - scalars)
    specs += [pl.BlockSpec(memory_space=HBM)] * len(far)
    args += tuple(pltpu.with_memory_space_constraint(a, HBM) for a in far)
    return pl.pallas_call(
        kernel,
        out_shape=[
            HBM(s, d) if where is HBM else jax.ShapeDtypeStruct(s, d) for (s, d), where in zip(outs, places)
        ],
        in_specs=specs,
        out_specs=[pl.BlockSpec(memory_space=where) for where in places],
        scratch_shapes=list(scratch),
        compiler_params=pltpu.CompilerParams(vmem_limit_bytes=need + WORKSPACE),
        cost_estimate=pl.CostEstimate(flops=0, bytes_accessed=int(cost * 3.5e6), transcendentals=0),
    )(*args)


def held(shapes):
    return [pltpu.VMEM(s, d) for s, d in shapes]


def partner_swaps(axis):
    count_x, count_y = lax.axis_size("gx"), lax.axis_size("gy")
    near, far = [], []
    for x in range(count_x):
        for y in range(count_y):
            me = x * count_y + y
            across, along = x * count_y + (y ^ 1), (x ^ 1) * count_y + y
            if axis == "gx":
                other = x - 1 if x % 2 == 0 else x + 1
                near.append((me, along))
                far.append((me, other * count_y + y if 0 <= other < count_x else across))
            else:
                other = y - 1 if y % 2 == 0 else y + 1
                near.append((me, across))
                far.append((me, x * count_y + other if 0 <= other < count_y else along))
    return near, far


def swap_near(axis, value):
    return lax.ppermute(narrow(axis, value), ("gx", "gy"), partner_swaps(axis)[0])


def swap_far(axis, value):
    return lax.ppermute(narrow(axis, value), ("gx", "gy"), partner_swaps(axis)[1])


def narrow(axis, value):
    return value.astype(jnp.float16) if axis == "gx" else value


def swap(axis, near_value, far_value):
    far_in = swap_far(axis, far_value)
    return swap_near(axis, near_value), far_in


def tap_tables(psf_taps, kernel_index):
    gx, gy = lax.axis_index("gx"), lax.axis_index("gy")
    even_x, even_y = gx % 2 == 0, gy % 2 == 0
    anchor = jnp.zeros((), i32)
    bordered = jnp.pad(kernel_index, ((1, 1), (1, 1), (0, 0), (0, 0)), constant_values=-1)
    around = lax.dynamic_slice(
        bordered, (gx.astype(i32), gy.astype(i32), anchor, anchor), (ROLES, ROLES, V, 3)
    )
    low, middle, high = around[:1], around[1:2], around[2:]
    around = jnp.where(
        even_x, jnp.concatenate([middle, high, low]), jnp.concatenate([middle, low, high])
    )
    low, middle, high = around[:, :1], around[:, 1:2], around[:, 2:]
    around = jnp.where(
        even_y, jnp.concatenate([middle, high, low], 1), jnp.concatenate([middle, low, high], 1)
    )
    normal = psf_taps / jnp.sum(psf_taps, axis=-1, keepdims=True)
    chosen = (around.reshape(-1)[:, None] == jnp.arange(psf_taps.shape[0], dtype=i32)).astype(f32)
    kernels = jnp.dot(chosen, normal, precision=lax.Precision.HIGHEST)
    kernels = jnp.pad(kernels, ((0, 0), (0, LANES - TAPS)))
    backward = jnp.pad(kernels[:, :TAPS][:, ::-1], ((0, 0), (0, LANES - TAPS)))
    role = jnp.arange(kernels.shape[0])
    axis, yr, xr = role % 3, role // (3 * V) % ROLES, role // (3 * V * ROLES)
    step = jnp.where(axis == 0, jnp.where(xr == 1, 1, jnp.where(xr == 2, -1, 0)), 0)
    step = step * jnp.where(even_x, 1, -1)
    step_y = jnp.where(axis == 1, jnp.where(yr == 1, 1, jnp.where(yr == 2, -1, 0)), 0)
    step = (step + step_y * jnp.where(even_y, 1, -1))[:, None]

    def moved(a, sign):
        return jnp.where(
            step * sign > 0, jnp.roll(a, -STRIP, 1), jnp.where(step * sign < 0, jnp.roll(a, STRIP, 1), a)
        )

    return moved(kernels, 1), moved(backward, -1)


def shards(estimate, stored, placement, psf_taps, kernel_index):
    devices_y = lax.axis_size("gy")
    devices = lax.axis_size("gx") * devices_y
    slots = stored.shape[0]
    cap = 2 * slots // devices
    rows = devices * cap
    plane = BX * BY
    me = (lax.axis_index("gx") * devices_y + lax.axis_index("gy")).astype(i32)

    half, message = (2 * NZ, LANES), (FIELD + 4 * NZ, LANES)
    scaled = (FIELD + 4 * NZ + STRIP, LANES)
    one, every = (FIELD, LANES), (V, FIELD, LANES)
    even_y = lax.axis_index("gy") % 2 == 0
    info = jnp.stack([jnp.where(even_y, STRIP, 0), jnp.where(even_y, 0, STRIP)]).astype(i32)
    slots_of = placement.reshape(devices, slots)
    field, up, down, slots_near, stored_near = call(
        start_kernel,
        [(one, f32), (half, f32), (half, f32), (slots_of.shape, i32), (stored.shape, bf16)],
        info, scalars=1, far=(estimate, slots_of, stored),
        scratch=[pltpu.VMEM(estimate.shape, f32), pltpu.SemaphoreType.DMA((3,))],
    )
    up_in, down_in = swap("gy", up, down)
    (outgoing,) = call(
        functools.partial(route_kernel, cap), [((rows, plane), bf16)], me.reshape(1), slots_near, stored_near,
        scalars=1, scratch=[pltpu.VMEM((slots * BX, BY), f32)],
    )
    outgoing, psf_taps, kernel_index, slots_of = lax.optimization_barrier(
        (outgoing, psf_taps, kernel_index, slots_of)
    )
    arrived = lax.all_to_all(
        outgoing.reshape(devices, cap, plane), ("gx", "gy"), split_axis=0, concat_axis=0, tiled=True
    ).reshape(rows, plane)

    old = jnp.concatenate([field, up_in, down_in], axis=0)
    near, far = (a.astype(f32) for a in swap("gx", old, old))
    taps, backward = tap_tables(psf_taps, kernel_index)

    def shapes(y_shape, z_shape):
        return ROLES * [
            ((V, FIELD, FIELD), bf16),
            (y_shape, bf16),
            ((2, V, 2 * LANES, 2 * LANES), bf16),
            ((2,) + z_shape, bf16),
        ]

    forward_shapes = shapes((3 * BY, V * BY), (V * NZ, LANES))
    adjoint_shapes = shapes((V, 2 * BY, 2 * BY), (NZ, V * LANES))
    sems = [pltpu.SemaphoreType.DMA((4 * ROLES,))]
    forward = call(functools.partial(build_forward_kernel, ORDER), forward_shapes, taps, backward, cost=3.0)
    adjoint = call(
        build_adjoint_kernel, adjoint_shapes, taps, backward,
        out_place=HBM, scratch=held(adjoint_shapes) + sems, cost=4.0,
    )
    forward_far, forward_near, forward_center = forward[:4], forward[4:8], forward[8:]

    blurred = ()
    for message_in, matrices in ((old, forward_center), (near, forward_near)):
        blurred = call(
            forward_first_kernel, [(every, f32)], info, *blurred, message_in, *matrices, scalars=1
        )
    (inverse,) = call(
        forward_inverse_kernel, [(every, f32)], info, *blurred, far, *forward_far, scalars=1,
        out_place=HBM, scratch=[pltpu.VMEM(every, f32), pltpu.SemaphoreType.DMA],
    )
    adjoint_of_far, adjoint_near, adjoint_center = adjoint[:4], adjoint[4:8], adjoint[8:]
    (table,) = call(
        functools.partial(arrival_kernel, cap), [((slots, rows), bf16)],
        me.reshape(1), jnp.repeat(slots_of, cap, axis=0), scalars=1,
        out_place=HBM, scratch=[pltpu.VMEM((slots, rows), bf16), pltpu.SemaphoreType.DMA],
    )

    edges = ((V, 2) + half, f32)
    fetched = (table, inverse, *adjoint_of_far)
    data, quotient, edge, far = call(
        quotient_first_kernel, [(every, bf16), (every, f32), edges, (scaled, f32)],
        info, arrived, scalars=1, far=fetched,
        scratch=held([(a.shape, a.dtype) for a in fetched])
        + [pltpu.VMEM((slots, plane), f32), pltpu.SemaphoreType.DMA((len(fetched) + V - 1,))],
    )

    def sides(quotient, edge, far):
        far = swap_far("gx", far)
        (near,) = call(adjoint_side_kernel, [(scaled, f32)], quotient, edge, *adjoint_near)
        near = swap_near("gx", near)
        center = [(one, f32), ((2,) + half, f32)]
        field, strips = call(adjoint_center_kernel, center, quotient, edge, *adjoint_center, cost=QUICK)
        return field, strips, near.astype(f32), far.astype(f32)

    both = (4 * NZ, LANES)
    total, up, down = call(
        gather_kernel, [(one, f32), (both, f32), (both, f32)], info, *sides(quotient, edge, far), scalars=1
    )
    up_in, down_in = swap("gy", up, down)
    taps, backward, up, down = lax.optimization_barrier((taps, backward, up, down))
    forward = call(
        functools.partial(build_forward_kernel, ORDER[1:]), forward_shapes[4:], taps, backward
    )
    old, *forward = lax.optimization_barrier((old, *forward))
    forward_near, forward_center = forward[:4], forward[4:]
    new, new_scaled = call(
        update_kernel, [(message, f32), (scaled, f32)],
        info, old, total, up, down, up_in, down_in, scalars=1,
    )
    far = swap_far("gx", new_scaled)
    near = swap_near("gx", new_scaled)
    (blurred,) = call(forward_center_kernel, [(every, f32)], info, new, *forward_center, scalars=1, cost=QUICK)
    (blurred,) = call(
        forward_near_kernel, [(every, f32)], info, blurred, near.astype(f32), *forward_near, scalars=1, cost=QUICK
    )
    taps, backward, blurred = lax.optimization_barrier((taps, backward, blurred))
    forward_far = call(
        functools.partial(build_forward_kernel, ORDER[:1]), forward_shapes[:4], taps, backward
    )
    quotient, edge, far = call(
        middle_kernel, [(every, f32), edges, (scaled, f32)],
        info, data, blurred, far.astype(f32), *forward_far, *adjoint_of_far, scalars=1, cost=QUICK,
    )
    total, up, down = call(
        gather_last_kernel, [(one, f32), (half, f32), (half, f32)], *sides(quotient, edge, far)
    )
    up_in, down_in = swap("gy", up, down)
    (refined,) = call(
        final_kernel, [(estimate.shape, f32)], info, new, total, up_in, down_in, scalars=1, out_place=HBM,
        scratch=[pltpu.VMEM(estimate.shape, f32), pltpu.SemaphoreType.DMA((2,))],
    )
    return refined


def solution(mesh):
    return jax.shard_map(
        shards,
        mesh=mesh,
        in_specs=(P(None, "gx", "gy"), P(("gx", "gy"), None, None), P(), P(), P()),
        out_specs=P(None, "gx", "gy"),
        check_vma=False,
    )
```

```python
import functools
import math

import jax
import jax.numpy as jnp
from jax import lax
from jax.experimental import pallas as pl
from jax.experimental.pallas import tpu as pltpu
from jax.sharding import PartitionSpec as P

f32 = jnp.float32
bf16 = jnp.bfloat16
i32 = jnp.int32

NZ = 32
BX = 16
BY = 128
V = 4
TAPS = 31
RADIUS = 15
FIELD = BX * NZ
STRIP = 16
LANES = 128
WORKSPACE = 8 * 2**20
PEAK = 14.0
QUICK = 0.02
ROLES = 3
CENTER, NEAR, FAR = range(ROLES)
ORDER = (FAR, NEAR, CENTER)


def iota(shape, axis):
    return lax.broadcasted_iota(i32, shape, axis)


def one_hot(mask):
    return jnp.where(mask, 1.0, 0.0).astype(bf16)


def split(a):
    hi = a.astype(bf16)
    return hi, (a - hi.astype(f32)).astype(bf16)


def dot(a, b):
    return jnp.dot(a, b, preferred_element_type=f32)


def earlier(count):
    return one_hot(iota((count, count), 0) < iota((count, count), 1))


def fetch(outside, held, sems):
    copies = [pltpu.make_async_copy(a, b, sems.at[n]) for n, (a, b) in enumerate(zip(outside, held))]
    for copy in copies:
        copy.start()
    return copies


def route_kernel(cap, me_ref, slots_ref, stored_ref, out_ref, wide_ref):
    rows, slots = out_ref.shape[0], stored_ref.shape[0]
    me = me_ref[0]
    wide_ref[...] = stored_ref[...].reshape(slots * BX, BY).astype(f32)
    target = jnp.right_shift(slots_ref[pl.ds(me, 1), :], slots.bit_length() - 1)
    place = iota((rows, slots), 0) - target * cap
    marked = jnp.logical_and(place >= 0, place < cap)
    rank = dot(one_hot(marked), earlier(slots))
    chosen = one_hot(jnp.logical_and(marked, rank == place.astype(f32)))
    for x in range(0, BX, 2):
        pair = [wide_ref[pl.ds(x + n, slots, stride=BX), :].astype(bf16) for n in range(2)]
        out_ref[:, x * BY : (x + 2) * BY] = dot(chosen, jnp.concatenate(pair, axis=1)).astype(bf16)


def arrival_kernel(cap, me_ref, slots_ref, out_ref, table_ref, sem):
    rows, slots = slots_ref.shape
    item = slots_ref[...] - me_ref[0] * slots
    wanted = jnp.logical_and(item >= 0, item < slots)
    rank = dot(one_hot(wanted), earlier(slots))
    order = jnp.bitwise_and(iota((rows, slots), 0), cap - 1)
    found = jnp.logical_and(wanted, rank == order.astype(f32))
    item_of = jnp.sum(jnp.where(found, item + 1, 0).astype(f32), axis=1, keepdims=True) - 1.0
    table = jnp.where(item_of == iota((rows, slots), 1).astype(f32), 1.0, 0.0)
    table_ref[...] = table.T.astype(bf16)
    copy = pltpu.make_async_copy(table_ref, out_ref, sem)
    copy.start()
    copy.wait()


def toeplitz(row, count):
    spread = jnp.broadcast_to(row, (count, LANES))
    return pltpu.roll(spread, LANES - RADIUS, 1, stride=1, stride_axis=0)


def expand(table, selector):
    first = table.astype(bf16)
    rest = table - first.astype(f32)
    second = rest.astype(bf16)
    third = (rest - second.astype(f32)).astype(bf16)
    return dot(first, selector) + dot(second, selector) + dot(third, selector)


def selectors(width, count):
    lane = iota((LANES, width * count), 1)
    row = iota((LANES, width * count), 0)
    each = one_hot(row == jnp.right_shift(lane, width.bit_length() - 1))
    tiled = one_hot(row == jnp.bitwise_and(lane, width - 1))
    return each, tiled


def row_of(xr, yr, view, axis):
    return ((xr * ROLES + yr) * V + view) * 3 + axis


def kron_rows(out, outer, inner, count, width):
    for i in range(count):
        out[i * width : (i + 1) * width, :] = (inner * outer[i : i + 1, :]).astype(bf16)


def stack3(table):
    hi, lo = split(table)
    return jnp.concatenate([hi, hi, lo], axis=0)


def lanes3(table, width):
    inside = iota(table.shape, 1) < width
    kept = jnp.where(inside, table, 0.0)
    hi, lo = split(kept)
    hi, lo = hi.astype(f32), lo.astype(f32)
    return (hi + pltpu.roll(lo, width, 1) + pltpu.roll(hi, 2 * width, 1)).astype(bf16)


def banded_y(row):
    table = toeplitz(row, BY)
    off = iota((BY, BY), 0) - iota((BY, BY), 1)
    return jnp.where(jnp.abs(off) <= RADIUS, table, 0.0)


def build_forward_kernel(taps_ref, back_ref, *held):
    each, tiled = selectors(NZ, BX)
    each16, tiled16 = selectors(STRIP, BX)
    for n, xr in enumerate(ORDER):
        k_ref, y_ref, xy_ref, z_ref = held[4 * n : 4 * n + 4]
        for v in range(V):
            def fwd(yr, e):
                r = row_of(xr, yr, v, e)
                return taps_ref[r : r + 1, :]

            def bwd(yr, e):
                r = row_of(xr, yr, v, e)
                return back_ref[r : r + 1, :]

            outer = expand(toeplitz(fwd(0, 0), BX), each)
            inner = expand(toeplitz(fwd(0, 2), NZ), tiled)
            kron_rows(k_ref.at[v], outer, inner, BX, NZ)
            y_ref[:, v * BY : (v + 1) * BY] = stack3(banded_y(bwd(0, 1)))
            for yr in (1, 2):
                outer = expand(toeplitz(bwd(yr, 0), BX), each16)
                inner = expand(toeplitz(bwd(yr, 1), STRIP), tiled16)
                kron_rows(xy_ref.at[yr - 1, v], outer, inner, BX, STRIP)
                z_ref[yr - 1, v * NZ : (v + 1) * NZ, :] = lanes3(toeplitz(fwd(yr, 2), NZ), NZ)


def build_adjoint_kernel(taps_ref, back_ref, *refs):
    out, held, sems = refs[:12], refs[12:24], refs[24]
    copies = [pltpu.make_async_copy(a, b, sems.at[n]) for n, (a, b) in enumerate(zip(held, out))]
    each, tiled = selectors(NZ, BX)
    each16, tiled16 = selectors(STRIP, BX)
    for n, xr in enumerate(ORDER):
        k_ref, y_ref, xy_ref, z_ref = held[4 * n : 4 * n + 4]
        for v in range(V):
            def fwd(yr, e):
                r = row_of(xr, yr, v, e)
                return taps_ref[r : r + 1, :]

            def bwd(yr, e):
                r = row_of(xr, yr, v, e)
                return back_ref[r : r + 1, :]

            outer = expand(toeplitz(bwd(0, 0), BX), each)
            inner = expand(toeplitz(bwd(0, 2), NZ), tiled) * (1.0 / V)
            kron_rows(k_ref.at[v], outer, inner, BX, NZ)
            hi, lo = split(banded_y(fwd(0, 1)))
            y_ref[v, :BY, :BY] = hi
            y_ref[v, :BY, BY:] = lo
            y_ref[v, BY:, :BY] = hi
            y_ref[v, BY:, BY:] = jnp.zeros_like(hi)
            for yr in (1, 2):
                outer = expand(toeplitz(fwd(yr, 0), BX), each16)
                inner = expand(toeplitz(fwd(yr, 1), STRIP), tiled16)
                kron_rows(xy_ref.at[yr - 1, v], outer, inner, BX, STRIP)
                z_ref[yr - 1, :, v * LANES : (v + 1) * LANES] = lanes3(
                    toeplitz(bwd(yr, 2), NZ) * (1.0 / V), NZ
                )
        for copy in copies[4 * n : 4 * n + 4]:
            copy.start()
    for copy in copies:
        copy.wait()


def pack_strip(field, shift):
    lane = iota((NZ, LANES), 1)
    halves = []
    for half in range(2):
        total = jnp.zeros((NZ, LANES), f32)
        for j in range(8):
            x = half * 8 + j
            moved = pltpu.roll(field[x * NZ : (x + 1) * NZ, :], shift + STRIP * j, 1)
            inside = jnp.logical_and(lane >= STRIP * j, lane < STRIP * (j + 1))
            total = jnp.where(inside, moved, total)
        halves.append(total)
    return jnp.concatenate(halves, axis=0)


def unpack_strips(up, down, shifts, planes=slice(0, NZ)):
    first, last = planes.start, planes.stop
    lane = iota((last - first, LANES), 1)
    inside = []
    for shift in shifts:
        edge = jnp.where(shift > 0, BY - STRIP, 0)
        inside.append(jnp.logical_and(lane >= edge, lane < edge + STRIP))
    rows = []
    for x in range(BX):
        half, j = x // 8, x % 8
        moved = [
            pltpu.roll(a[half * NZ + first : half * NZ + last, :], 2 * LANES - shift - STRIP * j, 1)
            for a, shift in zip((up, down), shifts)
        ]
        rows.append(jnp.where(inside[0], moved[0], jnp.where(inside[1], moved[1], 0.0)))
    return jnp.concatenate(rows, axis=0)


def wide(halves):
    return jnp.concatenate([halves[:NZ], halves[NZ:]], axis=1)


def tall(strip):
    return jnp.concatenate([strip[:, :LANES], strip[:, LANES:]], axis=0)


def column3(a):
    hi, lo = split(a)
    return jnp.concatenate([hi, hi, lo, jnp.zeros_like(hi)], axis=0)


def two_rows(a, matrix):
    hi, lo = split(a)
    both = dot(jnp.concatenate([hi, lo], axis=0), matrix)
    return both[: a.shape[0]] + both[a.shape[0] :]


def two_lanes(matrix, a):
    hi, lo = split(a)
    both = dot(matrix, jnp.concatenate([hi, lo], axis=1))
    return both[:, :LANES] + both[:, LANES:]


def three_lanes(a, stacked):
    hi, lo = split(a)
    return dot(jnp.concatenate([hi, lo, hi], axis=1), stacked)


def forward_parts(message, matrices, shifts, add):
    k, y, xy, z = matrices
    field, strips = message_parts(message)
    spread = three_lanes(field, y[...])
    alongs = [dot(z[yr], column3(wide(strips[yr]))) for yr in range(2)]
    for v in range(V):
        center = two_lanes(k[v], spread[:, v * BY : (v + 1) * BY])
        rows = slice(v * NZ, (v + 1) * NZ)
        up, down = [tall(two_rows(alongs[yr][rows], xy[yr, v])) for yr in range(2)]
        add(v, center + unpack_strips(up, down, shifts))


def adjoint_parts(quotient_ref, edge_ref, refs):
    k_ref, y_ref, xy_ref, z_ref = refs
    columns = []
    for v in range(V):
        hi, lo = split(quotient_ref[v])
        both = dot(jnp.concatenate([hi, lo], axis=1), y_ref[v])
        columns.append(jnp.concatenate(split(both[:, :BY] + both[:, BY:]), axis=1))
    both = dot(
        jnp.concatenate([k_ref[v] for v in range(V)], axis=1), jnp.concatenate(columns, axis=0)
    )
    strips = []
    for yr in range(2):
        parts = [column3(two_rows(wide(edge_ref[v, yr]), xy_ref[yr, v])) for v in range(V)]
        strips.append(tall(dot(z_ref[yr], jnp.concatenate(parts, axis=0))))
    return both[:, :BY] + both[:, BY:], strips


def write_message(ref, field, strips):
    ref[:FIELD] = field
    for n in range(2):
        ref[FIELD + n * 2 * NZ : FIELD + (n + 1) * 2 * NZ] = strips[n]


def write_scaled(ref, field, strips):
    peak = jnp.max(jnp.abs(field), axis=0, keepdims=True)
    for strip in strips:
        peak = jnp.maximum(peak, jnp.max(jnp.abs(strip), axis=0, keepdims=True))
    peak = jnp.maximum(jnp.max(peak, axis=1, keepdims=True), 1e-30)
    power = PEAK - jnp.ceil(jnp.log2(peak))
    scale = jnp.exp2(power)
    write_message(ref, field * scale, [strip * scale for strip in strips])
    ref[FIELD + 4 * NZ :] = jnp.broadcast_to(power, (STRIP, LANES))


def read_scaled(ref):
    scale = jnp.exp2(-ref[FIELD + 4 * NZ : FIELD + 4 * NZ + 1, :1])
    return ref[: FIELD + 4 * NZ] * scale


def message_parts(message):
    return message[:FIELD], [message[FIELD : FIELD + 2 * NZ], message[FIELD + 2 * NZ :]]


def start_kernel(info_ref, *refs):
    outside, (field_ref, first_ref, second_ref), held, estimate_ref, sems = (
        refs[:3], refs[3:6], refs[6:8], refs[8], refs[9],
    )
    copies = fetch(outside, (estimate_ref, *held), sems)
    copies[0].wait()

    @pl.when(info_ref[0] >= 0)
    def _():
        for x in range(BX):
            field_ref[x * NZ : (x + 1) * NZ, :] = estimate_ref[:, x, :]
        field = field_ref[...]
        first_ref[...] = pack_strip(field, info_ref[0])
        second_ref[...] = pack_strip(field, info_ref[1])

    for copy in copies[1:]:
        copy.wait()


def forward_first_kernel(info_ref, *refs):
    before = len(refs) - 6
    message_ref, matrices, out_ref = refs[before], refs[before + 1 : before + 5], refs[-1]
    shifts = (info_ref[0], info_ref[1])

    def add(v, part):
        out_ref[v] = part + refs[0][v] if before else part

    forward_parts(message_ref[...], matrices, shifts, add)


def forward_inverse_kernel(info_ref, blurred_ref, message_ref, k_ref, y_ref, xy_ref, z_ref, result_ref, out_ref, sem):
    shifts = (info_ref[0], info_ref[1])

    def add(v, part):
        out_ref[v] = 1.0 / (blurred_ref[v] + part)

    forward_parts(message_ref[...], (k_ref, y_ref, xy_ref, z_ref), shifts, add)
    copy = pltpu.make_async_copy(out_ref, result_ref, sem)
    copy.start()
    copy.wait()


def quotient_first_kernel(info_ref, arrived_ref, *refs):
    outside, (data_ref, quotient_ref, edge_ref, far_ref), held, planes_ref, sems = (
        refs[:6], refs[6:10], refs[10:16], refs[16], refs[17],
    )
    parts = [(outside[0], held[0])] + [(outside[1].at[v], held[1].at[v]) for v in range(V)]
    parts += list(zip(outside[2:], held[2:]))
    copies = fetch(*zip(*parts), sems)
    table_ref, inverse_ref, *matrices = held
    shifts = (info_ref[0], info_ref[1])
    copies[0].wait()

    @pl.when(shifts[0] >= 0)
    def _():
        planes_ref[...] = dot(table_ref[...], arrived_ref[...])

    for copy in copies[1 : 1 + V]:
        copy.wait()

    @pl.when(shifts[0] >= 0)
    def _():
        for v in range(V):
            for x in range(BX):
                rows = slice(x * NZ, (x + 1) * NZ)
                piece = planes_ref[v * NZ : (v + 1) * NZ, x * BY : (x + 1) * BY]
                data_ref[v, rows, :] = piece.astype(bf16)
                quotient_ref[v, rows, :] = piece * inverse_ref[v, rows, :]
            for yr in range(2):
                edge_ref[v, yr] = pack_strip(quotient_ref[v], shifts[yr])

    for copy in copies[1 + V :]:
        copy.wait()
    write_scaled(far_ref, *adjoint_parts(quotient_ref, edge_ref, matrices))


def adjoint_side_kernel(quotient_ref, edge_ref, k_ref, y_ref, xy_ref, z_ref, message_ref):
    write_scaled(message_ref, *adjoint_parts(quotient_ref, edge_ref, (k_ref, y_ref, xy_ref, z_ref)))


def adjoint_center_kernel(quotient_ref, edge_ref, k_ref, y_ref, xy_ref, z_ref, field_ref, strips_ref):
    field, strips = adjoint_parts(quotient_ref, edge_ref, (k_ref, y_ref, xy_ref, z_ref))
    field_ref[...] = field
    strips_ref[0] = strips[0]
    strips_ref[1] = strips[1]


def gather_kernel(info_ref, field_ref, strips_ref, near_ref, far_ref, total_ref, up_ref, down_ref):
    near, far = read_scaled(near_ref), read_scaled(far_ref)
    total = field_ref[...] + near[:FIELD] + far[:FIELD]
    total_ref[...] = total
    for n, ref in enumerate((up_ref, down_ref)):
        rows = slice(FIELD + n * 2 * NZ, FIELD + (n + 1) * 2 * NZ)
        ref[: 2 * NZ] = strips_ref[n] + near[rows] + far[rows]
        ref[2 * NZ :] = pack_strip(total, info_ref[n])


def gather_last_kernel(field_ref, strips_ref, near_ref, far_ref, total_ref, up_ref, down_ref):
    near, far = read_scaled(near_ref), read_scaled(far_ref)
    total_ref[...] = field_ref[...] + near[:FIELD] + far[:FIELD]
    for n, ref in enumerate((up_ref, down_ref)):
        rows = slice(FIELD + n * 2 * NZ, FIELD + (n + 1) * 2 * NZ)
        ref[...] = strips_ref[n] + near[rows] + far[rows]


def update_kernel(
    info_ref, old_ref, total_ref, up_ref, down_ref, up_in_ref, down_in_ref, new_ref, scaled_ref
):
    half = 2 * NZ
    shifts = (info_ref[0], info_ref[1])
    field = old_ref[:FIELD] * (total_ref[...] + unpack_strips(up_in_ref[:half], down_in_ref[:half], shifts))
    strips = []
    for n, (ref, own) in enumerate(((up_in_ref, up_ref), (down_in_ref, down_ref))):
        rows = slice(FIELD + n * half, FIELD + (n + 1) * half)
        strips.append(old_ref[rows] * (ref[half:] + own[:half]))
    write_message(new_ref, field, strips)
    write_scaled(scaled_ref, field, strips)


def forward_center_kernel(info_ref, own_ref, k_ref, y_ref, xy_ref, z_ref, out_ref):
    shifts = (info_ref[0], info_ref[1])

    def add(v, part):
        out_ref[v] = part

    forward_parts(own_ref[...], (k_ref, y_ref, xy_ref, z_ref), shifts, add)


def forward_near_kernel(info_ref, blurred_ref, near_ref, k_ref, y_ref, xy_ref, z_ref, out_ref):
    shifts = (info_ref[0], info_ref[1])

    def add(v, part):
        out_ref[v] = blurred_ref[v] + part

    forward_parts(read_scaled(near_ref), (k_ref, y_ref, xy_ref, z_ref), shifts, add)


def middle_kernel(
    info_ref, data_ref, blurred_ref, from_far_ref, k_ref, y_ref, xy_ref, z_ref,
    ka_ref, ya_ref, xya_ref, za_ref, quotient_ref, edge_ref, far_ref,
):
    shifts = (info_ref[0], info_ref[1])

    def add(v, part):
        quotient_ref[v] = data_ref[v].astype(f32) / (blurred_ref[v] + part)
        for yr in range(2):
            edge_ref[v, yr] = pack_strip(quotient_ref[v], shifts[yr])

    forward_parts(read_scaled(from_far_ref), (k_ref, y_ref, xy_ref, z_ref), shifts, add)
    write_scaled(far_ref, *adjoint_parts(quotient_ref, edge_ref, (ka_ref, ya_ref, xya_ref, za_ref)))


def final_kernel(info_ref, old_ref, total_ref, up_in_ref, down_in_ref, out_ref, held_ref, sems):
    shifts = (info_ref[0], info_ref[1])
    half = NZ // 2
    copies = []
    for n in range(2):

        @pl.when(shifts[0] >= 0)
        def _():
            edges = unpack_strips(up_in_ref[...], down_in_ref[...], shifts, slice(n * half, (n + 1) * half))
            for x in range(BX):
                rows = slice(x * NZ + n * half, x * NZ + (n + 1) * half)
                correction = total_ref[rows] + edges[x * half : (x + 1) * half]
                held_ref[n * half : (n + 1) * half, x, :] = old_ref[rows] * correction

        part = slice(n * half, (n + 1) * half)
        copies.append(pltpu.make_async_copy(held_ref.at[part], out_ref.at[part], sems.at[n]))
        copies[-1].start()
    for copy in copies:
        copy.wait()


SMEM, VMEM, HBM = pltpu.SMEM, pltpu.VMEM, pltpu.HBM


def call(kernel, outs, *args, scalars=0, far=(), out_place=VMEM, scratch=(), cost=QUICK):
    arrays = [(a.size, a.dtype) for a in (*args[scalars:], *far)]
    arrays += [(math.prod(s), d) for s, d in outs]
    need = sum(count * jnp.dtype(d).itemsize for count, d in arrays)
    places = out_place if isinstance(out_place, list) else [out_place] * len(outs)
    specs = [pl.BlockSpec(memory_space=SMEM)] * scalars
    specs += [pl.BlockSpec(memory_space=VMEM)] * (len(args) - scalars)
    specs += [pl.BlockSpec(memory_space=HBM)] * len(far)
    args += tuple(pltpu.with_memory_space_constraint(a, HBM) for a in far)
    return pl.pallas_call(
        kernel,
        out_shape=[
            HBM(s, d) if where is HBM else jax.ShapeDtypeStruct(s, d) for (s, d), where in zip(outs, places)
        ],
        in_specs=specs,
        out_specs=[pl.BlockSpec(memory_space=where) for where in places],
        scratch_shapes=list(scratch),
        compiler_params=pltpu.CompilerParams(vmem_limit_bytes=need + WORKSPACE),
        cost_estimate=pl.CostEstimate(flops=0, bytes_accessed=int(cost * 3.5e6), transcendentals=0),
    )(*args)


def held(shapes):
    return [pltpu.VMEM(s, d) for s, d in shapes]


def partner_swaps(axis):
    count_x, count_y = lax.axis_size("gx"), lax.axis_size("gy")
    near, far = [], []
    for x in range(count_x):
        for y in range(count_y):
            me = x * count_y + y
            across, along = x * count_y + (y ^ 1), (x ^ 1) * count_y + y
            if axis == "gx":
                other = x - 1 if x % 2 == 0 else x + 1
                near.append((me, along))
                far.append((me, other * count_y + y if 0 <= other < count_x else across))
            else:
                other = y - 1 if y % 2 == 0 else y + 1
                near.append((me, across))
                far.append((me, x * count_y + other if 0 <= other < count_y else along))
    return near, far


def swap_near(axis, value):
    return lax.ppermute(narrow(axis, value), ("gx", "gy"), partner_swaps(axis)[0])


def swap_far(axis, value):
    return lax.ppermute(narrow(axis, value), ("gx", "gy"), partner_swaps(axis)[1])


def narrow(axis, value):
    return value.astype(jnp.float16) if axis == "gx" else value


def swap(axis, near_value, far_value):
    far_in = swap_far(axis, far_value)
    return swap_near(axis, near_value), far_in


def tap_tables(psf_taps, kernel_index):
    gx, gy = lax.axis_index("gx"), lax.axis_index("gy")
    even_x, even_y = gx % 2 == 0, gy % 2 == 0
    anchor = jnp.zeros((), i32)
    bordered = jnp.pad(kernel_index, ((1, 1), (1, 1), (0, 0), (0, 0)), constant_values=-1)
    around = lax.dynamic_slice(
        bordered, (gx.astype(i32), gy.astype(i32), anchor, anchor), (ROLES, ROLES, V, 3)
    )
    low, middle, high = around[:1], around[1:2], around[2:]
    around = jnp.where(
        even_x, jnp.concatenate([middle, high, low]), jnp.concatenate([middle, low, high])
    )
    low, middle, high = around[:, :1], around[:, 1:2], around[:, 2:]
    around = jnp.where(
        even_y, jnp.concatenate([middle, high, low], 1), jnp.concatenate([middle, low, high], 1)
    )
    normal = psf_taps / jnp.sum(psf_taps, axis=-1, keepdims=True)
    chosen = (around.reshape(-1)[:, None] == jnp.arange(psf_taps.shape[0], dtype=i32)).astype(f32)
    kernels = jnp.dot(chosen, normal, precision=lax.Precision.HIGHEST)
    kernels = jnp.pad(kernels, ((0, 0), (0, LANES - TAPS)))
    backward = jnp.pad(kernels[:, :TAPS][:, ::-1], ((0, 0), (0, LANES - TAPS)))
    role = jnp.arange(kernels.shape[0])
    axis, yr, xr = role % 3, role // (3 * V) % ROLES, role // (3 * V * ROLES)
    step = jnp.where(axis == 0, jnp.where(xr == 1, 1, jnp.where(xr == 2, -1, 0)), 0)
    step = step * jnp.where(even_x, 1, -1)
    step_y = jnp.where(axis == 1, jnp.where(yr == 1, 1, jnp.where(yr == 2, -1, 0)), 0)
    step = (step + step_y * jnp.where(even_y, 1, -1))[:, None]

    def moved(a, sign):
        return jnp.where(
            step * sign > 0, jnp.roll(a, -STRIP, 1), jnp.where(step * sign < 0, jnp.roll(a, STRIP, 1), a)
        )

    return moved(kernels, 1), moved(backward, -1)


def shards(estimate, stored, placement, psf_taps, kernel_index):
    devices_y = lax.axis_size("gy")
    devices = lax.axis_size("gx") * devices_y
    slots = stored.shape[0]
    cap = 2 * slots // devices
    rows = devices * cap
    plane = BX * BY
    me = (lax.axis_index("gx") * devices_y + lax.axis_index("gy")).astype(i32)

    half, message = (2 * NZ, LANES), (FIELD + 4 * NZ, LANES)
    scaled = (FIELD + 4 * NZ + STRIP, LANES)
    one, every = (FIELD, LANES), (V, FIELD, LANES)
    even_y = lax.axis_index("gy") % 2 == 0
    info = jnp.stack([jnp.where(even_y, STRIP, 0), jnp.where(even_y, 0, STRIP)]).astype(i32)
    slots_of = placement.reshape(devices, slots)
    field, up, down, slots_near, stored_near = call(
        start_kernel,
        [(one, f32), (half, f32), (half, f32), (slots_of.shape, i32), (stored.shape, bf16)],
        info, scalars=1, far=(estimate, slots_of, stored),
        scratch=[pltpu.VMEM(estimate.shape, f32), pltpu.SemaphoreType.DMA((3,))],
    )
    up_in, down_in = swap("gy", up, down)
    (outgoing,) = call(
        functools.partial(route_kernel, cap), [((rows, plane), bf16)], me.reshape(1), slots_near, stored_near,
        scalars=1, scratch=[pltpu.VMEM((slots * BX, BY), f32)],
    )
    outgoing, psf_taps, kernel_index, slots_of = lax.optimization_barrier(
        (outgoing, psf_taps, kernel_index, slots_of)
    )
    arrived = lax.all_to_all(
        outgoing.reshape(devices, cap, plane), ("gx", "gy"), split_axis=0, concat_axis=0, tiled=True
    ).reshape(rows, plane)

    old = jnp.concatenate([field, up_in, down_in], axis=0)
    near, far = (a.astype(f32) for a in swap("gx", old, old))
    taps, backward = tap_tables(psf_taps, kernel_index)

    def shapes(y_shape, z_shape):
        return ROLES * [
            ((V, FIELD, FIELD), bf16),
            (y_shape, bf16),
            ((2, V, 2 * LANES, 2 * LANES), bf16),
            ((2,) + z_shape, bf16),
        ]

    forward_shapes = shapes((3 * BY, V * BY), (V * NZ, LANES))
    adjoint_shapes = shapes((V, 2 * BY, 2 * BY), (NZ, V * LANES))
    sems = [pltpu.SemaphoreType.DMA((4 * ROLES,))]
    forward = call(build_forward_kernel, forward_shapes, taps, backward, cost=3.0)
    adjoint = call(
        build_adjoint_kernel, adjoint_shapes, taps, backward,
        out_place=HBM, scratch=held(adjoint_shapes) + sems, cost=4.0,
    )
    forward_far, forward_near, forward_center = forward[:4], forward[4:8], forward[8:]

    blurred = ()
    for message_in, matrices in ((old, forward_center), (near, forward_near)):
        blurred = call(
            forward_first_kernel, [(every, f32)], info, *blurred, message_in, *matrices, scalars=1
        )
    (inverse,) = call(
        forward_inverse_kernel, [(every, f32)], info, *blurred, far, *forward_far, scalars=1,
        out_place=HBM, scratch=[pltpu.VMEM(every, f32), pltpu.SemaphoreType.DMA],
    )
    adjoint_of_far, adjoint_near, adjoint_center = adjoint[:4], adjoint[4:8], adjoint[8:]
    (table,) = call(
        functools.partial(arrival_kernel, cap), [((slots, rows), bf16)],
        me.reshape(1), jnp.repeat(slots_of, cap, axis=0), scalars=1,
        out_place=HBM, scratch=[pltpu.VMEM((slots, rows), bf16), pltpu.SemaphoreType.DMA],
    )

    edges = ((V, 2) + half, f32)
    fetched = (table, inverse, *adjoint_of_far)
    data, quotient, edge, far = call(
        quotient_first_kernel, [(every, bf16), (every, f32), edges, (scaled, f32)],
        info, arrived, scalars=1, far=fetched,
        scratch=held([(a.shape, a.dtype) for a in fetched])
        + [pltpu.VMEM((slots, plane), f32), pltpu.SemaphoreType.DMA((len(fetched) + V - 1,))],
    )

    def sides(quotient, edge, far):
        far = swap_far("gx", far)
        (near,) = call(adjoint_side_kernel, [(scaled, f32)], quotient, edge, *adjoint_near)
        near = swap_near("gx", near)
        center = [(one, f32), ((2,) + half, f32)]
        field, strips = call(adjoint_center_kernel, center, quotient, edge, *adjoint_center, cost=QUICK)
        return field, strips, near.astype(f32), far.astype(f32)

    both = (4 * NZ, LANES)
    total, up, down = call(
        gather_kernel, [(one, f32), (both, f32), (both, f32)], info, *sides(quotient, edge, far), scalars=1
    )
    up_in, down_in = swap("gy", up, down)
    taps, backward, up, down = lax.optimization_barrier((taps, backward, up, down))
    forward = call(build_forward_kernel, forward_shapes, taps, backward)
    old, *forward = lax.optimization_barrier((old, *forward))
    forward_far, forward_near, forward_center = forward[:4], forward[4:8], forward[8:]
    new, new_scaled = call(
        update_kernel, [(message, f32), (scaled, f32)],
        info, old, total, up, down, up_in, down_in, scalars=1,
    )
    far = swap_far("gx", new_scaled)
    near = swap_near("gx", new_scaled)
    (blurred,) = call(forward_center_kernel, [(every, f32)], info, new, *forward_center, scalars=1, cost=QUICK)
    (blurred,) = call(
        forward_near_kernel, [(every, f32)], info, blurred, near.astype(f32), *forward_near, scalars=1, cost=QUICK
    )
    quotient, edge, far = call(
        middle_kernel, [(every, f32), edges, (scaled, f32)],
        info, data, blurred, far.astype(f32), *forward_far, *adjoint_of_far, scalars=1, cost=QUICK,
    )
    total, up, down = call(
        gather_last_kernel, [(one, f32), (half, f32), (half, f32)], *sides(quotient, edge, far)
    )
    up_in, down_in = swap("gy", up, down)
    (refined,) = call(
        final_kernel, [(estimate.shape, f32)], info, new, total, up_in, down_in, scalars=1, out_place=HBM,
        scratch=[pltpu.VMEM(estimate.shape, f32), pltpu.SemaphoreType.DMA((2,))],
    )
    return refined


def solution(mesh):
    return jax.shard_map(
        shards,
        mesh=mesh,
        in_specs=(P(None, "gx", "gy"), P(("gx", "gy"), None, None), P(), P(), P()),
        out_specs=P(None, "gx", "gy"),
        check_vma=False,
    )
```
